256 devices in a mesh: sy: 16 (over y, z_lo), sx: 8 (over x, core), fr: 2 (over z_hi).
Axes of the slice: x: 4, y: 4, z: 8 (z_hi: 2, z_lo: 4; z = z_hi * 4 + z_lo), core: 2. Of those that a mesh axis runs over, the one named last changes fastest.
Arguments:
- object_field: float32 [2048, 4096], P('sy', 'sx'), may hold values from 0.5 to 15
- frames_data: float32 [2, 2048, 4096], P('fr', 'sy', 'sx'), may hold values from 0.4 to 16
- patch_psfs: float32 [2, 16, 32, 128, 128], P('fr', 'sy', 'sx'), may hold values from 0 to 0.80009155
Outputs:
- gradient: float32 [2048, 4096], P('sy', 'sx')
- residual: float32 [2, 2048, 4096], P('fr', 'sy', 'sx')
The draws below stay inside these ranges and needn't reach their ends.
All inputs are finite; a program needn't handle non-finite values.
Results may differ from the reference program's by a relative error of at most 0.0003.
Values sent between devices are 32-bit elements; how exact they have to be, the bound alone decides.
No kernel may reach another device: no remote copies, remote signals or barrier semaphores. Data moves between devices by JAX's collectives and lax.ppermute only.
A program may use at most 128 MiB of HBM per device.

```python
import jax
import jax.numpy as jnp
from jax import lax

PATCH = 256
STRIDE = 128
SUPPORT = 128
LENGTH = 384
FRAMES = 2
NY = 2048
NX = 4096
NPY = 16
NPX = 32


def brightness(height, width):
    row_frac = lax.broadcasted_iota(jnp.float32, (height, width), 0) / height
    column_frac = lax.broadcasted_iota(jnp.float32, (height, width), 1) / width
    return 10.0 ** (0.5 * row_frac + 0.5 * column_frac)


def draw_object_field(key, part):
    key = jax.random.fold_in(key, 11)
    uniform_draw = jax.random.uniform(key, (NY, NX), jnp.float32)
    factor = 0.5 + uniform_draw
    return brightness(NY, NX) * factor


def draw_frames_data(key, part):
    key = jax.random.fold_in(key, 12)
    uniform_draw = jax.random.uniform(key, (FRAMES, NY, NX), jnp.float32)
    factor = 0.4 + 1.2 * uniform_draw
    return brightness(NY, NX)[None] * factor


def draw_patch_psfs(key, part):
    key = jax.random.fold_in(key, 13)
    halo_key, core_key = jax.random.split(key)
    shape = (FRAMES, NPY, NPX, SUPPORT, SUPPORT)
    uniform_draw = jax.random.uniform(halo_key, shape, jnp.float32)
    core = jax.random.uniform(core_key, (FRAMES, NPY, NPX, 1, 1), jnp.float32, 0.3, 0.8)
    halo_part = uniform_draw / (SUPPORT * SUPPORT)
    row_index = lax.broadcasted_iota(jnp.int32, shape, 3)
    column_index = lax.broadcasted_iota(jnp.int32, shape, 4)
    centre = jnp.where((row_index == SUPPORT // 2) & (column_index == SUPPORT // 2), 1.0, 0.0)
    return halo_part + core * centre


def setup_inputs(seed: int = 0) -> dict:
    seeds = jax.random.split(jax.random.key(seed), 4)
    return {
        "object_field": draw_object_field(jax.random.fold_in(seeds[3], 71), 0),
        "frames_data": draw_frames_data(jax.random.fold_in(seeds[3], 71), 0),
        "patch_psfs": draw_patch_psfs(jax.random.fold_in(seeds[3], 71), 0),
    }


def window_table(patch_size):
    position = jnp.arange(patch_size, dtype=jnp.float32)
    edge = jnp.sin(jnp.pi * (position + 0.5) / patch_size) ** 2
    return edge[:, None] * edge[None, :]


def cut_windows(field, stride, count_y, count_x, span_blocks):
    blocks = field.reshape(count_y + span_blocks - 1, stride, count_x + span_blocks - 1, stride)
    stacked = jnp.stack([blocks[a:a + count_y] for a in range(span_blocks)], axis=1)
    both = jnp.stack([stacked[:, :, :, b:b + count_x] for b in range(span_blocks)], axis=4)
    side = span_blocks * stride
    return both.transpose(0, 3, 1, 2, 4, 5).reshape(count_y, count_x, side, side)


def spread(pieces, stride):
    count_y, count_x = pieces.shape[0], pieces.shape[1]
    blocks = pieces.reshape(count_y, count_x, 3, stride, 3, stride)
    summed = jnp.zeros((count_y + 2, stride, count_x + 2, stride), pieces.dtype)
    for a in range(3):
        for b in range(3):
            placed = blocks[:, :, a, :, b, :].transpose(0, 2, 1, 3)
            summed = summed + jnp.pad(placed, ((a, 2 - a), (0, 0), (b, 2 - b), (0, 0)))
    return summed.reshape((count_y + 2) * stride, (count_x + 2) * stride)


def reference(object_field, frames_data, patch_psfs):
    stride = STRIDE
    half = stride // 2
    window = window_table(PATCH)
    pieces = cut_windows(jnp.pad(object_field, half), stride, NPY, NPX, 2) * window
    piece_spec = jnp.fft.rfft2(pieces, s=(LENGTH, LENGTH))
    gradient = jnp.zeros((NY, NX), jnp.float32)
    residuals = []
    for frame in range(FRAMES):
        psf_spec = jnp.fft.rfft2(patch_psfs[frame], s=(LENGTH, LENGTH))
        blurred = jnp.fft.irfft2(piece_spec * psf_spec, s=(LENGTH, LENGTH))
        model_tile = spread(blurred, stride)[stride:-stride, stride:-stride]
        observed = frames_data[frame]
        frame_gain = jnp.sum(observed) / jnp.sum(model_tile)
        residual = frame_gain * model_tile - observed
        windows = cut_windows(jnp.pad(residual, stride), stride, NPY, NPX, 3)
        adjoint = jnp.fft.irfft2(jnp.conj(psf_spec) * jnp.fft.rfft2(windows), s=(LENGTH, LENGTH))[..., :PATCH, :PATCH]
        shares = frame_gain * window * adjoint
        shares = jnp.pad(shares, ((0, 0), (0, 0), (half, half), (half, half)))
        gradient = gradient + spread(shares, stride)[stride:-stride, stride:-stride]
        residuals.append(residual)
    return gradient, jnp.stack(residuals)
```

```python
import functools
import math

import jax
import jax.numpy as jnp
import numpy as np
from jax import lax
from jax.experimental import pallas as pl
from jax.experimental.pallas import tpu as pltpu
from jax.sharding import PartitionSpec as P

S = 128
L = 256
H = 64
F32 = jnp.float32
BF16 = jnp.bfloat16


def half_windows():
    n = np.arange(L, dtype=np.float64)
    s = np.sin(np.pi * (n + 0.5) / L) ** 2
    return s[:S], s[S:]


def phases(freqs, positions):
    product = (2 * np.arange(freqs)[:, None] + 1) * positions[None, :] % (2 * L)
    angle = product.astype(np.float64) * (math.pi / L)
    return np.cos(angle), np.sin(angle)


def forward_left(positions):
    c, s = phases(L, positions)
    return np.block([[c, s], [-s, c]])


def inverse_left(positions):
    c, s = phases(L, positions)
    return np.block([[c.T, -s.T], [s.T, c.T]]) / L


def forward_right(positions):
    c, s = phases(S, positions)
    return np.concatenate([c.T, -s.T], axis=1)


def inverse_right(positions):
    c, s = phases(S, positions)
    return np.concatenate([c, -s], axis=0) * (2.0 / L)


def bf16_parts(table):
    hi = table.astype(np.float32).astype(BF16)
    lo = (table - hi.astype(np.float64)).astype(np.float32).astype(BF16)
    return hi, lo


def left_table(table):
    hi, lo = bf16_parts(table)
    return np.concatenate([hi, hi, lo], axis=-1)


def right_table(table):
    hi, lo = bf16_parts(table)
    return np.concatenate([hi, hi, lo], axis=-2)


@functools.lru_cache(maxsize=1)
def tables():
    near, far = np.arange(S), np.arange(S, L)
    up, down = half_windows()
    first_half = near < H
    t = {}
    t["psf_right"] = right_table(forward_right(near))
    t["psf_left"] = left_table(forward_left(near))
    t["obj_right"] = right_table(
        np.concatenate([up[:, None] * forward_right(near), down[:, None] * forward_right(near)], axis=1)
    )
    rows_forward, rows_inverse = [], []
    for first in (False, True):
        row_up = np.where(first_half & first, 0.0, up)
        row_down = np.where(~first_half & first, 0.0, down)
        base, back = forward_left(near), inverse_left(near)
        rows_forward.append(
            np.concatenate([base * np.tile(w, 2)[None, :] for w in (row_up, row_down)], axis=0)
        )
        rows_inverse.append(
            np.concatenate([np.tile(w, 2)[:, None] * back for w in (row_up, row_down)], axis=1)
        )
    t["obj_left"] = left_table(np.stack(rows_forward))
    t["grad_left"] = left_table(np.stack(rows_inverse))
    t["top_inverse"] = left_table(inverse_left(near))
    t["bottom_inverse"] = left_table(inverse_left(far))
    t["out_right"] = right_table(inverse_right(np.arange(L)))
    t["res_right"] = right_table(forward_right(np.arange(L)))
    t["top_forward"] = left_table(forward_left(near))
    t["bottom_forward"] = left_table(forward_left(far))
    t["grad_right"] = right_table(
        np.concatenate([inverse_right(near) * up[None, :], inverse_right(near) * down[None, :]], axis=0)
    )
    return t


def split(value):
    hi = value.astype(BF16)
    return hi, (value - hi.astype(F32)).astype(BF16)


def times_right(value, table):
    hi, lo = split(value)
    return jnp.dot(jnp.concatenate([hi, lo, hi], axis=1), table, preferred_element_type=F32)


def times_left(table, value):
    hi, lo = split(value)
    return jnp.dot(table, jnp.concatenate([hi, lo, hi], axis=0), preferred_element_type=F32)


def stacked_parts(value):
    return jnp.concatenate([value[:, :S], value[:, S:]], axis=0)


def side_by_side(value):
    half = value.shape[0] // 2
    return jnp.concatenate([value[:half], value[half:]], axis=1)


def psf_spectra(psf_ref, right_ref, left_ref, out_ref):
    right, left = right_ref[...], left_ref[...]
    for j in range(psf_ref.shape[0]):
        lanes = times_right(psf_ref[j], right)
        out_ref[:, j * S : (j + 1) * S] = times_left(left, stacked_parts(lanes))


def units(q, count):
    return [(w, j) for w, j in ((0, q), (1, q - 1)) if 0 <= j < count]


def psf_kernel(psf_ref, frame_ref, right_ref, left_ref, spec_ref, total_ref):
    psf_spectra(psf_ref, right_ref, left_ref, spec_ref)
    total_ref[...] = jnp.full(total_ref.shape, jnp.sum(frame_ref[...]), F32)


def model_kernel(
    flags, above_ref, own_ref, left_ref, right_ref, psf_ref, spec_ref, total_ref,
    psf_right, psf_left, obj_right, obj_left, top_inverse, bottom_inverse, out_right,
    spec_above, spill_left, middle, spill_right, flux_ref, x_ref, spill,
):
    count = psf_ref.shape[0]
    width = own_ref.shape[1]
    alpha = 1.0 - flags[0].astype(F32)
    psf_spectra(psf_ref, psf_right, psf_left, spec_above)
    x_ref[:H] = above_ref[...]
    x_ref[H:] = jnp.concatenate([left_ref[:H], own_ref[:H], right_ref[:H]], axis=1)
    spill[...] = jnp.zeros(spill.shape, F32)
    specs = (spec_ref, spec_above)
    for q in range(count + 1):
        lanes = times_right(x_ref[:, q * S : (q + 1) * S], obj_right[...])
        pieces = jnp.concatenate(
            [stacked_parts(lanes[:, w * L : (w + 1) * L]) for w, _ in units(q, count)], axis=1
        )
        x_spec = times_left(obj_left[...], pieces)
        rows = []
        for r in range(2):
            re, im = 0.0, 0.0
            for u, (_, j) in enumerate(units(q, count)):
                x_re = x_spec[2 * r * L : (2 * r + 1) * L, u * S : (u + 1) * S]
                x_im = x_spec[(2 * r + 1) * L : (2 * r + 2) * L, u * S : (u + 1) * S]
                h_re = specs[r][:L, j * S : (j + 1) * S]
                h_im = specs[r][L:, j * S : (j + 1) * S]
                re = re + (x_re * h_re - x_im * h_im)
                im = im + (x_re * h_im + x_im * h_re)
            rows.append(jnp.concatenate([re, im], axis=0))
        top = times_left(top_inverse[...], rows[1] + alpha * rows[0])
        bottom = times_left(bottom_inverse[...], rows[0] + alpha * rows[1])
        both = jnp.concatenate([side_by_side(top), side_by_side(bottom)], axis=0)
        spill[:, q * S : (q + 2) * S] += times_right(both, out_right[...])
    spill_left[...] = spill[:, :S]
    middle[...] = spill[:, S : S + width]
    spill_right[...] = spill[:, S + width :]
    in_left, in_right = (1.0 - flags[1].astype(F32), 1.0 - flags[2].astype(F32))
    flux = (
        jnp.sum(spill[:, S : S + width])
        + in_left * jnp.sum(spill[:, :S])
        + in_right * jnp.sum(spill[:, S + width :])
    )
    row = lax.broadcasted_iota(jnp.int32, flux_ref.shape, 0)
    flux_ref[...] = jnp.where(row < 4, flux, total_ref[...])


def gradient_kernel(
    flags, top_left, top_middle, top_right, own_left, own_ref, own_right, gain_ref, spec_ref, spec_above,
    res_right, top_forward, bottom_forward, grad_left, grad_right,
    out_left, out_top, out_bottom, out_right, r_ref, grad,
):
    width = own_ref.shape[1]
    count = width // S
    alpha = 1.0 - flags[0].astype(F32)
    r_ref[:S] = jnp.concatenate([top_left[...], top_middle[...], top_right[...]], axis=1)
    r_ref[S:] = jnp.concatenate([own_left[...], own_ref[...], own_right[...]], axis=1)
    specs = (spec_ref, spec_above)
    gain = gain_ref[0, 0]
    for q in range(count + 1):
        lanes = times_right(r_ref[:, q * S : (q + 2) * S], res_right[...])
        top = times_left(top_forward[...], stacked_parts(lanes[:S]))
        bottom = times_left(bottom_forward[...], stacked_parts(lanes[S:]))
        seen = (bottom + alpha * top, top + alpha * bottom)
        columns = []
        for _, j in units(q, count):
            parts = []
            for r in range(2):
                h_re = specs[r][:L, j * S : (j + 1) * S]
                h_im = specs[r][L:, j * S : (j + 1) * S]
                r_re, r_im = seen[r][:L], seen[r][L:]
                parts += [r_re * h_re + r_im * h_im, r_im * h_re - r_re * h_im]
            columns.append(jnp.concatenate(parts, axis=0))
        rows = times_left(grad_left[...], jnp.concatenate(columns, axis=1))
        total = 0.0
        for u, (w, _) in enumerate(units(q, count)):
            table = grad_right[w]
            total = total + times_right(side_by_side(rows[:, u * S : (u + 1) * S]), table)
        grad[:, q * S : (q + 1) * S] = total * gain
    out_left[...] = grad[:, :H]
    out_top[...] = grad[:H, H : H + width]
    out_bottom[...] = grad[H:, H : H + width]
    out_right[...] = grad[:, H + width :]


WHOLE = pl.BlockSpec(memory_space=pltpu.VMEM)
SCALARS = pl.BlockSpec(memory_space=pltpu.SMEM)


def picked(table):
    block = (None,) + table.shape[1:]
    return pl.BlockSpec(block, lambda i, flags: (flags[0], 0, 0))


def params():
    return pltpu.CompilerParams(vmem_limit_bytes=44 * 2**20)


def f32(*shape):
    return jax.ShapeDtypeStruct(shape, F32)


def call(kernel, flags, operands, outs, scratch, chosen=(), flops=10**9):
    def spec(shape):
        return pl.BlockSpec(shape, lambda i, flags, n=len(shape): (0,) * n)

    in_specs = [picked(x) if n in chosen else spec(x.shape) for n, x in enumerate(operands)]
    size = sum(math.prod(x.shape) * x.dtype.itemsize for x in operands)
    return pl.pallas_call(
        kernel,
        out_shape=outs,
        grid_spec=pltpu.PrefetchScalarGridSpec(
            num_scalar_prefetch=1,
            grid=(1,),
            in_specs=in_specs,
            out_specs=[spec(o.shape) for o in outs],
            scratch_shapes=scratch,
        ),
        compiler_params=params(),
        cost_estimate=pl.CostEstimate(flops=flops, bytes_accessed=size, transcendentals=0),
    )(flags, *operands)


def cyclic(value, axis, steps):
    count = lax.axis_size(axis)
    return lax.ppermute(value, axis, [(s, (s + steps) % count) for s in range(count)])


def shifted(value, axis, steps):
    count = lax.axis_size(axis)
    pairs = [(s, s + steps) for s in range(count) if 0 <= s + steps < count]
    return lax.ppermute(value, axis, pairs)


def mirrored(value, axis, bits):
    count = lax.axis_size(axis)
    return lax.ppermute(value, axis, [(s, s ^ bits) for s in range(count)])


def summed(value, axis):
    count, step = lax.axis_size(axis), 1
    while step < count:
        radix = 4 if count // step % 4 == 0 else 2
        value = sum([mirrored(value, axis, step * k) for k in range(1, radix)], value)
        step *= radix
    return value


def per_device(object_field, frames_data, patch_psfs):
    rows, width = object_field.shape
    count = width // S
    psfs = patch_psfs.reshape(count, S, S)
    observed = frames_data[0]
    t = {name: jnp.asarray(value) for name, value in tables().items()}
    y, x = lax.axis_index("sy"), lax.axis_index("sx")
    flags = jnp.stack([y == 0, x == 0, x == lax.axis_size("sx") - 1]).astype(jnp.int32)

    psf_above = cyclic(psfs, "sy", 1)
    obj_left = shifted(object_field[:, -H:], "sx", 1)
    obj_right = shifted(object_field[:, :H], "sx", -1)
    obj_wide = jnp.concatenate([obj_left[H:], object_field[H:], obj_right[H:]], axis=1)
    obj_above = cyclic(obj_wide, "sy", 1)

    spec, total = call(
        lambda flags, *refs: psf_kernel(*refs),
        flags,
        (psfs, observed, t["psf_right"], t["psf_left"]),
        (f32(2 * L, width), f32(8, S)),
        [],
        flops=6 * 84 * 10**6,
    )
    spec_above, spill_left, middle, spill_right, flux = call(
        model_kernel,
        flags,
        (obj_above, object_field, obj_left, obj_right, psf_above, spec, total)
        + tuple(
            t[k]
            for k in (
                "psf_right", "psf_left", "obj_right", "obj_left",
                "top_inverse", "bottom_inverse", "out_right",
            )
        ),
        (f32(2 * L, width), f32(L, S), f32(L, width), f32(L, S), f32(8, S)),
        [pltpu.VMEM((S, width + S), F32), pltpu.VMEM((L, width + 2 * S), F32)],
        chosen=(10,),
        flops=6 * 600 * 10**6,
    )
    from_right = shifted(spill_left, "sx", -1)
    from_left = shifted(spill_right, "sx", 1)
    folded = jnp.concatenate(
        [middle[:, :S] + from_left, middle[:, S:-S], middle[:, -S:] + from_right], axis=1
    )
    from_below = cyclic(folded[:S], "sy", -1)
    flux = summed(summed(flux, "sx"), "sy")
    gain = flux[4, 0] / flux[0, 0]
    residual = gain * (folded[S:] + from_below) - observed

    own_left = shifted(residual[:, -S:], "sx", 1)
    own_right = shifted(residual[:, :S], "sx", -1)
    top_middle = cyclic(residual, "sy", 1)
    top_left = shifted(top_middle[:, -S:], "sx", 1)
    top_right = shifted(top_middle[:, :S], "sx", -1)
    grad_right = t["grad_right"].reshape(3, 2, L, S).transpose(1, 0, 2, 3).reshape(2, 3 * L, S)
    g_left, g_top, g_bottom, g_right = call(
        gradient_kernel,
        flags,
        (top_left, top_middle, top_right, own_left, residual, own_right,
         jnp.full((8, S), gain), spec, spec_above)
        + tuple(t[k] for k in ("res_right", "top_forward", "bottom_forward", "grad_left"))
        + (grad_right,),
        (f32(S, H), f32(H, width), f32(H, width), f32(S, H)),
        [pltpu.VMEM((L, width + 2 * S), F32), pltpu.VMEM((S, width + S), F32)],
        chosen=(12,),
        flops=6 * 500 * 10**6,
    )
    g_from_right = shifted(g_left, "sx", -1)
    g_from_left = shifted(g_right, "sx", 1)

    def joined(part, lo, hi):
        return jnp.concatenate(
            [part[:, :H] + g_from_left[lo:hi], part[:, H:-H], part[:, -H:] + g_from_right[lo:hi]], axis=1
        )

    g_top, g_bottom = joined(g_top, 0, H), joined(g_bottom, H, S)
    top_same = cyclic(g_top, "sy", -1)
    top_other = mirrored_up(g_top)
    bottom_other = mirrored(g_bottom, "fr", 1)
    gradient = jnp.concatenate([g_bottom + bottom_other, top_same + top_other], axis=0)
    return gradient, residual[None]


def mirrored_up(value):
    count_y, count_f = lax.axis_size("sy"), lax.axis_size("fr")
    pairs = [
        (y * count_f + f, (y - 1) % count_y * count_f + (f ^ 1))
        for y in range(count_y)
        for f in range(count_f)
    ]
    return lax.ppermute(value, ("sy", "fr"), pairs)


def solution(mesh):
    placed = (P("sy", "sx"), P("fr", "sy", "sx"), P("fr", "sy", "sx", None, None))
    return jax.shard_map(
        per_device,
        mesh=mesh,
        in_specs=placed,
        out_specs=(P("sy", "sx"), P("fr", "sy", "sx")),
        check_vma=False,
    )
```

```python
import functools
import math

import jax
import jax.numpy as jnp
import numpy as np
from jax import lax
from jax.experimental import pallas as pl
from jax.experimental.pallas import tpu as pltpu
from jax.sharding import PartitionSpec as P

S = 128
L = 256
H = 64
F32 = jnp.float32
BF16 = jnp.bfloat16


def half_windows():
    n = np.arange(L, dtype=np.float64)
    s = np.sin(np.pi * (n + 0.5) / L) ** 2
    return s[:S], s[S:]


def phases(freqs, positions):
    product = (2 * np.arange(freqs)[:, None] + 1) * positions[None, :] % (2 * L)
    angle = product.astype(np.float64) * (math.pi / L)
    return np.cos(angle), np.sin(angle)


def forward_left(positions):
    c, s = phases(L, positions)
    return np.block([[c, s], [-s, c]])


def inverse_left(positions):
    c, s = phases(L, positions)
    return np.block([[c.T, -s.T], [s.T, c.T]]) / L


def forward_right(positions):
    c, s = phases(S, positions)
    return np.concatenate([c.T, -s.T], axis=1)


def inverse_right(positions):
    c, s = phases(S, positions)
    return np.concatenate([c, -s], axis=0) * (2.0 / L)


def bf16_parts(table):
    hi = table.astype(np.float32).astype(BF16)
    lo = (table - hi.astype(np.float64)).astype(np.float32).astype(BF16)
    return hi, lo


def left_table(table):
    hi, lo = bf16_parts(table)
    return np.concatenate([hi, hi, lo], axis=-1)


def right_table(table):
    hi, lo = bf16_parts(table)
    return np.concatenate([hi, hi, lo], axis=-2)


@functools.lru_cache(maxsize=1)
def tables():
    near, far = np.arange(S), np.arange(S, L)
    up, down = half_windows()
    masked_up, masked_down = np.where(near < H, 0.0, up), np.where(near < H, down, 0.0)
    pairs = ((up, down), (masked_up, masked_down))
    base, back = forward_left(near), inverse_left(near)
    lanes, lanes_back = forward_right(near), inverse_right(near)
    t = {}
    t["near_right"] = right_table(lanes)
    t["near_left"] = left_table(base)
    t["obj_right"] = np.stack(
        [right_table(np.concatenate([w[:, None] * lanes for w in pair], axis=1)) for pair in pairs]
    )
    t["obj_left"] = np.stack(
        [left_table(np.concatenate([base * np.tile(w, 2)[None, :] for w in pair], axis=0)) for pair in pairs]
    )
    t["top_inverse"] = left_table(inverse_left(near))
    t["bottom_inverse"] = left_table(inverse_left(far))
    t["out_right"] = right_table(inverse_right(np.arange(L)))
    t["far_right"] = right_table(forward_right(far))
    t["res_right"] = right_table(forward_right(np.arange(L)))
    t["bottom_forward"] = left_table(forward_left(far))
    t["grad_left"] = np.stack(
        [left_table(np.concatenate([np.tile(w, 2)[:, None] * back for w in pair], axis=1)) for pair in pairs]
    )
    t["grad_right"] = np.stack(
        [right_table(np.concatenate([lanes_back * w[None, :] for w in pair], axis=0)) for pair in pairs]
    )
    return t


def split(value):
    hi = value.astype(BF16)
    return hi, (value - hi.astype(F32)).astype(BF16)


def wide_parts(value):
    hi, lo = split(value)
    return jnp.concatenate([hi, lo, hi], axis=1)


def store_parts(ref, lanes, value):
    hi, lo = split(value)
    depth = value.shape[0]
    ref[:depth, lanes] = hi
    ref[depth : 2 * depth, lanes] = lo
    ref[2 * depth :, lanes] = hi


def dot(a, b):
    return jnp.dot(a, b, preferred_element_type=F32)


def stacked(value):
    half = value.shape[1] // 2
    return jnp.concatenate([value[:, :half], value[:, half:]], axis=0)


def side_by_side(value):
    half = value.shape[0] // 2
    return jnp.concatenate([value[:half], value[half:]], axis=1)


def at(n, size=S):
    return slice(n * size, (n + 1) * size)


class Copies:
    def __init__(self, sources, buffers, semaphores):
        self.copies = [
            pltpu.make_async_copy(source, buffer, semaphores.at[n])
            for n, (source, buffer) in enumerate(zip(sources, buffers))
        ]
        self.buffers, self.waited = buffers, set()
        for copy in self.copies:
            copy.start()

    def __getitem__(self, n):
        if n not in self.waited:
            self.waited.add(n)
            self.copies[n].wait()
        return self.buffers[n]


def spectra(psfs, right, left, parts_ref):
    lanes = dot(wide_parts(jnp.concatenate(psfs, axis=0)), right[...])
    for n in range(len(psfs)):
        store_parts(parts_ref, at(n), stacked(lanes[at(n)]))
    return dot(left[...], parts_ref[:, : len(psfs) * S])


def psf_kernel(flags, psf_ref, frame_ref, right_hbm, left_hbm, spec_ref, total_ref, right, left, parts, sems):
    t = Copies((right_hbm, left_hbm), (right, left), sems)
    total_ref[...] = jnp.full(total_ref.shape, jnp.sum(frame_ref[...]), F32)
    spec_ref[...] = spectra([psf_ref[j] for j in range(psf_ref.shape[0])], t[0], t[1], parts)


def pack_kernel(obj_ref, psf_ref, right_ref, diagonal_ref):
    last = obj_ref[:, obj_ref.shape[1] - S :]
    right_ref[:S] = psf_ref[psf_ref.shape[0] - 1]
    diagonal_ref[:S] = psf_ref[psf_ref.shape[0] - 1]
    right_ref[S:] = last[:H]
    diagonal_ref[S:] = last[H:]


def model_kernel(
    flags, psf_ref, above_ref, right_ref, diagonal_ref, own_ref, spec_ref, total_ref, *refs
):
    hbm, refs = refs[:7], refs[7:]
    more_ref, mid_top, mid_bottom, first_ref, last_ref, flux_ref = refs[:6]
    buffers, (sems, psf_parts, x_ref, x_parts, top_parts, bottom_parts) = refs[6:14], refs[14:]
    row_edge, column_edge = flags[0], flags[1]
    sources = [hbm[0], hbm[1], hbm[2].at[0], hbm[2].at[column_edge], hbm[3].at[row_edge]] + list(hbm[4:7])
    t = Copies(sources, buffers, sems)
    alpha, beta = 1.0 - row_edge.astype(F32), 1.0 - column_edge.astype(F32)
    width = own_ref.shape[1]
    count = width // S
    psfs = [diagonal_ref[:S]] + [psf_ref[j] for j in range(count)] + [right_ref[:S]]
    more_ref[...] = spectra(psfs, t[0], t[1], psf_parts)
    for q in range(count):
        lo = q * S
        if q == 0:
            left = jnp.concatenate([diagonal_ref[S:], right_ref[S:]], axis=0)[:, H:]
        else:
            left = jnp.concatenate([above_ref[:, lo - S : lo], own_ref[:H, lo - S : lo]], axis=0)[:, H:]
        here = jnp.concatenate([above_ref[:, lo : lo + S], own_ref[:H, lo : lo + S]], axis=0)[:, :H]
        x_ref[at(q)] = jnp.concatenate([left, here], axis=1)
    first = dot(wide_parts(x_ref[:S]), t[3][...])
    others = dot(wide_parts(x_ref[S:]), t[2][...])
    for q in range(count):
        lanes = first if q == 0 else others[at(q - 1)]
        for w in range(2):
            store_parts(x_parts, at(2 * q + w), stacked(lanes[:, at(w, L)]))
    for q in range(count):
        x_spec = dot(t[4][...], x_parts[:, at(q, L)])
        y = {}
        for r in range(2):
            for w in range(2):
                x_re = x_spec[at(2 * r, L), at(w)]
                x_im = x_spec[at(2 * r + 1, L), at(w)]
                j = q - w
                if r == 0:
                    source, lanes = (spec_ref, at(j)) if j >= 0 else (more_ref, at(count + 1))
                else:
                    source, lanes = more_ref, at(j + 1)
                h_re, h_im = source[:L, lanes], source[L:, lanes]
                y[r, w] = (x_re * h_re - x_im * h_im, x_re * h_im + x_im * h_re)
        if q == 0:
            variants = [
                [tuple(y[r, 1][c] + beta * y[r, 0][c] for c in range(2)) for r in range(2)],
                [tuple(y[r, 0][c] + beta * y[r, 1][c] for c in range(2)) for r in range(2)],
            ]
        else:
            variants = [[tuple(y[r, 0][c] + y[r, 1][c] for c in range(2)) for r in range(2)]]
        for v, rows in enumerate(variants):
            slot = at(v if q == 0 else q + 1)
            both = [jnp.concatenate(parts, axis=0) for parts in rows]
            store_parts(top_parts, slot, both[1] + alpha * both[0])
            store_parts(bottom_parts, slot, both[0] + alpha * both[1])
    halves = (dot(t[5][...], top_parts[...]), dot(t[6][...], bottom_parts[...]))
    right = t[7]
    flux = 0.0
    for half, rows in enumerate(halves):
        first_left = dot(wide_parts(side_by_side(rows[:, at(0)])), right[:, :S])
        first_right = dot(wide_parts(side_by_side(rows[:, at(1)])), right[:, S:])
        rest = dot(
            wide_parts(jnp.concatenate([side_by_side(rows[:, at(q + 1)]) for q in range(1, count)], axis=0)),
            right[...],
        )
        lefts = [first_left] + [rest[at(q), :S] for q in range(count - 1)]
        rights = [first_right] + [rest[at(q), S:] for q in range(count - 1)]
        first_ref[at(half)] = lefts[0]
        last_ref[at(half)] = rights[-1]
        middle = mid_bottom if half else mid_top
        total = lefts[0] + rights[-1]
        for q in range(1, count):
            block = lefts[q] + rights[q - 1]
            middle[:, at(q - 1)] = block
            total = total + block
        flux = flux + jnp.sum(total)
    row = lax.broadcasted_iota(jnp.int32, flux_ref.shape, 0)
    flux_ref[...] = jnp.where(row < 4, flux, total_ref[...])


def gradient_kernel(
    flags, top_ref, bottom_ref, above_ref, below_ref,
    obs_ref, obs_above, obs_left, obs_diagonal, gain_ref, spec_ref, more_ref, *refs
):
    hbm, refs = refs[:7], refs[7:]
    residual_ref, out_top, out_bottom = refs[:3]
    buffers, (sems, r_ref, top_parts, bottom_parts, g_parts) = refs[3:11], refs[11:]
    row_edge, column_edge = flags[0], flags[1]
    sources = list(hbm[:5]) + [hbm[5].at[row_edge], hbm[6].at[0], hbm[6].at[column_edge]]
    t = Copies(sources, buffers, sems)
    alpha, beta = 1.0 - row_edge.astype(F32), 1.0 - column_edge.astype(F32)
    width = obs_ref.shape[1]
    count = width // S
    gain = gain_ref[0, 0]
    r_ref[:S] = gain * (top_ref[...] + above_ref[...])
    r_ref[S:] = gain * (bottom_ref[...] + below_ref[...])
    r_ref[:S, :S] -= obs_diagonal[...]
    r_ref[S:, :S] -= obs_left[...]
    r_ref[:S, S:] -= obs_above[...]
    r_ref[S:, S:] -= obs_ref[...]
    residual_ref[...] = r_ref[S:, S:]
    near = dot(wide_parts(r_ref[:, :S]), t[0][...])
    far = dot(wide_parts(r_ref[:, S : 2 * S]), t[1][...])
    lanes = [far + beta * near, near + beta * far]
    rest = dot(wide_parts(jnp.concatenate([r_ref[:, q * S : (q + 2) * S] for q in range(1, count)], axis=0)), t[2][...])
    lanes += [rest[at(q, L)] for q in range(count - 1)]
    for n, value in enumerate(lanes):
        store_parts(top_parts, at(n), stacked(value[:S]))
        store_parts(bottom_parts, at(n), stacked(value[S:]))
    top = dot(t[3][...], top_parts[...])
    bottom = dot(t[4][...], bottom_parts[...])
    rows = []
    for q in range(count):
        for w in range(2):
            slot = at(w if q == 0 else q + 1)
            j = q - w
            for r in range(2):
                if r == 0:
                    source, lanes = (spec_ref, at(j)) if j >= 0 else (more_ref, at(count + 1))
                    seen = bottom[:, slot] + alpha * top[:, slot]
                else:
                    source, lanes = more_ref, at(j + 1)
                    seen = top[:, slot] + alpha * bottom[:, slot]
                h_re, h_im = source[:L, lanes], source[L:, lanes]
                r_re, r_im = seen[:L], seen[L:]
                for c, part in enumerate((r_re * h_re + r_im * h_im, r_im * h_re - r_re * h_im)):
                    hi, lo = split(part)
                    place = (2 * r + c) * L
                    for n, value in enumerate((hi, lo, hi)):
                        g_parts[4 * n * L + place : 4 * n * L + place + L, at(w)] = value
        g = dot(t[5][...], g_parts[...])
        rows.append(jnp.concatenate([side_by_side(g[:, at(w)]) for w in range(2)], axis=1))
    first = dot(wide_parts(rows[0]), t[7][...]) * gain
    rest = dot(wide_parts(jnp.concatenate(rows[1:], axis=0)), t[6][...]) * gain
    grad = jnp.concatenate([first] + [rest[at(q)] for q in range(count - 1)], axis=1)
    out_top[...] = grad[:H]
    out_bottom[...] = grad[H:]


def f32(*shape):
    return jax.ShapeDtypeStruct(shape, F32)


def call(kernel, flags, operands, in_hbm, outs, scratch, flops):
    def spec(shape):
        return pl.BlockSpec(shape, lambda i, flags, n=len(shape): (0,) * n)

    kept = [pl.BlockSpec(memory_space=pltpu.HBM) for _ in in_hbm]
    size = sum(math.prod(x.shape) * x.dtype.itemsize for x in tuple(operands) + tuple(in_hbm))
    return pl.pallas_call(
        kernel,
        out_shape=outs,
        grid_spec=pltpu.PrefetchScalarGridSpec(
            num_scalar_prefetch=1,
            grid=(1,),
            in_specs=[spec(x.shape) for x in operands] + kept,
            out_specs=[spec(o.shape) for o in outs],
            scratch_shapes=scratch,
        ),
        compiler_params=pltpu.CompilerParams(vmem_limit_bytes=60 * 2**20),
        cost_estimate=pl.CostEstimate(flops=flops, bytes_accessed=size, transcendentals=0),
    )(flags, *operands, *in_hbm)


def buffer(table, picks=0):
    return pltpu.VMEM(table.shape[1:] if picks else table.shape, BF16)


def ring(value, axes, moves):
    sizes = [lax.axis_size(a) for a in axes]
    pairs = []
    for source in np.ndindex(*sizes):
        target = [(p + m) % n for p, m, n in zip(source, moves, sizes)]
        pairs.append((int(np.ravel_multi_index(source, sizes)), int(np.ravel_multi_index(target, sizes))))
    return lax.ppermute(value, axes, pairs)


def mirrored(value, axis, bits):
    count = lax.axis_size(axis)
    return lax.ppermute(value, axis, [(s, s ^ bits) for s in range(count)])


def summed(value, axis):
    count = lax.axis_size(axis)
    spread = jnp.broadcast_to(value[None], (count,) + value.shape)
    return jnp.sum(lax.all_to_all(spread, axis, 0, 0), axis=0)


def down(value):
    return ring(value, ("sy",), (1,))


def up(value):
    return ring(value, ("sy",), (-1,))


def per_device(object_field, frames_data, patch_psfs):
    rows, width = object_field.shape
    count = width // S
    psfs = patch_psfs.reshape(count, S, S)
    observed = frames_data[0]
    t = {name: jnp.asarray(value) for name, value in tables().items()}
    y, x = lax.axis_index("sy"), lax.axis_index("sx")
    flags = jnp.stack([y == 0, x == 0]).astype(jnp.int32)

    psf_above = down(psfs)
    obj_above = down(object_field[H:])
    pack_right, pack_diagonal = pl.pallas_call(
        pack_kernel, out_shape=(f32(S + H, S), f32(S + H, S))
    )(object_field, psfs)
    got_diagonal = ring(pack_diagonal, ("sy", "sx"), (1, 1))
    got_right = ring(pack_right, ("sx",), (1,))
    obs_above = down(observed)
    obs_last = observed[:, -S:]
    obs_left = ring(obs_last, ("sx",), (1,))
    obs_diagonal = ring(obs_last, ("sy", "sx"), (1, 1))

    semaphores = pltpu.SemaphoreType.DMA((8,))
    spec, total = call(
        psf_kernel,
        flags,
        (psfs, observed),
        (t["near_right"], t["near_left"]),
        (f32(2 * L, width), f32(8, S)),
        [buffer(t["near_right"]), buffer(t["near_left"]), pltpu.VMEM((6 * S, width), BF16), semaphores],
        6 * 84 * 10**6,
    )
    more, mid_top, mid_bottom, first, last, flux = call(
        model_kernel,
        flags,
        (psf_above, obj_above, got_right, got_diagonal, object_field, spec, total),
        tuple(t[k] for k in ("near_right", "near_left", "obj_right", "obj_left",
                             "top_inverse", "bottom_inverse", "out_right")),
        (f32(2 * L, width + 2 * S), f32(S, width - S), f32(S, width - S), f32(L, S), f32(L, S), f32(8, S)),
        [buffer(t["near_right"]), buffer(t["near_left"]), buffer(t["obj_right"], 1), buffer(t["obj_right"], 1),
         buffer(t["obj_left"], 1), buffer(t["top_inverse"]), buffer(t["bottom_inverse"]), buffer(t["out_right"]),
         semaphores,
         pltpu.VMEM((6 * S, width + 2 * S), BF16), pltpu.VMEM((width, S), F32),
         pltpu.VMEM((6 * S, 2 * width), BF16),
         pltpu.VMEM((6 * L, width + S), BF16), pltpu.VMEM((6 * L, width + S), BF16)],
        6 * 600 * 10**6,
    )
    mid_top, mid_bottom, first, last, obs_above, obs_left, obs_diagonal = lax.optimization_barrier(
        (mid_top, mid_bottom, first, last, obs_above, obs_left, obs_diagonal)
    )
    from_right = ring(first, ("sx",), (-1,))
    from_left = ring(last, ("sx",), (1,))
    flux = summed(flux, "sx")
    flux, from_left, from_right = lax.optimization_barrier((flux, from_left, from_right))
    wide_top = jnp.concatenate([first[:S] + from_left[:S], mid_top, last[:S] + from_right[:S]], axis=1)
    wide_bottom = jnp.concatenate([first[S:] + from_left[S:], mid_bottom, last[S:] + from_right[S:]], axis=1)
    below = up(wide_top)
    above = down(wide_bottom)
    flux = summed(flux, "sy")
    gain = jnp.full((8, S), flux[4, 0] / flux[0, 0])

    residual, g_top, g_bottom = call(
        gradient_kernel,
        flags,
        (wide_top, wide_bottom, above, below,
         observed, obs_above, obs_left, obs_diagonal, gain, spec, more),
        tuple(t[k] for k in ("near_right", "far_right", "res_right", "near_left",
                             "bottom_forward", "grad_left", "grad_right")),
        (f32(S, width), f32(H, width), f32(H, width)),
        [buffer(t["near_right"]), buffer(t["far_right"]), buffer(t["res_right"]), buffer(t["near_left"]),
         buffer(t["bottom_forward"]), buffer(t["grad_left"], 1), buffer(t["grad_right"], 1),
         buffer(t["grad_right"], 1), semaphores,
         pltpu.VMEM((L, width + S), F32), pltpu.VMEM((6 * S, width + S), BF16),
         pltpu.VMEM((6 * S, width + S), BF16), pltpu.VMEM((12 * L, L), BF16)],
        6 * 500 * 10**6,
    )
    bottom_other = mirrored(g_bottom, "fr", 1)
    top_other = ring(g_top, ("sy", "fr"), (-1, 1))
    top_same = up(g_top)
    total = jnp.concatenate([g_bottom + bottom_other, top_same + top_other], axis=0)
    side = ring(total[:, :H], ("sx",), (-1,))
    gradient = jnp.concatenate([total[:, H:], side], axis=1)
    return gradient, residual[None]


def solution(mesh):
    placed = (P("sy", "sx"), P("fr", "sy", "sx"), P("fr", "sy", "sx", None, None))
    return jax.shard_map(
        per_device,
        mesh=mesh,
        in_specs=placed,
        out_specs=(P("sy", "sx"), P("fr", "sy", "sx")),
        check_vma=False,
    )
```

```python
import functools
import math

import jax
import jax.numpy as jnp
import numpy as np
from jax import lax
from jax.experimental import pallas as pl
from jax.experimental.pallas import tpu as pltpu
from jax.sharding import PartitionSpec as P

S = 128
L = 256
H = 64
F32 = jnp.float32
BF16 = jnp.bfloat16


def half_windows():
    n = np.arange(L, dtype=np.float64)
    s = np.sin(np.pi * (n + 0.5) / L) ** 2
    return s[:S], s[S:]


def phases(freqs, positions):
    product = (2 * np.arange(freqs)[:, None] + 1) * positions[None, :] % (2 * L)
    angle = product.astype(np.float64) * (math.pi / L)
    return np.cos(angle), np.sin(angle)


def forward_left(positions):
    c, s = phases(L, positions)
    return np.block([[c, s], [-s, c]])


def inverse_left(positions):
    c, s = phases(L, positions)
    return np.block([[c.T, -s.T], [s.T, c.T]]) / L


def forward_right(positions):
    c, s = phases(S, positions)
    return np.concatenate([c.T, -s.T], axis=1)


def inverse_right(positions):
    c, s = phases(S, positions)
    return np.concatenate([c, -s], axis=0) * (2.0 / L)


def bf16_parts(table):
    hi = table.astype(np.float32).astype(BF16)
    lo = (table - hi.astype(np.float64)).astype(np.float32).astype(BF16)
    return hi, lo


def left_table(table):
    hi, lo = bf16_parts(table)
    return np.concatenate([hi, hi, lo], axis=-1)


def right_table(table):
    hi, lo = bf16_parts(table)
    return np.concatenate([hi, hi, lo], axis=-2)


@functools.lru_cache(maxsize=1)
def tables():
    near = np.arange(S)
    up, down = half_windows()
    pairs = ((up, down), (np.where(near < H, 0.0, up), np.where(near < H, down, 0.0)))
    base, back = forward_left(near), inverse_left(near)
    t = {}
    t["near_right"] = right_table(forward_right(near))
    t["near_left"] = left_table(base)
    t["obj_left"] = np.stack(
        [left_table(np.concatenate([base * np.tile(w, 2)[None, :] for w in pair], axis=0)) for pair in pairs]
    )
    t["near_inverse"] = left_table(back)
    t["out_right"] = right_table(inverse_right(np.arange(L)))
    t["res_right"] = right_table(forward_right(np.arange(L)))
    t["grad_left"] = np.stack(
        [left_table(np.concatenate([np.tile(w, 2)[:, None] * back for w in pair], axis=1)) for pair in pairs]
    )
    t["grad_right"] = right_table(inverse_right(near))
    t["windows"] = np.stack([np.stack([np.tile(w, (8, 1)) for w in pair]) for pair in pairs]).astype(np.float32)
    return t


def split(value):
    hi = value.astype(BF16)
    return hi, (value - hi.astype(F32)).astype(BF16)


def wide_parts(value):
    hi, lo = split(value)
    return jnp.concatenate([hi, lo, hi], axis=1)


def store_parts(ref, lanes, value):
    hi, lo = split(value)
    depth = value.shape[0]
    ref[:depth, lanes] = hi
    ref[depth : 2 * depth, lanes] = lo
    ref[2 * depth :, lanes] = hi


def dot(a, b):
    return jnp.dot(a, b, preferred_element_type=F32)


def stacked(value):
    half = value.shape[1] // 2
    return jnp.concatenate([value[:, :half], value[:, half:]], axis=0)


def side_by_side(value):
    half = value.shape[0] // 2
    return jnp.concatenate([value[:half], value[half:]], axis=1)


def at(n, size=S):
    return slice(n * size, (n + 1) * size)


class Copies:
    def __init__(self, names, sources, refs, semaphores):
        self.buffers = dict(zip(names, refs))
        self.copies = {
            name: pltpu.make_async_copy(source, buffer, semaphores.at[n])
            for n, (name, source, buffer) in enumerate(zip(names, sources, refs))
        }
        self.waited = set()
        for name in names:
            self.copies[name].start()

    def __getitem__(self, name):
        if name not in self.waited:
            self.waited.add(name)
            self.copies[name].wait()
        return self.buffers[name]


def edges():
    return [(lax.axis_index(axis) == 0).astype(jnp.int32) for axis in ("sy", "sx")]


def picked(names, hbm):
    rows, columns = edges()
    edge = {"obj_left": rows, "grad_left": rows, "windows": columns}
    return [h.at[edge[n]] if n in edge else h for n, h in zip(names, hbm)]


def psf_kernel(names, *refs):
    total = len(names)
    hbm, refs = refs[:total], refs[total:]
    spec_hbm, spec_ref, total_ref, *buffers = refs[:-4]
    psf, frame, sems, parts = refs[-4:]
    t = Copies(names, picked(names, hbm), (psf, frame) + tuple(buffers), sems)
    psf = t["psf"]
    lanes = dot(wide_parts(jnp.concatenate([psf[j] for j in range(psf.shape[0])], axis=0)), t["near_right"][...])
    for j in range(psf.shape[0]):
        store_parts(parts, at(j), stacked(lanes[at(j)]))
    spec_ref[...] = dot(t["near_left"][...], parts[...])
    out = pltpu.make_async_copy(spec_ref, spec_hbm, sems.at[total])
    out.start()
    total_ref[...] = jnp.full(total_ref.shape, jnp.sum(t["frame"][...]), F32)
    for name in names:
        t[name]
    out.wait()


def pack_kernel(obj_ref, frame_ref, psf_ref, down_ref, right_ref, diagonal_ref, frame_last):
    width = obj_ref.shape[1]
    last = obj_ref[:, width - S :]
    down_ref[...] = obj_ref[H:]
    right_ref[:S] = psf_ref[psf_ref.shape[0] - 1]
    right_ref[S:] = last[:H]
    diagonal_ref[:S] = psf_ref[psf_ref.shape[0] - 1]
    diagonal_ref[S:] = last[H:]
    frame_last[...] = frame_ref[:, width - S :]


def alternating():
    k = lax.broadcasted_iota(jnp.int32, (L, S), 0)
    return jnp.where(k % 2 == 0, 1.0, -1.0).astype(F32)


def model_kernel(names, ready, *refs):
    total = len(names)
    hbm, refs = refs[:total], refs[total:]
    t, refs = dict(zip(ready, refs)), refs[len(ready) :]
    outs_hbm, flux_ref, refs = refs[:5], refs[5], refs[6:]
    buffers, sems, (more_ref, mid_top, mid_bottom, first_ref, last_ref) = refs[:total], refs[total], refs[total + 1 : total + 6]
    x_ref, x_parts, y_parts = refs[total + 6 :]
    got = Copies(names, hbm, buffers, sems)
    outs = [
        pltpu.make_async_copy(source, out, sems.at[total + n])
        for n, (source, out) in enumerate(zip((more_ref, mid_top, mid_bottom, first_ref, last_ref), outs_hbm))
    ]
    row_edge, column_edge = edges()
    alpha, beta = 1.0 - row_edge.astype(F32), 1.0 - column_edge.astype(F32)
    right_ref, diagonal_ref, above_ref, own_ref = [got[n] for n in ("right", "diagonal", "above", "own")]
    count = own_ref.shape[1] // S
    windows = [t["windows"][w, :1] for w in range(2)]
    plain = [t["plain"][w, :1] for w in range(2)]
    for q in range(count):
        lo = q * S
        if q == 0:
            left = jnp.concatenate([diagonal_ref[S:], right_ref[S:]], axis=0)[:, H:]
        else:
            left = jnp.concatenate([above_ref[:, lo - S : lo], own_ref[:H, lo - S : lo]], axis=0)[:, H:]
        here = jnp.concatenate([above_ref[:, lo : lo + S], own_ref[:H, lo : lo + S]], axis=0)[:, :H]
        x = jnp.concatenate([left, here], axis=1)
        for w in range(2):
            x_ref[at(2 * q + w)] = x * (windows if q == 0 else plain)[w]
    psf_above = got["psf_above"]
    psfs = [diagonal_ref[:S]] + [psf_above[j] for j in range(count)] + [right_ref[:S]]
    lanes = dot(wide_parts(jnp.concatenate([x_ref[...]] + psfs, axis=0)), t["near_right"][...])
    for n in range(3 * count + 2):
        store_parts(x_parts, at(n), stacked(lanes[at(n)]))
    more_ref[...] = dot(t["near_left"][...], x_parts[:, 2 * count * S :])
    outs[0].start()
    spec_ref = t["spec"]
    obj_left = t["obj_left"]
    sign = alternating()
    for pair in range(count // 2):
        x_specs = dot(obj_left[...], x_parts[:, pair * 4 * S : (pair + 1) * 4 * S])
        for q in (2 * pair, 2 * pair + 1):
            y = {}
            for r in range(2):
                for w in range(2):
                    lanes = at(2 * (q % 2) + w)
                    x_re = x_specs[at(2 * r, L), lanes]
                    x_im = x_specs[at(2 * r + 1, L), lanes]
                    j = q - w
                    if r == 0:
                        source, lanes = (spec_ref, at(j)) if j >= 0 else (more_ref, at(count + 1))
                    else:
                        source, lanes = more_ref, at(j + 1)
                    h_re, h_im = source[:L, lanes], source[L:, lanes]
                    y[r, w] = (x_re * h_re - x_im * h_im, x_re * h_im + x_im * h_re)
            if q == 0:
                variants = [
                    [tuple(y[r, 1][c] + beta * y[r, 0][c] for c in range(2)) for r in range(2)],
                    [tuple(y[r, 0][c] + beta * y[r, 1][c] for c in range(2)) for r in range(2)],
                ]
            else:
                variants = [[tuple(y[r, 0][c] + y[r, 1][c] for c in range(2)) for r in range(2)]]
            for v, (upper, lower) in enumerate(variants):
                slot = v if q == 0 else q + 1
                top = [lower[c] + alpha * upper[c] for c in range(2)]
                bottom = [upper[c] + alpha * lower[c] for c in range(2)]
                store_parts(y_parts, at(slot), jnp.concatenate(top, axis=0))
                turned = jnp.concatenate([-sign * bottom[1], sign * bottom[0]], axis=0)
                store_parts(y_parts, at(count + 1 + slot), turned)
    rows = dot(t["near_inverse"][...], y_parts[...])
    blocks = jnp.concatenate([side_by_side(rows[:, at(n)]) for n in range(2 * count + 2)], axis=0)
    out = dot(wide_parts(blocks), t["out_right"][...])
    flux = 0.0
    for half in range(2):
        base = half * (count + 1)
        lefts = [out[at(base), :S]] + [out[at(base + q + 1), :S] for q in range(1, count)]
        rights = [out[at(base + q + 1), S:] for q in range(count)]
        first_ref[at(half)] = lefts[0]
        last_ref[at(half)] = rights[-1]
        middle = mid_bottom if half else mid_top
        together = lefts[0] + rights[-1]
        for q in range(1, count):
            block = lefts[q] + rights[q - 1]
            middle[:, at(q - 1)] = block
            together = together + block
        flux = flux + jnp.sum(together)
    for copy in outs[1:]:
        copy.start()
    row = lax.broadcasted_iota(jnp.int32, flux_ref.shape, 1)
    flux_ref[...] = jnp.where(row < 4, flux, t["total"][...][None])
    for copy in outs:
        copy.wait()


def edge_kernel(first, last, from_left, from_right, flux_ref, top_ref, bottom_ref, totals_ref):
    for half, out in ((0, top_ref), (1, bottom_ref)):
        out[:, :S] = first[at(half)] + from_left[at(half)]
        out[:, S:] = last[at(half)] + from_right[at(half)]
    totals_ref[...] = jnp.broadcast_to(jnp.sum(flux_ref[...], axis=0)[None], totals_ref.shape)


def gradient_kernel(names, *refs):
    total = len(names)
    hbm, refs = refs[:total], refs[total:]
    residual_hbm, top_hbm, bottom_hbm = refs[:3]
    buffers, sems, (residual_ref, out_top, out_bottom) = refs[3 : 3 + total], refs[3 + total], refs[4 + total : 7 + total]
    r_ref, r_parts, g_parts = refs[7 + total :]
    t = Copies(names, picked(names, hbm), buffers, sems)
    sent = [
        pltpu.make_async_copy(source, out, sems.at[total + n])
        for n, (source, out) in enumerate(
            zip((residual_ref, out_top, out_bottom), (residual_hbm, top_hbm, bottom_hbm))
        )
    ]
    row_edge, column_edge = edges()
    alpha, beta = 1.0 - row_edge.astype(F32), 1.0 - column_edge.astype(F32)
    width = residual_ref.shape[1]
    count = width // S
    sums = jnp.sum(t["flux"][...], axis=0)
    gain = sums[4, 0] / sums[0, 0]
    r_ref[:S, S:width] = gain * (t["mid_top"][...] + t["mid_above"][...]) - t["obs_above"][:, : width - S]
    r_ref[S:, S:width] = gain * (t["mid_bottom"][...] + t["mid_below"][...]) - t["obs"][:, : width - S]
    top, bottom, above, below = (t[n] for n in ("edge_top", "edge_bottom", "edge_above", "edge_below"))
    r_ref[:S, :S] = gain * (top[:, :S] + above[:, :S]) - t["obs_diagonal"][...]
    r_ref[S:, :S] = gain * (bottom[:, :S] + below[:, :S]) - t["obs_left"][...]
    r_ref[:S, width:] = gain * (top[:, S:] + above[:, S:]) - t["obs_above"][:, width - S :]
    r_ref[S:, width:] = gain * (bottom[:, S:] + below[:, S:]) - t["obs"][:, width - S :]
    residual_ref[...] = r_ref[S:, S:]
    sent[0].start()
    near, far = r_ref[:, :S], r_ref[:, S : 2 * S]
    blocks = [
        jnp.concatenate([beta * near, far], axis=1),
        jnp.concatenate([near, beta * far], axis=1),
    ] + [r_ref[:, q * S : (q + 2) * S] for q in range(1, count)]
    lanes = dot(wide_parts(jnp.concatenate(blocks, axis=0)), t["res_right"][...])
    for n in range(count + 1):
        value = lanes[at(n, L)]
        store_parts(r_parts, at(n), stacked(value[:S]))
        store_parts(r_parts, at(count + 1 + n), stacked(value[S:]))
    spectra = dot(t["near_left"][...], r_parts[...])
    sign = alternating()
    spec_ref, more_ref = t["spec"], t["more"]
    seen = []
    for n in range(count + 1):
        top = [spectra[at(c, L), at(n)] for c in range(2)]
        raw = [spectra[at(c, L), at(count + 1 + n)] for c in range(2)]
        bottom = [sign * raw[1], -sign * raw[0]]
        seen.append(
            [
                [bottom[c] + alpha * top[c] for c in range(2)],
                [top[c] + alpha * bottom[c] for c in range(2)],
            ]
        )
    grad_left = t["grad_left"]
    outs = []
    for pair in range(count // 2):
        for q in (2 * pair, 2 * pair + 1):
            for w in range(2):
                slot = w if q == 0 else q + 1
                j = q - w
                for r in range(2):
                    if r == 0:
                        source, lanes = (spec_ref, at(j)) if j >= 0 else (more_ref, at(count + 1))
                    else:
                        source, lanes = more_ref, at(j + 1)
                    h_re, h_im = source[:L, lanes], source[L:, lanes]
                    r_re, r_im = seen[slot][r]
                    for c, part in enumerate((r_re * h_re + r_im * h_im, r_im * h_re - r_re * h_im)):
                        hi, lo = split(part)
                        place = (2 * r + c) * L
                        for n, value in enumerate((hi, lo, hi)):
                            g_parts[4 * n * L + place : 4 * n * L + place + L, at(2 * q + w)] = value
        g = dot(grad_left[...], g_parts[:, pair * 4 * S : (pair + 1) * 4 * S])
        outs += [side_by_side(g[:, at(n)]) for n in range(4)]
    out = dot(wide_parts(jnp.concatenate(outs, axis=0)), t["grad_right"][...])
    for q in range(count):
        windows = t["windows"] if q == 0 else t["plain"]
        grad = gain * (out[at(2 * q)] * windows[0, :1] + out[at(2 * q + 1)] * windows[1, :1])
        out_top[:, at(q)] = grad[:H]
        out_bottom[:, at(q)] = grad[H:]
    for copy in sent[1:]:
        copy.start()
    for copy in sent:
        copy.wait()


def f32(*shape):
    return jax.ShapeDtypeStruct(shape, F32)


def call(kernel, named, ready, outs, scratch, limit, flops):
    hbm, vmem = pl.BlockSpec(memory_space=pltpu.HBM), pl.BlockSpec(memory_space=pltpu.VMEM)
    held = [pltpu.with_memory_space_constraint(x, pltpu.HBM) for x in named.values()]
    size = sum(math.prod(x.shape) * x.dtype.itemsize for x in named.values())
    return pl.pallas_call(
        kernel,
        out_shape=[place(o.shape, o.dtype) for place, o in outs],
        in_specs=[hbm] * len(named) + [vmem] * len(ready),
        out_specs=[hbm if place is pltpu.HBM else vmem for place, _ in outs],
        scratch_shapes=scratch,
        compiler_params=pltpu.CompilerParams(vmem_limit_bytes=limit * 2**20),
        cost_estimate=pl.CostEstimate(flops=flops, bytes_accessed=size, transcendentals=0),
    )(*held, *ready.values())


def like(arrays):
    return [pltpu.VMEM(x.shape[1:] if n in PICKED else x.shape, x.dtype) for n, x in arrays.items()]


PICKED = ("windows", "obj_left", "grad_left")


def ring(value, axes, moves):
    sizes = [lax.axis_size(a) for a in axes]
    pairs = []
    for source in np.ndindex(*sizes):
        target = [(p + m) % n for p, m, n in zip(source, moves, sizes)]
        pairs.append((int(np.ravel_multi_index(source, sizes)), int(np.ravel_multi_index(target, sizes))))
    return lax.ppermute(value, axes, pairs)


def mirrored(value, axis, bits):
    count = lax.axis_size(axis)
    return lax.ppermute(value, axis, [(s, s ^ bits) for s in range(count)])


def exchanged(value, axis):
    return lax.all_to_all(value, axis, 0, 0)


def down(value):
    return ring(value, ("sy",), (1,))


def up(value):
    return ring(value, ("sy",), (-1,))


def per_device(object_field, frames_data, patch_psfs):
    rows, width = object_field.shape
    count = width // S
    psfs = patch_psfs.reshape(count, S, S)
    observed = frames_data[0]
    t = {name: jnp.asarray(value) for name, value in tables().items()}
    psf_above = down(psfs)
    pack_down, pack_right, pack_diagonal, obs_last = pl.pallas_call(
        pack_kernel,
        out_shape=(f32(H, width), f32(S + H, S), f32(S + H, S), f32(S, S)),
    )(object_field, observed, psfs)
    obj_above = down(pack_down)
    got_diagonal = ring(pack_diagonal, ("sy", "sx"), (1, 1))
    got_right = ring(pack_right, ("sx",), (1,))
    obs_above = down(observed)
    obs_left = ring(obs_last, ("sx",), (1,))
    obs_diagonal = ring(obs_last, ("sy", "sx"), (1, 1))

    kept = {k: t[k] for k in ("near_right", "near_left", "windows", "obj_left", "near_inverse", "out_right")}
    named = {"psf": psfs, "frame": observed} | kept
    spec, spec_here, total, *got = call(
        functools.partial(psf_kernel, tuple(named)),
        named,
        {},
        [(pltpu.HBM, f32(2 * L, width)), (pltpu.VMEM, f32(2 * L, width)), (pltpu.VMEM, f32(8, S))]
        + [(pltpu.VMEM, x) for x in like(kept)],
        [pltpu.VMEM(psfs.shape, F32), pltpu.VMEM(observed.shape, F32),
         pltpu.SemaphoreType.DMA((len(named) + 1,)), pltpu.VMEM((6 * S, width), BF16)],
        16,
        6 * 84 * 10**6,
    )
    ready = dict(zip(kept, got)) | {"spec": spec_here, "total": total, "plain": t["windows"][0]}
    named = {"right": got_right, "diagonal": got_diagonal, "above": obj_above, "own": object_field,
             "psf_above": psf_above}
    outs = [f32(2 * L, width + 2 * S), f32(S, width - S), f32(S, width - S), f32(L, S), f32(L, S)]
    more, mid_top, mid_bottom, first, last, flux = call(
        functools.partial(model_kernel, tuple(named), tuple(ready)),
        named,
        ready,
        [(pltpu.HBM, o) for o in outs] + [(pltpu.VMEM, f32(lax.axis_size("sx"), 8, S))],
        like(named) + [pltpu.SemaphoreType.DMA((len(named) + len(outs),))]
        + [pltpu.VMEM(o.shape, F32) for o in outs]
        + [pltpu.VMEM((2 * width, S), F32), pltpu.VMEM((6 * S, 3 * width + 2 * S), BF16),
           pltpu.VMEM((6 * L, 2 * width + 2 * S), BF16)],
        36,
        6 * 600 * 10**6,
    )
    mid_top, mid_bottom, first, last, flux, obs_above, obs_left, obs_diagonal = lax.optimization_barrier(
        (mid_top, mid_bottom, first, last, flux, obs_above, obs_left, obs_diagonal)
    )
    mid_below = up(mid_top)
    mid_above = down(mid_bottom)
    from_right = ring(first, ("sx",), (-1,))
    from_left = ring(last, ("sx",), (1,))
    flux = exchanged(flux, "sx")
    edge_top, edge_bottom, flux = pl.pallas_call(
        edge_kernel, out_shape=(f32(S, L), f32(S, L), f32(lax.axis_size("sy"), 8, S))
    )(first, last, from_left, from_right, flux)
    edge_below = up(edge_top)
    edge_above = down(edge_bottom)
    flux = exchanged(flux, "sy")

    named = {"flux": flux, "mid_top": mid_top, "mid_above": mid_above, "obs_above": obs_above,
             "mid_bottom": mid_bottom, "mid_below": mid_below, "obs": observed,
             "edge_top": edge_top, "edge_above": edge_above, "edge_bottom": edge_bottom, "edge_below": edge_below,
             "obs_diagonal": obs_diagonal, "obs_left": obs_left,
             "res_right": t["res_right"], "near_left": t["near_left"], "spec": spec, "more": more,
             "grad_left": t["grad_left"], "grad_right": t["grad_right"],
             "windows": t["windows"], "plain": t["windows"][0]}
    outs = [f32(S, width), f32(H, width), f32(H, width)]
    residual, g_top, g_bottom = call(
        functools.partial(gradient_kernel, tuple(named)),
        named,
        {},
        [(pltpu.HBM, o) for o in outs],
        like(named) + [pltpu.SemaphoreType.DMA((len(named) + len(outs),))]
        + [pltpu.VMEM(o.shape, F32) for o in outs]
        + [pltpu.VMEM((L, width + S), F32), pltpu.VMEM((6 * S, 2 * width + 2 * S), BF16),
           pltpu.VMEM((12 * L, 2 * width), BF16)],
        44,
        6 * 500 * 10**6,
    )
    bottom_other = mirrored(g_bottom, "fr", 1)
    top_other = ring(g_top, ("sy", "fr"), (-1, 1))
    top_same = up(g_top)
    total = jnp.concatenate([g_bottom + bottom_other, top_same + top_other], axis=0)
    side = ring(total[:, :H], ("sx",), (-1,))
    gradient = jnp.concatenate([total[:, H:], side], axis=1)
    return gradient, residual[None]


def solution(mesh):
    placed = (P("sy", "sx"), P("fr", "sy", "sx"), P("fr", "sy", "sx", None, None))
    return jax.shard_map(
        per_device,
        mesh=mesh,
        in_specs=placed,
        out_specs=(P("sy", "sx"), P("fr", "sy", "sx")),
        check_vma=False,
    )
```

```python
import functools
import math

import jax
import jax.numpy as jnp
import numpy as np
from jax import lax
from jax.experimental import pallas as pl
from jax.experimental.pallas import tpu as pltpu
from jax.sharding import PartitionSpec as P

S = 128
L = 256
H = 64
F32 = jnp.float32
BF16 = jnp.bfloat16


def half_windows():
    n = np.arange(L, dtype=np.float64)
    s = np.sin(np.pi * (n + 0.5) / L) ** 2
    return s[:S], s[S:]


def phases(freqs, positions):
    product = (2 * np.arange(freqs)[:, None] + 1) * positions[None, :] % (2 * L)
    angle = product.astype(np.float64) * (math.pi / L)
    return np.cos(angle), np.sin(angle)


def forward_left(positions):
    c, s = phases(L, positions)
    return np.block([[c, s], [-s, c]])


def inverse_left(positions):
    c, s = phases(L, positions)
    return np.block([[c.T, -s.T], [s.T, c.T]]) / L


def forward_right(positions):
    c, s = phases(S, positions)
    return np.concatenate([c.T, -s.T], axis=1)


def inverse_right(positions):
    c, s = phases(S, positions)
    return np.concatenate([c, -s], axis=0) * (2.0 / L)


def bf16_parts(table):
    hi = table.astype(np.float32).astype(BF16)
    lo = (table - hi.astype(np.float64)).astype(np.float32).astype(BF16)
    return hi, lo


def left_table(table):
    hi, lo = bf16_parts(table)
    return np.concatenate([hi, hi, lo], axis=-1)


def right_table(table):
    hi, lo = bf16_parts(table)
    return np.concatenate([hi, hi, lo], axis=-2)


@functools.lru_cache(maxsize=1)
def tables():
    near = np.arange(S)
    up, down = half_windows()
    pairs = ((up, down), (np.where(near < H, 0.0, up), np.where(near < H, down, 0.0)))
    base, back = forward_left(near), inverse_left(near)
    t = {}
    t["near_right"] = right_table(forward_right(near))
    t["near_left"] = left_table(base)
    t["obj_left"] = np.stack(
        [left_table(np.concatenate([base * np.tile(w, 2)[None, :] for w in pair], axis=0)) for pair in pairs]
    )
    t["near_inverse"] = left_table(back)
    t["out_right"] = right_table(inverse_right(np.arange(L)))
    t["res_right"] = right_table(forward_right(np.arange(L)))
    t["grad_left"] = np.stack(
        [left_table(np.concatenate([np.tile(w, 2)[:, None] * back for w in pair], axis=1)) for pair in pairs]
    )
    t["grad_right"] = right_table(inverse_right(near))
    t["windows"] = np.stack([np.stack([np.tile(w, (8, 1)) for w in pair]) for pair in pairs]).astype(np.float32)
    return t


def split(value):
    hi = value.astype(BF16)
    return hi, (value - hi.astype(F32)).astype(BF16)


def wide_parts(value):
    hi, lo = split(value)
    return jnp.concatenate([hi, lo, hi], axis=1)


def store_parts(ref, lanes, value):
    hi, lo = split(value)
    depth = value.shape[0]
    ref[:depth, lanes] = hi
    ref[depth : 2 * depth, lanes] = lo
    ref[2 * depth :, lanes] = hi


def dot(a, b):
    return jnp.dot(a, b, preferred_element_type=F32)


def stacked(value):
    half = value.shape[1] // 2
    return jnp.concatenate([value[:, :half], value[:, half:]], axis=0)


def side_by_side(value):
    half = value.shape[0] // 2
    return jnp.concatenate([value[:half], value[half:]], axis=1)


def at(n, size=S):
    return slice(n * size, (n + 1) * size)


class Copies:
    def __init__(self, names, sources, refs, semaphores):
        self.buffers = dict(zip(names, refs))
        self.copies = {
            name: pltpu.make_async_copy(source, buffer, semaphores.at[n])
            for n, (name, source, buffer) in enumerate(zip(names, sources, refs))
        }
        self.waited = set()
        for name in names:
            self.copies[name].start()

    def __getitem__(self, name):
        if name not in self.waited:
            self.waited.add(name)
            self.copies[name].wait()
        return self.buffers[name]


def edges():
    return [(lax.axis_index(axis) == 0).astype(jnp.int32) for axis in ("sy", "sx")]


def picked(names, hbm):
    rows, columns = edges()
    edge = {"obj_left": rows, "grad_left": rows, "windows": columns}
    return [h.at[edge[n]] if n in edge else h for n, h in zip(names, hbm)]


def psf_kernel(names, *refs):
    total = len(names)
    hbm, refs = refs[:total], refs[total:]
    spec_hbm, spec_ref, total_ref, *buffers = refs[:-4]
    psf, frame, sems, parts = refs[-4:]
    t = Copies(names, picked(names, hbm), (psf, frame) + tuple(buffers), sems)
    psf = t["psf"]
    lanes = dot(wide_parts(jnp.concatenate([psf[j] for j in range(psf.shape[0])], axis=0)), t["near_right"][...])
    for j in range(psf.shape[0]):
        store_parts(parts, at(j), stacked(lanes[at(j)]))
    spec_ref[...] = dot(t["near_left"][...], parts[...])
    out = pltpu.make_async_copy(spec_ref, spec_hbm, sems.at[total])
    out.start()
    total_ref[...] = jnp.full(total_ref.shape, jnp.sum(t["frame"][...]), F32)
    for name in names:
        t[name]
    out.wait()


def pack_kernel(obj_ref, frame_ref, psf_ref, down_ref, right_ref, diagonal_ref, frame_last):
    width = obj_ref.shape[1]
    last = obj_ref[:, width - S :]
    down_ref[...] = obj_ref[H:]
    right_ref[:S] = psf_ref[psf_ref.shape[0] - 1]
    right_ref[S:] = last[:H]
    diagonal_ref[:S] = psf_ref[psf_ref.shape[0] - 1]
    diagonal_ref[S:] = last[H:]
    frame_last[...] = frame_ref[:, width - S :]


def alternating():
    k = lax.broadcasted_iota(jnp.int32, (L, S), 0)
    return jnp.where(k % 2 == 0, 1.0, -1.0).astype(F32)


def model_kernel(names, ready, *refs):
    total = len(names)
    hbm, refs = refs[:total], refs[total:]
    t, refs = dict(zip(ready, refs)), refs[len(ready) :]
    outs_hbm, flux_ref, refs = refs[:5], refs[5], refs[6:]
    buffers, sems, (more_ref, mid_top, mid_bottom, first_ref, last_ref) = refs[:total], refs[total], refs[total + 1 : total + 6]
    x_ref, x_parts, y_parts = refs[total + 6 :]
    got = Copies(names, hbm, buffers, sems)
    outs = [
        pltpu.make_async_copy(source, out, sems.at[total + n])
        for n, (source, out) in enumerate(zip((more_ref, mid_top, mid_bottom, first_ref, last_ref), outs_hbm))
    ]
    row_edge, column_edge = edges()
    alpha, beta = 1.0 - row_edge.astype(F32), 1.0 - column_edge.astype(F32)
    right_ref, diagonal_ref, above_ref, own_ref = [got[n] for n in ("right", "diagonal", "above", "own")]
    count = own_ref.shape[1] // S
    windows = [t["windows"][w, :1] for w in range(2)]
    plain = [t["plain"][w, :1] for w in range(2)]
    for q in range(count):
        lo = q * S
        if q == 0:
            left = jnp.concatenate([diagonal_ref[S:], right_ref[S:]], axis=0)[:, H:]
        else:
            left = jnp.concatenate([above_ref[:, lo - S : lo], own_ref[:H, lo - S : lo]], axis=0)[:, H:]
        here = jnp.concatenate([above_ref[:, lo : lo + S], own_ref[:H, lo : lo + S]], axis=0)[:, :H]
        x = jnp.concatenate([left, here], axis=1)
        for w in range(2):
            x_ref[at(2 * q + w)] = x * (windows if q == 0 else plain)[w]
    psf_above = got["psf_above"]
    psfs = [diagonal_ref[:S]] + [psf_above[j] for j in range(count)] + [right_ref[:S]]
    lanes = dot(wide_parts(jnp.concatenate([x_ref[...]] + psfs, axis=0)), t["near_right"][...])
    for n in range(3 * count + 2):
        store_parts(x_parts, at(n), stacked(lanes[at(n)]))
    more_ref[...] = dot(t["near_left"][...], x_parts[:, 2 * count * S :])
    outs[0].start()
    spec_ref = t["spec"]
    obj_left = t["obj_left"]
    sign = alternating()
    for pair in range(count // 2):
        x_specs = dot(obj_left[...], x_parts[:, pair * 4 * S : (pair + 1) * 4 * S])
        for q in (2 * pair, 2 * pair + 1):
            y = {}
            for r in range(2):
                for w in range(2):
                    lanes = at(2 * (q % 2) + w)
                    x_re = x_specs[at(2 * r, L), lanes]
                    x_im = x_specs[at(2 * r + 1, L), lanes]
                    j = q - w
                    if r == 0:
                        source, lanes = (spec_ref, at(j)) if j >= 0 else (more_ref, at(count + 1))
                    else:
                        source, lanes = more_ref, at(j + 1)
                    h_re, h_im = source[:L, lanes], source[L:, lanes]
                    y[r, w] = (x_re * h_re - x_im * h_im, x_re * h_im + x_im * h_re)
            if q == 0:
                variants = [
                    [tuple(y[r, 1][c] + beta * y[r, 0][c] for c in range(2)) for r in range(2)],
                    [tuple(y[r, 0][c] + beta * y[r, 1][c] for c in range(2)) for r in range(2)],
                ]
            else:
                variants = [[tuple(y[r, 0][c] + y[r, 1][c] for c in range(2)) for r in range(2)]]
            for v, (upper, lower) in enumerate(variants):
                slot = v if q == 0 else q + 1
                top = [lower[c] + alpha * upper[c] for c in range(2)]
                bottom = [upper[c] + alpha * lower[c] for c in range(2)]
                store_parts(y_parts, at(slot), jnp.concatenate(top, axis=0))
                turned = jnp.concatenate([-sign * bottom[1], sign * bottom[0]], axis=0)
                store_parts(y_parts, at(count + 1 + slot), turned)
    rows = dot(t["near_inverse"][...], y_parts[...])
    blocks = jnp.concatenate([side_by_side(rows[:, at(n)]) for n in range(2 * count + 2)], axis=0)
    out = dot(wide_parts(blocks), t["out_right"][...])
    flux = 0.0
    for half in range(2):
        base = half * (count + 1)
        lefts = [out[at(base), :S]] + [out[at(base + q + 1), :S] for q in range(1, count)]
        rights = [out[at(base + q + 1), S:] for q in range(count)]
        first_ref[at(half)] = lefts[0]
        last_ref[at(half)] = rights[-1]
        middle = mid_bottom if half else mid_top
        together = lefts[0] + rights[-1]
        for q in range(1, count):
            block = lefts[q] + rights[q - 1]
            middle[:, at(q - 1)] = block
            together = together + block
        flux = flux + jnp.sum(together)
    for copy in outs[1:]:
        copy.start()
    lane = lax.broadcasted_iota(jnp.int32, flux_ref.shape, 1)
    flux_ref[...] = jnp.where(lane < H, flux, t["total"][...])
    for copy in outs:
        copy.wait()


def join_kernel(names, parts, *refs):
    total = len(names)
    hbm, fluxes, refs = refs[:total], refs[total : total + parts], refs[total + parts :]
    top_hbm, bottom_hbm, totals_ref = refs[:3]
    buffers, sems, top_ref, bottom_ref = refs[3 : 3 + total], refs[3 + total], refs[4 + total], refs[5 + total]
    t = Copies(names, hbm, buffers, sems)
    outs = []
    for half, out, place in ((0, top_ref, top_hbm), (1, bottom_ref, bottom_hbm)):
        mid = t["mid_bottom" if half else "mid_top"]
        width = mid.shape[1]
        out[:, S : S + width] = mid[...]
        out[:, :S] = t["first"][at(half)] + t["from_left"][at(half)]
        out[:, S + width :] = t["last"][at(half)] + t["from_right"][at(half)]
        outs.append(pltpu.make_async_copy(out, place, sems.at[total + half]))
        outs[-1].start()
    flux = sum([f[...] for f in fluxes[1:]], fluxes[0][...])
    totals_ref[...] = jnp.broadcast_to(flux[None], totals_ref.shape)
    for copy in outs:
        copy.wait()


def gradient_kernel(names, *refs):
    total = len(names)
    hbm, flux_ref, refs = refs[:total], refs[total], refs[total + 1 :]
    residual_hbm, top_hbm, bottom_hbm = refs[:3]
    buffers, sems, (residual_ref, out_top, out_bottom) = refs[3 : 3 + total], refs[3 + total], refs[4 + total : 7 + total]
    r_ref, r_parts, g_parts = refs[7 + total :]
    t = Copies(names, picked(names, hbm), buffers, sems)
    sent = [
        pltpu.make_async_copy(source, out, sems.at[total + n])
        for n, (source, out) in enumerate(
            zip((residual_ref, out_top, out_bottom), (residual_hbm, top_hbm, bottom_hbm))
        )
    ]
    row_edge, column_edge = edges()
    alpha, beta = 1.0 - row_edge.astype(F32), 1.0 - column_edge.astype(F32)
    width = residual_ref.shape[1]
    count = width // S
    sums = jnp.sum(flux_ref[...], axis=0)
    gain = sums[0, H] / sums[0, 0]
    r_ref[:S] = gain * (t["top"][...] + t["above"][...])
    r_ref[S:] = gain * (t["bottom"][...] + t["below"][...])
    r_ref[:S, S:] -= t["obs_above"][...]
    r_ref[S:, S:] -= t["obs"][...]
    r_ref[:S, :S] -= t["obs_diagonal"][...]
    r_ref[S:, :S] -= t["obs_left"][...]
    residual_ref[...] = r_ref[S:, S:]
    sent[0].start()
    near, far = r_ref[:, :S], r_ref[:, S : 2 * S]
    blocks = [
        jnp.concatenate([beta * near, far], axis=1),
        jnp.concatenate([near, beta * far], axis=1),
    ] + [r_ref[:, q * S : (q + 2) * S] for q in range(1, count)]
    lanes = dot(wide_parts(jnp.concatenate(blocks, axis=0)), t["res_right"][...])
    for n in range(count + 1):
        value = lanes[at(n, L)]
        store_parts(r_parts, at(n), stacked(value[:S]))
        store_parts(r_parts, at(count + 1 + n), stacked(value[S:]))
    spectra = dot(t["near_left"][...], r_parts[...])
    sign = alternating()
    spec_ref, more_ref = t["spec"], t["more"]
    seen = []
    for n in range(count + 1):
        top = [spectra[at(c, L), at(n)] for c in range(2)]
        raw = [spectra[at(c, L), at(count + 1 + n)] for c in range(2)]
        bottom = [sign * raw[1], -sign * raw[0]]
        seen.append(
            [
                [bottom[c] + alpha * top[c] for c in range(2)],
                [top[c] + alpha * bottom[c] for c in range(2)],
            ]
        )
    grad_left = t["grad_left"]
    outs = []
    for pair in range(count // 2):
        for q in (2 * pair, 2 * pair + 1):
            for w in range(2):
                slot = w if q == 0 else q + 1
                j = q - w
                for r in range(2):
                    if r == 0:
                        source, lanes = (spec_ref, at(j)) if j >= 0 else (more_ref, at(count + 1))
                    else:
                        source, lanes = more_ref, at(j + 1)
                    h_re, h_im = source[:L, lanes], source[L:, lanes]
                    r_re, r_im = seen[slot][r]
                    for c, part in enumerate((r_re * h_re + r_im * h_im, r_im * h_re - r_re * h_im)):
                        hi, lo = split(part)
                        place = (2 * r + c) * L
                        for n, value in enumerate((hi, lo, hi)):
                            g_parts[4 * n * L + place : 4 * n * L + place + L, at(2 * q + w)] = value
        g = dot(grad_left[...], g_parts[:, pair * 4 * S : (pair + 1) * 4 * S])
        outs += [side_by_side(g[:, at(n)]) for n in range(4)]
    out = dot(wide_parts(jnp.concatenate(outs, axis=0)), t["grad_right"][...])
    for q in range(count):
        windows = t["windows"] if q == 0 else t["plain"]
        grad = gain * (out[at(2 * q)] * windows[0, :1] + out[at(2 * q + 1)] * windows[1, :1])
        out_top[:, at(q)] = grad[:H]
        out_bottom[:, at(q)] = grad[H:]
    for copy in sent[1:]:
        copy.start()
    for copy in sent:
        copy.wait()


def f32(*shape):
    return jax.ShapeDtypeStruct(shape, F32)


def call(kernel, named, ready, outs, scratch, limit, flops, loose=()):
    hbm, vmem = pl.BlockSpec(memory_space=pltpu.HBM), pl.BlockSpec(memory_space=pltpu.VMEM)
    held = [x if n in loose else pltpu.with_memory_space_constraint(x, pltpu.HBM) for n, x in named.items()]
    size = sum(math.prod(x.shape) * x.dtype.itemsize for x in named.values())
    return pl.pallas_call(
        kernel,
        out_shape=[place(o.shape, o.dtype) for place, o in outs],
        in_specs=[hbm] * len(named) + [vmem] * len(ready),
        out_specs=[hbm if place is pltpu.HBM else vmem for place, _ in outs],
        scratch_shapes=scratch,
        compiler_params=pltpu.CompilerParams(vmem_limit_bytes=limit * 2**20),
        cost_estimate=pl.CostEstimate(flops=flops, bytes_accessed=size, transcendentals=0),
    )(*held, *ready.values())


def like(arrays):
    return [pltpu.VMEM(x.shape[1:] if n in PICKED else x.shape, x.dtype) for n, x in arrays.items()]


PICKED = ("windows", "obj_left", "grad_left")


def ring(value, axes, moves):
    sizes = [lax.axis_size(a) for a in axes]
    pairs = []
    for source in np.ndindex(*sizes):
        target = [(p + m) % n for p, m, n in zip(source, moves, sizes)]
        pairs.append((int(np.ravel_multi_index(source, sizes)), int(np.ravel_multi_index(target, sizes))))
    return lax.ppermute(value, axes, pairs)


def mirrored(value, axis, bits):
    count = lax.axis_size(axis)
    return lax.ppermute(value, axis, [(s, s ^ bits) for s in range(count)])


def runs():
    count = lax.axis_size("sy")
    return 4 if count % 4 == 0 else count


def exchanged(value):
    count_y, count_x, run = lax.axis_size("sy"), lax.axis_size("sx"), runs()
    index = np.arange(count_y * count_x).reshape(count_y // run, run, count_x)
    groups = index.transpose(1, 0, 2).reshape(run, -1).tolist()
    return lax.all_to_all(value, ("sy", "sx"), 0, 0, axis_index_groups=groups)


def down(value):
    return ring(value, ("sy",), (1,))


def up(value):
    return ring(value, ("sy",), (-1,))


def per_device(object_field, frames_data, patch_psfs):
    rows, width = object_field.shape
    count = width // S
    psfs = patch_psfs.reshape(count, S, S)
    observed = frames_data[0]
    t = {name: jnp.asarray(value) for name, value in tables().items()}
    psf_above = down(psfs)
    pack_down, pack_right, pack_diagonal, obs_last = pl.pallas_call(
        pack_kernel,
        out_shape=(f32(H, width), f32(S + H, S), f32(S + H, S), f32(S, S)),
    )(object_field, observed, psfs)
    obj_above = down(pack_down)
    got_diagonal = ring(pack_diagonal, ("sy", "sx"), (1, 1))
    got_right = ring(pack_right, ("sx",), (1,))
    obs_above = down(observed)
    obs_left = ring(obs_last, ("sx",), (1,))
    obs_diagonal = ring(obs_last, ("sy", "sx"), (1, 1))

    kept = {k: t[k] for k in ("near_right", "near_left", "windows", "obj_left", "near_inverse", "out_right")}
    named = {"psf": psfs, "frame": observed} | kept
    spec, spec_here, total, *got = call(
        functools.partial(psf_kernel, tuple(named)),
        named,
        {},
        [(pltpu.HBM, f32(2 * L, width)), (pltpu.VMEM, f32(2 * L, width)), (pltpu.VMEM, f32(8, S))]
        + [(pltpu.VMEM, x) for x in like(kept)],
        [pltpu.VMEM(psfs.shape, F32), pltpu.VMEM(observed.shape, F32),
         pltpu.SemaphoreType.DMA((len(named) + 1,)), pltpu.VMEM((6 * S, width), BF16)],
        16,
        6 * 84 * 10**6,
    )
    ready = dict(zip(kept, got)) | {"spec": spec_here, "total": total, "plain": t["windows"][0]}
    named = {"right": got_right, "diagonal": got_diagonal, "above": obj_above, "own": object_field,
             "psf_above": psf_above}
    outs = [f32(2 * L, width + 2 * S), f32(S, width - S), f32(S, width - S), f32(L, S), f32(L, S)]
    more, mid_top, mid_bottom, first, last, flux = call(
        functools.partial(model_kernel, tuple(named), tuple(ready)),
        named,
        ready,
        [(pltpu.HBM, o) for o in outs] + [(pltpu.VMEM, f32(8, S))],
        like(named) + [pltpu.SemaphoreType.DMA((len(named) + len(outs),))]
        + [pltpu.VMEM(o.shape, F32) for o in outs]
        + [pltpu.VMEM((2 * width, S), F32), pltpu.VMEM((6 * S, 3 * width + 2 * S), BF16),
           pltpu.VMEM((6 * L, 2 * width + 2 * S), BF16)],
        36,
        6 * 600 * 10**6,
        ("right", "diagonal", "above", "psf_above"),
    )
    mid_top, mid_bottom, first, last, flux, obs_above, obs_left, obs_diagonal = lax.optimization_barrier(
        (mid_top, mid_bottom, first, last, flux, obs_above, obs_left, obs_diagonal)
    )
    from_right = ring(first, ("sx",), (-1,))
    from_left = ring(last, ("sx",), (1,))
    fluxes = [flux] + [mirrored(flux, "sy", k) for k in range(1, runs())]
    named = {"mid_top": mid_top, "mid_bottom": mid_bottom, "first": first, "from_left": from_left,
             "last": last, "from_right": from_right}
    outs = [f32(S, width + S)] * 2
    top, bottom, flux = call(
        functools.partial(join_kernel, tuple(named), len(fluxes)),
        named,
        dict(enumerate(fluxes)),
        [(pltpu.HBM, o) for o in outs]
        + [(pltpu.VMEM, f32(lax.axis_size("sy") // runs() * lax.axis_size("sx"), 8, S))],
        like(named) + [pltpu.SemaphoreType.DMA((len(named) + len(outs),))] + [pltpu.VMEM(o.shape, F32) for o in outs],
        16,
        10**6,
        ("from_left", "from_right"),
    )
    below = up(top)
    above = down(bottom)
    flux = exchanged(flux)

    named = {"top": top, "above": above, "bottom": bottom, "below": below,
             "obs_above": obs_above, "obs": observed,
             "obs_diagonal": obs_diagonal, "obs_left": obs_left,
             "res_right": t["res_right"], "near_left": t["near_left"], "spec": spec, "more": more,
             "grad_left": t["grad_left"], "grad_right": t["grad_right"],
             "windows": t["windows"], "plain": t["windows"][0]}
    outs = [f32(S, width), f32(H, width), f32(H, width)]
    residual, g_top, g_bottom = call(
        functools.partial(gradient_kernel, tuple(named)),
        named,
        {"flux": flux},
        [(pltpu.HBM, o) for o in outs],
        like(named) + [pltpu.SemaphoreType.DMA((len(named) + len(outs),))]
        + [pltpu.VMEM(o.shape, F32) for o in outs]
        + [pltpu.VMEM((L, width + S), F32), pltpu.VMEM((6 * S, 2 * width + 2 * S), BF16),
           pltpu.VMEM((12 * L, 2 * width), BF16)],
        44,
        6 * 500 * 10**6,
        ("above", "below", "obs_above", "obs_diagonal", "obs_left"),
    )
    bottom_other = mirrored(g_bottom, "fr", 1)
    top_other = ring(g_top, ("sy", "fr"), (-1, 1))
    top_same = up(g_top)
    total = jnp.concatenate([g_bottom + bottom_other, top_same + top_other], axis=0)
    side = ring(total[:, :H], ("sx",), (-1,))
    gradient = jnp.concatenate([total[:, H:], side], axis=1)
    return gradient, residual[None]


def solution(mesh):
    placed = (P("sy", "sx"), P("fr", "sy", "sx"), P("fr", "sy", "sx", None, None))
    return jax.shard_map(
        per_device,
        mesh=mesh,
        in_specs=placed,
        out_specs=(P("sy", "sx"), P("fr", "sy", "sx")),
        check_vma=False,
    )
```

```python
import functools
import math

import jax
import jax.numpy as jnp
import numpy as np
from jax import lax
from jax.experimental import pallas as pl
from jax.experimental.pallas import tpu as pltpu
from jax.sharding import PartitionSpec as P

S = 128
L = 256
H = 64
F32 = jnp.float32
BF16 = jnp.bfloat16


def half_windows():
    n = np.arange(L, dtype=np.float64)
    s = np.sin(np.pi * (n + 0.5) / L) ** 2
    return s[:S], s[S:]


def phases(freqs, positions):
    product = (2 * np.arange(freqs)[:, None] + 1) * positions[None, :] % (2 * L)
    angle = product.astype(np.float64) * (math.pi / L)
    return np.cos(angle), np.sin(angle)


def forward_left(positions):
    c, s = phases(L, positions)
    return np.block([[c, s], [-s, c]])


def inverse_left(positions):
    c, s = phases(L, positions)
    return np.block([[c.T, -s.T], [s.T, c.T]]) / L


def forward_right(positions):
    c, s = phases(S, positions)
    return np.concatenate([c.T, -s.T], axis=1)


def inverse_right(positions):
    c, s = phases(S, positions)
    return np.concatenate([c, -s], axis=0) * (2.0 / L)


def bf16_parts(table):
    hi = table.astype(np.float32).astype(BF16)
    lo = (table - hi.astype(np.float64)).astype(np.float32).astype(BF16)
    return hi, lo


def left_table(table):
    hi, lo = bf16_parts(table)
    return np.concatenate([hi, hi, lo], axis=-1)


def right_table(table):
    hi, lo = bf16_parts(table)
    return np.concatenate([hi, hi, lo], axis=-2)


@functools.lru_cache(maxsize=1)
def tables():
    near = np.arange(S)
    up, down = half_windows()
    pairs = ((up, down), (np.where(near < H, 0.0, up), np.where(near < H, down, 0.0)))
    base, back = forward_left(near), inverse_left(near)
    t = {}
    t["near_right"] = right_table(forward_right(near))
    t["near_left"] = left_table(base)
    t["obj_left"] = np.stack(
        [left_table(np.concatenate([base * np.tile(w, 2)[None, :] for w in pair], axis=0)) for pair in pairs]
    )
    t["near_inverse"] = left_table(back)
    t["out_right"] = right_table(inverse_right(np.arange(L)))
    t["res_right"] = right_table(forward_right(np.arange(L)))
    t["grad_left"] = np.stack(
        [left_table(np.concatenate([np.tile(w, 2)[:, None] * back for w in pair], axis=1)) for pair in pairs]
    )
    t["grad_right"] = right_table(inverse_right(near))
    t["windows"] = np.stack([np.stack([np.tile(w, (8, 1)) for w in pair]) for pair in pairs]).astype(np.float32)
    return t


def split(value):
    hi = value.astype(BF16)
    return hi, (value - hi.astype(F32)).astype(BF16)


def wide_parts(value):
    hi, lo = split(value)
    return jnp.concatenate([hi, lo, hi], axis=1)


def store_parts(ref, lanes, value):
    hi, lo = split(value)
    depth = value.shape[0]
    ref[:depth, lanes] = hi
    ref[depth : 2 * depth, lanes] = lo
    ref[2 * depth :, lanes] = hi


def dot(a, b):
    return jnp.dot(a, b, preferred_element_type=F32)


def stacked(value):
    half = value.shape[1] // 2
    return jnp.concatenate([value[:, :half], value[:, half:]], axis=0)


def side_by_side(value):
    half = value.shape[0] // 2
    return jnp.concatenate([value[:half], value[half:]], axis=1)


def at(n, size=S):
    return slice(n * size, (n + 1) * size)


class Copies:
    def __init__(self, names, sources, refs, semaphores):
        self.buffers = dict(zip(names, refs))
        self.copies = {
            name: pltpu.make_async_copy(source, buffer, semaphores.at[n])
            for n, (name, source, buffer) in enumerate(zip(names, sources, refs))
        }
        self.waited = set()
        for name in names:
            self.copies[name].start()

    def __getitem__(self, name):
        if name not in self.waited:
            self.waited.add(name)
            self.copies[name].wait()
        return self.buffers[name]


def edges():
    return [(lax.axis_index(axis) == 0).astype(jnp.int32) for axis in ("sy", "sx")]


def picked(names, hbm):
    rows, columns = edges()
    edge = {"obj_left": rows, "grad_left": rows, "windows": columns}
    part = {"right": pl.ds(0, S + H), "obs_left": pl.ds(S + H, S)}
    return [h.at[edge[n]] if n in edge else h.at[part[n]] if n in part else h for n, h in zip(names, hbm)]


def psf_kernel(names, *refs):
    total = len(names)
    hbm, refs = refs[:total], refs[total:]
    down_hbm, right_hbm, diagonal_hbm, frame_hbm, spec_hbm, spec_ref, total_ref, *buffers = refs[:-5]
    psf, obj, frame, sems, parts = refs[-5:]
    t = Copies(names, picked(names, hbm), (psf, obj, frame) + tuple(buffers), sems)
    count, last = psf.shape[0], pl.ds(obj.shape[1] - S, S)
    psf, obj, frame = t["psf"], t["object"], t["frame"]
    moves = [
        (obj.at[pl.ds(H, H)], down_hbm),
        (psf.at[count - 1], right_hbm.at[pl.ds(0, S)]),
        (obj.at[pl.ds(0, H), last], right_hbm.at[pl.ds(S, H)]),
        (frame.at[:, last], right_hbm.at[pl.ds(S + H, S)]),
        (psf.at[count - 1], diagonal_hbm.at[pl.ds(0, S)]),
        (obj.at[pl.ds(H, H), last], diagonal_hbm.at[pl.ds(S, H)]),
        (frame.at[:, last], frame_hbm),
    ]
    moves = [pltpu.make_async_copy(*move, sems.at[total + 1 + n]) for n, move in enumerate(moves)]
    for copy in moves:
        copy.start()
    lanes = dot(wide_parts(jnp.concatenate([psf[j] for j in range(count)], axis=0)), t["near_right"][...])
    for j in range(count):
        store_parts(parts, at(j), stacked(lanes[at(j)]))
    spec_ref[...] = dot(t["near_left"][...], parts[...])
    out = pltpu.make_async_copy(spec_ref, spec_hbm, sems.at[total])
    out.start()
    total_ref[...] = jnp.full(total_ref.shape, jnp.sum(t["frame"][...]), F32)
    for name in names:
        t[name]
    for copy in moves + [out]:
        copy.wait()


def above_kernel(psf_hbm, right, left, spec_hbm, spec_ref, psf, sems, parts):
    t = Copies(("psf",), (psf_hbm,), (psf,), sems)
    count = psf.shape[0]
    lanes = dot(wide_parts(jnp.concatenate([t["psf"][j] for j in range(count)], axis=0)), right[...])
    for j in range(count):
        store_parts(parts, at(j), stacked(lanes[at(j)]))
    spec_ref[...] = dot(left[...], parts[...])
    out = pltpu.make_async_copy(spec_ref, spec_hbm, sems.at[1])
    out.start()
    out.wait()


def alternating():
    k = lax.broadcasted_iota(jnp.int32, (L, S), 0)
    return jnp.where(k % 2 == 0, 1.0, -1.0).astype(F32)


def model_kernel(names, ready, *refs):
    total = len(names)
    hbm, refs = refs[:total], refs[total:]
    t, refs = dict(zip(ready, refs)), refs[len(ready) :]
    outs_hbm, flux_ref, refs = refs[:5], refs[5], refs[6:]
    buffers, sems, (more_ref, mid_top, mid_bottom, first_ref, last_ref) = refs[:total], refs[total], refs[total + 1 : total + 6]
    x_ref, x_parts, y_parts = refs[total + 6 :]
    got = Copies(names, picked(names, hbm), buffers, sems)
    outs = [
        pltpu.make_async_copy(source, out, sems.at[total + n])
        for n, (source, out) in enumerate(zip((more_ref, mid_top, mid_bottom, first_ref, last_ref), outs_hbm))
    ]
    row_edge, column_edge = edges()
    alpha, beta = 1.0 - row_edge.astype(F32), 1.0 - column_edge.astype(F32)
    right_ref, diagonal_ref, above_ref, own_ref = [got[n] for n in ("right", "diagonal", "above", "own")]
    count = own_ref.shape[1] // S
    windows = [t["windows"][w, :1] for w in range(2)]
    plain = [t["plain"][w, :1] for w in range(2)]
    for q in range(count):
        lo = q * S
        if q == 0:
            left = jnp.concatenate([diagonal_ref[S:], right_ref[S:]], axis=0)[:, H:]
        else:
            left = jnp.concatenate([above_ref[:, lo - S : lo], own_ref[:H, lo - S : lo]], axis=0)[:, H:]
        here = jnp.concatenate([above_ref[:, lo : lo + S], own_ref[:H, lo : lo + S]], axis=0)[:, :H]
        x = jnp.concatenate([left, here], axis=1)
        for w in range(2):
            x_ref[at(2 * q + w)] = x * (windows if q == 0 else plain)[w]
    psfs = [diagonal_ref[:S], right_ref[:S]]
    lanes = dot(wide_parts(jnp.concatenate([x_ref[...]] + psfs, axis=0)), t["near_right"][...])
    for n in range(2 * count + 2):
        store_parts(x_parts, at(n), stacked(lanes[at(n)]))
    more_ref[...] = dot(t["near_left"][...], x_parts[:, 2 * count * S :])
    outs[0].start()
    spec_ref, spec_above = t["spec"], t["spec_above"]
    obj_left = t["obj_left"]
    sign = alternating()
    for pair in range(count // 2):
        x_specs = dot(obj_left[...], x_parts[:, pair * 4 * S : (pair + 1) * 4 * S])
        for q in (2 * pair, 2 * pair + 1):
            y = {}
            for r in range(2):
                for w in range(2):
                    lanes = at(2 * (q % 2) + w)
                    x_re = x_specs[at(2 * r, L), lanes]
                    x_im = x_specs[at(2 * r + 1, L), lanes]
                    j = q - w
                    own = (spec_ref, spec_above)[r]
                    source, lanes = (own, at(j)) if j >= 0 else (more_ref, at(1 - r))
                    h_re, h_im = source[:L, lanes], source[L:, lanes]
                    y[r, w] = (x_re * h_re - x_im * h_im, x_re * h_im + x_im * h_re)
            if q == 0:
                variants = [
                    [tuple(y[r, 1][c] + beta * y[r, 0][c] for c in range(2)) for r in range(2)],
                    [tuple(y[r, 0][c] + beta * y[r, 1][c] for c in range(2)) for r in range(2)],
                ]
            else:
                variants = [[tuple(y[r, 0][c] + y[r, 1][c] for c in range(2)) for r in range(2)]]
            for v, (upper, lower) in enumerate(variants):
                slot = v if q == 0 else q + 1
                top = [lower[c] + alpha * upper[c] for c in range(2)]
                bottom = [upper[c] + alpha * lower[c] for c in range(2)]
                store_parts(y_parts, at(slot), jnp.concatenate(top, axis=0))
                turned = jnp.concatenate([-sign * bottom[1], sign * bottom[0]], axis=0)
                store_parts(y_parts, at(count + 1 + slot), turned)
    rows = dot(t["near_inverse"][...], y_parts[...])
    blocks = jnp.concatenate([side_by_side(rows[:, at(n)]) for n in range(2 * count + 2)], axis=0)
    out = dot(wide_parts(blocks), t["out_right"][...])
    flux = 0.0
    for half in range(2):
        base = half * (count + 1)
        lefts = [out[at(base), :S]] + [out[at(base + q + 1), :S] for q in range(1, count)]
        rights = [out[at(base + q + 1), S:] for q in range(count)]
        first_ref[at(half)] = lefts[0]
        last_ref[at(half)] = rights[-1]
        middle = mid_bottom if half else mid_top
        together = lefts[0] + rights[-1]
        for q in range(1, count):
            block = lefts[q] + rights[q - 1]
            middle[:, at(q - 1)] = block
            together = together + block
        flux = flux + jnp.sum(together)
    for copy in outs[1:]:
        copy.start()
    lane = lax.broadcasted_iota(jnp.int32, flux_ref.shape, 1)
    flux_ref[...] = jnp.where(lane < H, flux, t["total"][...])
    for copy in outs:
        copy.wait()


def join_kernel(names, parts, *refs):
    total = len(names)
    hbm, fluxes, refs = refs[:total], refs[total : total + parts], refs[total + parts :]
    top_hbm, bottom_hbm, totals_ref = refs[:3]
    buffers, sems, top_ref, bottom_ref = refs[3 : 3 + total], refs[3 + total], refs[4 + total], refs[5 + total]
    t = Copies(names, hbm, buffers, sems)
    outs = []
    for half, out, place in ((0, top_ref, top_hbm), (1, bottom_ref, bottom_hbm)):
        mid = t["mid_bottom" if half else "mid_top"]
        width = mid.shape[1]
        out[:, S : S + width] = mid[...]
        out[:, :S] = t["first"][at(half)] + t["from_left"][at(half)]
        out[:, S + width :] = t["last"][at(half)] + t["from_right"][at(half)]
        outs.append(pltpu.make_async_copy(out, place, sems.at[total + half]))
        outs[-1].start()
    flux = sum([f[...] for f in fluxes[1:]], fluxes[0][...])
    totals_ref[...] = jnp.broadcast_to(flux[None], totals_ref.shape)
    for copy in outs:
        copy.wait()


def gradient_kernel(names, *refs):
    total = len(names)
    hbm, flux_ref, refs = refs[:total], refs[total], refs[total + 1 :]
    residual_hbm, top_hbm, bottom_hbm = refs[:3]
    buffers, sems, (residual_ref, out_top, out_bottom) = refs[3 : 3 + total], refs[3 + total], refs[4 + total : 7 + total]
    r_ref, r_parts, g_parts = refs[7 + total :]
    t = Copies(names, picked(names, hbm), buffers, sems)
    sent = [
        pltpu.make_async_copy(source, out, sems.at[total + n])
        for n, (source, out) in enumerate(
            zip((residual_ref, out_top, out_bottom), (residual_hbm, top_hbm, bottom_hbm))
        )
    ]
    row_edge, column_edge = edges()
    alpha, beta = 1.0 - row_edge.astype(F32), 1.0 - column_edge.astype(F32)
    width = residual_ref.shape[1]
    count = width // S
    sums = jnp.sum(flux_ref[...], axis=0)
    gain = sums[0, H] / sums[0, 0]
    r_ref[:S] = gain * (t["top"][...] + t["above"][...])
    r_ref[S:] = gain * (t["bottom"][...] + t["below"][...])
    r_ref[:S, S:] -= t["obs_above"][...]
    r_ref[S:, S:] -= t["obs"][...]
    r_ref[:S, :S] -= t["obs_diagonal"][...]
    r_ref[S:, :S] -= t["obs_left"][...]
    residual_ref[...] = r_ref[S:, S:]
    sent[0].start()
    near, far = r_ref[:, :S], r_ref[:, S : 2 * S]
    blocks = [
        jnp.concatenate([beta * near, far], axis=1),
        jnp.concatenate([near, beta * far], axis=1),
    ] + [r_ref[:, q * S : (q + 2) * S] for q in range(1, count)]
    lanes = dot(wide_parts(jnp.concatenate(blocks, axis=0)), t["res_right"][...])
    for n in range(count + 1):
        value = lanes[at(n, L)]
        store_parts(r_parts, at(n), stacked(value[:S]))
        store_parts(r_parts, at(count + 1 + n), stacked(value[S:]))
    spectra = dot(t["near_left"][...], r_parts[...])
    sign = alternating()
    spec_ref, spec_above, more_ref = t["spec"], t["spec_above"], t["more"]
    seen = []
    for n in range(count + 1):
        top = [spectra[at(c, L), at(n)] for c in range(2)]
        raw = [spectra[at(c, L), at(count + 1 + n)] for c in range(2)]
        bottom = [sign * raw[1], -sign * raw[0]]
        seen.append(
            [
                [bottom[c] + alpha * top[c] for c in range(2)],
                [top[c] + alpha * bottom[c] for c in range(2)],
            ]
        )
    grad_left = t["grad_left"]
    outs = []
    for pair in range(count // 2):
        for q in (2 * pair, 2 * pair + 1):
            for w in range(2):
                slot = w if q == 0 else q + 1
                j = q - w
                for r in range(2):
                    own = (spec_ref, spec_above)[r]
                    source, lanes = (own, at(j)) if j >= 0 else (more_ref, at(1 - r))
                    h_re, h_im = source[:L, lanes], source[L:, lanes]
                    r_re, r_im = seen[slot][r]
                    for c, part in enumerate((r_re * h_re + r_im * h_im, r_im * h_re - r_re * h_im)):
                        hi, lo = split(part)
                        place = (2 * r + c) * L
                        for n, value in enumerate((hi, lo, hi)):
                            g_parts[4 * n * L + place : 4 * n * L + place + L, at(2 * q + w)] = value
        g = dot(grad_left[...], g_parts[:, pair * 4 * S : (pair + 1) * 4 * S])
        outs += [side_by_side(g[:, at(n)]) for n in range(4)]
    out = dot(wide_parts(jnp.concatenate(outs, axis=0)), t["grad_right"][...])
    for q in range(count):
        windows = t["windows"] if q == 0 else t["plain"]
        grad = gain * (out[at(2 * q)] * windows[0, :1] + out[at(2 * q + 1)] * windows[1, :1])
        out_top[:, at(q)] = grad[:H]
        out_bottom[:, at(q)] = grad[H:]
    for copy in sent[1:]:
        copy.start()
    for copy in sent:
        copy.wait()


def f32(*shape):
    return jax.ShapeDtypeStruct(shape, F32)


def call(kernel, named, ready, outs, scratch, limit, flops, loose=()):
    hbm, vmem = pl.BlockSpec(memory_space=pltpu.HBM), pl.BlockSpec(memory_space=pltpu.VMEM)
    held = [x if n in loose else pltpu.with_memory_space_constraint(x, pltpu.HBM) for n, x in named.items()]
    size = sum(math.prod(x.shape) * x.dtype.itemsize for x in named.values())
    return pl.pallas_call(
        kernel,
        out_shape=[place(o.shape, o.dtype) for place, o in outs],
        in_specs=[hbm] * len(named) + [vmem] * len(ready),
        out_specs=[hbm if place is pltpu.HBM else vmem for place, _ in outs],
        scratch_shapes=scratch,
        compiler_params=pltpu.CompilerParams(vmem_limit_bytes=limit * 2**20),
        cost_estimate=pl.CostEstimate(flops=flops, bytes_accessed=size, transcendentals=0),
    )(*held, *ready.values())


def like(arrays):
    shapes = {"right": (S + H, S), "obs_left": (S, S)}
    shapes |= {n: arrays[n].shape[1:] for n in ("windows", "obj_left", "grad_left") if n in arrays}
    return [pltpu.VMEM(shapes.get(n, x.shape), x.dtype) for n, x in arrays.items()]


def ring(value, axes, moves):
    sizes = [lax.axis_size(a) for a in axes]
    pairs = []
    for source in np.ndindex(*sizes):
        target = [(p + m) % n for p, m, n in zip(source, moves, sizes)]
        pairs.append((int(np.ravel_multi_index(source, sizes)), int(np.ravel_multi_index(target, sizes))))
    return lax.ppermute(value, axes, pairs)


def mirrored(value, axis, bits):
    count = lax.axis_size(axis)
    return lax.ppermute(value, axis, [(s, s ^ bits) for s in range(count)])


def runs():
    count = lax.axis_size("sy")
    return 4 if count % 4 == 0 else count


def exchanged(value):
    count_y, count_x, run = lax.axis_size("sy"), lax.axis_size("sx"), runs()
    index = np.arange(count_y * count_x).reshape(count_y // run, run, count_x)
    groups = index.transpose(1, 0, 2).reshape(run, -1).tolist()
    return lax.all_to_all(value, ("sy", "sx"), 0, 0, axis_index_groups=groups)


def down(value):
    return ring(value, ("sy",), (1,))


def up(value):
    return ring(value, ("sy",), (-1,))


def per_device(object_field, frames_data, patch_psfs):
    rows, width = object_field.shape
    count = width // S
    psfs = patch_psfs.reshape(count, S, S)
    observed = frames_data[0]
    t = {name: jnp.asarray(value) for name, value in tables().items()}
    psf_above = down(psfs)
    kept = {k: t[k] for k in ("near_right", "near_left", "windows", "obj_left", "near_inverse", "out_right")}
    named = {"psf": psfs, "object": object_field, "frame": observed} | kept
    pack_down, pack_right, pack_diagonal, obs_last, spec, spec_here, total, *got = call(
        functools.partial(psf_kernel, tuple(named)),
        named,
        {},
        [(pltpu.HBM, f32(H, width)), (pltpu.HBM, f32(2 * S + H, S)), (pltpu.HBM, f32(S + H, S)),
         (pltpu.HBM, f32(S, S)),
         (pltpu.HBM, f32(2 * L, width)), (pltpu.VMEM, f32(2 * L, width)), (pltpu.VMEM, f32(8, S))]
        + [(pltpu.VMEM, x) for x in like(kept)],
        [pltpu.VMEM(psfs.shape, F32), pltpu.VMEM(object_field.shape, F32), pltpu.VMEM(observed.shape, F32),
         pltpu.SemaphoreType.DMA((len(named) + 8,)), pltpu.VMEM((6 * S, width), BF16)],
        16,
        6 * 84 * 10**6,
    )
    obj_above = down(pack_down)
    got_diagonal = ring(pack_diagonal, ("sy", "sx"), (1, 1))
    got_right = ring(pack_right, ("sx",), (1,))
    obs_above = down(observed)
    obs_diagonal = ring(obs_last, ("sy", "sx"), (1, 1))
    ready = dict(zip(kept, got))
    spec_above, spec_above_here = call(
        above_kernel,
        {"psf": psf_above},
        {k: ready[k] for k in ("near_right", "near_left")},
        [(pltpu.HBM, f32(2 * L, width)), (pltpu.VMEM, f32(2 * L, width))],
        [pltpu.VMEM(psfs.shape, F32), pltpu.SemaphoreType.DMA((2,)), pltpu.VMEM((6 * S, width), BF16)],
        16,
        6 * 84 * 10**6,
        ("psf",),
    )
    ready |= {"spec_above": spec_above_here, "spec": spec_here, "total": total, "plain": t["windows"][0]}
    named = {"right": got_right, "diagonal": got_diagonal, "above": obj_above, "own": object_field}
    outs = [f32(2 * L, 2 * S), f32(S, width - S), f32(S, width - S), f32(L, S), f32(L, S)]
    more, mid_top, mid_bottom, first, last, flux = call(
        functools.partial(model_kernel, tuple(named), tuple(ready)),
        named,
        ready,
        [(pltpu.HBM, o) for o in outs] + [(pltpu.VMEM, f32(8, S))],
        like(named) + [pltpu.SemaphoreType.DMA((len(named) + len(outs),))]
        + [pltpu.VMEM(o.shape, F32) for o in outs]
        + [pltpu.VMEM((2 * width, S), F32), pltpu.VMEM((6 * S, 2 * width + 2 * S), BF16),
           pltpu.VMEM((6 * L, 2 * width + 2 * S), BF16)],
        36,
        6 * 600 * 10**6,
        ("right", "diagonal", "above"),
    )
    mid_top, mid_bottom, first, last, flux, obs_above, obs_diagonal = lax.optimization_barrier(
        (mid_top, mid_bottom, first, last, flux, obs_above, obs_diagonal)
    )
    from_right = ring(first, ("sx",), (-1,))
    from_left = ring(last, ("sx",), (1,))
    fluxes = [flux] + [mirrored(flux, "sy", k) for k in range(1, runs())]
    named = {"mid_top": mid_top, "mid_bottom": mid_bottom, "first": first, "from_left": from_left,
             "last": last, "from_right": from_right}
    outs = [f32(S, width + S)] * 2
    top, bottom, flux = call(
        functools.partial(join_kernel, tuple(named), len(fluxes)),
        named,
        dict(enumerate(fluxes)),
        [(pltpu.HBM, o) for o in outs]
        + [(pltpu.VMEM, f32(lax.axis_size("sy") // runs() * lax.axis_size("sx"), 8, S))],
        like(named) + [pltpu.SemaphoreType.DMA((len(named) + len(outs),))] + [pltpu.VMEM(o.shape, F32) for o in outs],
        16,
        10**6,
        ("from_left", "from_right"),
    )
    below = up(top)
    above = down(bottom)
    flux = exchanged(flux)

    named = {"top": top, "above": above, "bottom": bottom, "below": below,
             "obs_above": obs_above, "obs": observed,
             "obs_diagonal": obs_diagonal, "obs_left": got_right,
             "res_right": t["res_right"], "near_left": t["near_left"], "spec": spec, "spec_above": spec_above, "more": more,
             "grad_left": t["grad_left"], "grad_right": t["grad_right"],
             "windows": t["windows"], "plain": t["windows"][0]}
    outs = [f32(S, width), f32(H, width), f32(H, width)]
    residual, g_top, g_bottom = call(
        functools.partial(gradient_kernel, tuple(named)),
        named,
        {"flux": flux},
        [(pltpu.HBM, o) for o in outs],
        like(named) + [pltpu.SemaphoreType.DMA((len(named) + len(outs),))]
        + [pltpu.VMEM(o.shape, F32) for o in outs]
        + [pltpu.VMEM((L, width + S), F32), pltpu.VMEM((6 * S, 2 * width + 2 * S), BF16),
           pltpu.VMEM((12 * L, 2 * width), BF16)],
        44,
        6 * 500 * 10**6,
        ("above", "below", "obs_above", "obs_diagonal", "obs_left"),
    )
    bottom_other = mirrored(g_bottom, "fr", 1)
    top_other = ring(g_top, ("sy", "fr"), (-1, 1))
    top_same = up(g_top)
    total = jnp.concatenate([g_bottom + bottom_other, top_same + top_other], axis=0)
    side = ring(total[:, :H], ("sx",), (-1,))
    gradient = jnp.concatenate([total[:, H:], side], axis=1)
    return gradient, residual[None]


def solution(mesh):
    placed = (P("sy", "sx"), P("fr", "sy", "sx"), P("fr", "sy", "sx", None, None))
    return jax.shard_map(
        per_device,
        mesh=mesh,
        in_specs=placed,
        out_specs=(P("sy", "sx"), P("fr", "sy", "sx")),
        check_vma=False,
    )
```

```python
import functools
import math

import jax
import jax.numpy as jnp
import numpy as np
from jax import lax
from jax.experimental import pallas as pl
from jax.experimental.pallas import tpu as pltpu
from jax.sharding import PartitionSpec as P

S = 128
L = 256
H = 64
F32 = jnp.float32
BF16 = jnp.bfloat16


def half_windows():
    n = np.arange(L, dtype=np.float64)
    s = np.sin(np.pi * (n + 0.5) / L) ** 2
    return s[:S], s[S:]


def phases(freqs, positions):
    product = (2 * np.arange(freqs)[:, None] + 1) * positions[None, :] % (2 * L)
    angle = product.astype(np.float64) * (math.pi / L)
    return np.cos(angle), np.sin(angle)


def forward_left(positions):
    c, s = phases(L, positions)
    return np.block([[c, s], [-s, c]])


def inverse_left(positions):
    c, s = phases(L, positions)
    return np.block([[c.T, -s.T], [s.T, c.T]]) / L


def forward_right(positions):
    c, s = phases(S, positions)
    return np.concatenate([c.T, -s.T], axis=1)


def inverse_right(positions):
    c, s = phases(S, positions)
    return np.concatenate([c, -s], axis=0) * (2.0 / L)


def bf16_parts(table):
    hi = table.astype(np.float32).astype(BF16)
    lo = (table - hi.astype(np.float64)).astype(np.float32).astype(BF16)
    return hi, lo


def left_table(table):
    hi, lo = bf16_parts(table)
    return np.concatenate([hi, hi, lo], axis=-1)


def right_table(table):
    hi, lo = bf16_parts(table)
    return np.concatenate([hi, hi, lo], axis=-2)


@functools.lru_cache(maxsize=1)
def tables():
    near = np.arange(S)
    up, down = half_windows()
    pairs = ((up, down), (np.where(near < H, 0.0, up), np.where(near < H, down, 0.0)))
    base, back = forward_left(near), inverse_left(near)
    t = {}
    t["near_right"] = right_table(forward_right(near))
    t["near_left"] = left_table(base)
    t["obj_left"] = np.stack(
        [left_table(np.concatenate([base * np.tile(w, 2)[None, :] for w in pair], axis=0)) for pair in pairs]
    )
    t["near_inverse"] = left_table(back)
    t["out_right"] = right_table(inverse_right(np.arange(L)))
    t["res_right"] = right_table(forward_right(np.arange(L)))
    t["grad_left"] = np.stack(
        [left_table(np.concatenate([np.tile(w, 2)[:, None] * back for w in pair], axis=1)) for pair in pairs]
    )
    t["grad_right"] = right_table(inverse_right(near))
    t["windows"] = np.stack([np.stack([np.tile(w, (8, 1)) for w in pair]) for pair in pairs]).astype(np.float32)
    return t


def split(value):
    hi = value.astype(BF16)
    return hi, (value - hi.astype(F32)).astype(BF16)


def wide_parts(value):
    hi, lo = split(value)
    return jnp.concatenate([hi, lo, hi], axis=1)


def store_parts(ref, lanes, value):
    hi, lo = split(value)
    depth = value.shape[0]
    ref[:depth, lanes] = hi
    ref[depth : 2 * depth, lanes] = lo
    ref[2 * depth :, lanes] = hi


def dot(a, b):
    return jnp.dot(a, b, preferred_element_type=F32)


def stacked(value):
    half = value.shape[1] // 2
    return jnp.concatenate([value[:, :half], value[:, half:]], axis=0)


def side_by_side(value):
    half = value.shape[0] // 2
    return jnp.concatenate([value[:half], value[half:]], axis=1)


def at(n, size=S):
    return slice(n * size, (n + 1) * size)


class Copies:
    def __init__(self, names, sources, refs, semaphores):
        self.buffers = dict(zip(names, refs))
        self.copies = {
            name: pltpu.make_async_copy(source, buffer, semaphores.at[n])
            for n, (name, source, buffer) in enumerate(zip(names, sources, refs))
        }
        self.waited = set()
        for name in names:
            self.copies[name].start()

    def __getitem__(self, name):
        if name not in self.waited:
            self.waited.add(name)
            self.copies[name].wait()
        return self.buffers[name]


def edges():
    return [(lax.axis_index(axis) == 0).astype(jnp.int32) for axis in ("sy", "sx")]


def picked(names, hbm):
    rows, columns = edges()
    edge = {"obj_left": rows, "grad_left": rows, "windows": columns}
    part = {"right": pl.ds(0, S + H), "obs_left": pl.ds(S + H, S)}
    return [h.at[edge[n]] if n in edge else h.at[part[n]] if n in part else h for n, h in zip(names, hbm)]


def psf_kernel(names, *refs):
    total = len(names)
    hbm, refs = refs[:total], refs[total:]
    down_hbm, right_hbm, diagonal_hbm, frame_hbm, spec_hbm, spec_ref, total_ref, *buffers = refs[:-5]
    psf, obj, frame, sems, parts = refs[-5:]
    t = Copies(names, picked(names, hbm), (psf, obj, frame) + tuple(buffers), sems)
    count, last = psf.shape[0], pl.ds(obj.shape[1] - S, S)
    psf, obj, frame = t["psf"], t["object"], t["frame"]
    moves = [
        (obj.at[pl.ds(H, H)], down_hbm),
        (psf.at[count - 1], right_hbm.at[pl.ds(0, S)]),
        (obj.at[pl.ds(0, H), last], right_hbm.at[pl.ds(S, H)]),
        (frame.at[:, last], right_hbm.at[pl.ds(S + H, S)]),
        (psf.at[count - 1], diagonal_hbm.at[pl.ds(0, S)]),
        (obj.at[pl.ds(H, H), last], diagonal_hbm.at[pl.ds(S, H)]),
        (frame.at[:, last], frame_hbm),
    ]
    moves = [pltpu.make_async_copy(*move, sems.at[total + 1 + n]) for n, move in enumerate(moves)]
    for copy in moves:
        copy.start()
    lanes = dot(wide_parts(jnp.concatenate([psf[j] for j in range(count)], axis=0)), t["near_right"][...])
    for j in range(count):
        store_parts(parts, at(j), stacked(lanes[at(j)]))
    spec_ref[...] = dot(t["near_left"][...], parts[...])
    out = pltpu.make_async_copy(spec_ref, spec_hbm, sems.at[total])
    out.start()
    total_ref[...] = jnp.full(total_ref.shape, jnp.sum(t["frame"][...]), F32)
    for name in names:
        t[name]
    for copy in moves + [out]:
        copy.wait()


def above_kernel(psf_hbm, right, left, spec_hbm, spec_ref, psf, sems, parts):
    t = Copies(("psf",), (psf_hbm,), (psf,), sems)
    count = psf.shape[0]
    lanes = dot(wide_parts(jnp.concatenate([t["psf"][j] for j in range(count)], axis=0)), right[...])
    for j in range(count):
        store_parts(parts, at(j), stacked(lanes[at(j)]))
    spec_ref[...] = dot(left[...], parts[...])
    out = pltpu.make_async_copy(spec_ref, spec_hbm, sems.at[1])
    out.start()
    out.wait()


def alternating():
    k = lax.broadcasted_iota(jnp.int32, (L, S), 0)
    return jnp.where(k % 2 == 0, 1.0, -1.0).astype(F32)


def model_kernel(names, ready, *refs):
    total = len(names)
    hbm, refs = refs[:total], refs[total:]
    t, refs = dict(zip(ready, refs)), refs[len(ready) :]
    more_hbm, mid_top, mid_bottom, first_ref, last_ref, flux_ref = refs[:6]
    buffers, sems, more_ref, x_ref, x_parts, y_parts = refs[6 : 6 + total], *refs[6 + total :]
    got = Copies(names, picked(names, hbm), buffers, sems)
    out = pltpu.make_async_copy(more_ref, more_hbm, sems.at[total])
    row_edge, column_edge = edges()
    alpha, beta = 1.0 - row_edge.astype(F32), 1.0 - column_edge.astype(F32)
    right_ref, diagonal_ref, above_ref, own_ref = [got[n] for n in ("right", "diagonal", "above", "own")]
    count = own_ref.shape[1] // S
    windows = [t["windows"][w, :1] for w in range(2)]
    plain = [t["plain"][w, :1] for w in range(2)]
    for q in range(count):
        lo = q * S
        if q == 0:
            left = jnp.concatenate([diagonal_ref[S:], right_ref[S:]], axis=0)[:, H:]
        else:
            left = jnp.concatenate([above_ref[:, lo - S : lo], own_ref[:H, lo - S : lo]], axis=0)[:, H:]
        here = jnp.concatenate([above_ref[:, lo : lo + S], own_ref[:H, lo : lo + S]], axis=0)[:, :H]
        x = jnp.concatenate([left, here], axis=1)
        for w in range(2):
            x_ref[at(2 * q + w)] = x * (windows if q == 0 else plain)[w]
    psfs = [diagonal_ref[:S], right_ref[:S]]
    lanes = dot(wide_parts(jnp.concatenate([x_ref[...]] + psfs, axis=0)), t["near_right"][...])
    for n in range(2 * count + 2):
        store_parts(x_parts, at(n), stacked(lanes[at(n)]))
    more_ref[...] = dot(t["near_left"][...], x_parts[:, 2 * count * S :])
    out.start()
    spec_ref, spec_above = t["spec"], t["spec_above"]
    obj_left = t["obj_left"]
    sign = alternating()
    for pair in range(count // 2):
        x_specs = dot(obj_left[...], x_parts[:, pair * 4 * S : (pair + 1) * 4 * S])
        for q in (2 * pair, 2 * pair + 1):
            y = {}
            for r in range(2):
                for w in range(2):
                    lanes = at(2 * (q % 2) + w)
                    x_re = x_specs[at(2 * r, L), lanes]
                    x_im = x_specs[at(2 * r + 1, L), lanes]
                    j = q - w
                    own = (spec_ref, spec_above)[r]
                    source, lanes = (own, at(j)) if j >= 0 else (more_ref, at(1 - r))
                    h_re, h_im = source[:L, lanes], source[L:, lanes]
                    y[r, w] = (x_re * h_re - x_im * h_im, x_re * h_im + x_im * h_re)
            if q == 0:
                variants = [
                    [tuple(y[r, 1][c] + beta * y[r, 0][c] for c in range(2)) for r in range(2)],
                    [tuple(y[r, 0][c] + beta * y[r, 1][c] for c in range(2)) for r in range(2)],
                ]
            else:
                variants = [[tuple(y[r, 0][c] + y[r, 1][c] for c in range(2)) for r in range(2)]]
            for v, (upper, lower) in enumerate(variants):
                slot = v if q == 0 else q + 1
                top = [lower[c] + alpha * upper[c] for c in range(2)]
                bottom = [upper[c] + alpha * lower[c] for c in range(2)]
                store_parts(y_parts, at(slot), jnp.concatenate(top, axis=0))
                turned = jnp.concatenate([-sign * bottom[1], sign * bottom[0]], axis=0)
                store_parts(y_parts, at(count + 1 + slot), turned)
    rows = dot(t["near_inverse"][...], y_parts[...])
    blocks = jnp.concatenate([side_by_side(rows[:, at(n)]) for n in range(2 * count + 2)], axis=0)
    image = dot(wide_parts(blocks), t["out_right"][...])
    flux = 0.0
    for half in range(2):
        base = half * (count + 1)
        lefts = [image[at(base), :S]] + [image[at(base + q + 1), :S] for q in range(1, count)]
        rights = [image[at(base + q + 1), S:] for q in range(count)]
        first_ref[at(half)] = lefts[0]
        last_ref[at(half)] = rights[-1]
        middle = mid_bottom if half else mid_top
        together = lefts[0] + rights[-1]
        for q in range(1, count):
            block = lefts[q] + rights[q - 1]
            middle[:, at(q - 1)] = block
            together = together + block
        flux = flux + jnp.sum(together)
    lane = lax.broadcasted_iota(jnp.int32, flux_ref.shape, 1)
    flux_ref[...] = jnp.where(lane < H, flux, t["total"][...])
    out.wait()


def join_kernel(names, ready, *refs):
    total = len(names)
    hbm, refs = refs[:total], refs[total:]
    here, refs = dict(zip(ready, refs)), refs[len(ready) :]
    fluxes = [here[n] for n in ready if n not in ("mid_top", "mid_bottom", "first", "last")]
    top_hbm, bottom_hbm, totals_ref = refs[:3]
    buffers, sems, top_ref, bottom_ref = refs[3 : 3 + total], refs[3 + total], refs[4 + total], refs[5 + total]
    t = Copies(names, hbm, buffers, sems)
    outs = []
    for half, out, place in ((0, top_ref, top_hbm), (1, bottom_ref, bottom_hbm)):
        mid = here["mid_bottom" if half else "mid_top"]
        width = mid.shape[1]
        out[:, S : S + width] = mid[...]
        out[:, :S] = here["first"][at(half)] + t["from_left"][at(half)]
        out[:, S + width :] = here["last"][at(half)] + t["from_right"][at(half)]
        outs.append(pltpu.make_async_copy(out, place, sems.at[total + half]))
        outs[-1].start()
    flux = sum([f[...] for f in fluxes[1:]], fluxes[0][...])
    totals_ref[...] = jnp.broadcast_to(flux[None], totals_ref.shape)
    for copy in outs:
        copy.wait()


def gradient_kernel(names, *refs):
    total = len(names)
    hbm, flux_ref, refs = refs[:total], refs[total], refs[total + 1 :]
    residual_hbm, top_hbm, bottom_hbm, first_hbm, rest_hbm = refs[:5]
    buffers, sems, (residual_ref, out_top, out_bottom) = refs[5 : 5 + total], refs[5 + total], refs[6 + total : 9 + total]
    r_ref, r_parts, g_parts = refs[9 + total :]
    t = Copies(names, picked(names, hbm), buffers, sems)
    sent = [
        pltpu.make_async_copy(source, out, sems.at[total + n])
        for n, (source, out) in enumerate(
            (
                (residual_ref, residual_hbm),
                (out_bottom, bottom_hbm),
                (out_top, top_hbm),
                (out_top.at[:, pl.ds(0, S)], first_hbm),
                (out_top.at[:, pl.ds(S, rest_hbm.shape[1])], rest_hbm),
            )
        )
    ]
    row_edge, column_edge = edges()
    alpha, beta = 1.0 - row_edge.astype(F32), 1.0 - column_edge.astype(F32)
    width = residual_ref.shape[1]
    count = width // S
    sums = jnp.sum(flux_ref[...], axis=0)
    gain = sums[0, H] / sums[0, 0]
    r_ref[:S] = gain * (t["top"][...] + t["above"][...])
    r_ref[S:] = gain * (t["bottom"][...] + t["below"][...])
    r_ref[:S, S:] -= t["obs_above"][...]
    r_ref[S:, S:] -= t["obs"][...]
    r_ref[:S, :S] -= t["obs_diagonal"][...]
    r_ref[S:, :S] -= t["obs_left"][...]
    residual_ref[...] = r_ref[S:, S:]
    sent[0].start()
    near, far = r_ref[:, :S], r_ref[:, S : 2 * S]
    blocks = [
        jnp.concatenate([beta * near, far], axis=1),
        jnp.concatenate([near, beta * far], axis=1),
    ] + [r_ref[:, q * S : (q + 2) * S] for q in range(1, count)]
    lanes = dot(wide_parts(jnp.concatenate(blocks, axis=0)), t["res_right"][...])
    for n in range(count + 1):
        value = lanes[at(n, L)]
        store_parts(r_parts, at(n), stacked(value[:S]))
        store_parts(r_parts, at(count + 1 + n), stacked(value[S:]))
    spectra = dot(t["near_left"][...], r_parts[...])
    sign = alternating()
    spec_ref, spec_above, more_ref = t["spec"], t["spec_above"], t["more"]
    seen = []
    for n in range(count + 1):
        top = [spectra[at(c, L), at(n)] for c in range(2)]
        raw = [spectra[at(c, L), at(count + 1 + n)] for c in range(2)]
        bottom = [sign * raw[1], -sign * raw[0]]
        seen.append(
            [
                [bottom[c] + alpha * top[c] for c in range(2)],
                [top[c] + alpha * bottom[c] for c in range(2)],
            ]
        )
    grad_left = t["grad_left"]
    outs = []
    for pair in range(count // 2):
        for q in (2 * pair, 2 * pair + 1):
            for w in range(2):
                slot = w if q == 0 else q + 1
                j = q - w
                for r in range(2):
                    own = (spec_ref, spec_above)[r]
                    source, lanes = (own, at(j)) if j >= 0 else (more_ref, at(1 - r))
                    h_re, h_im = source[:L, lanes], source[L:, lanes]
                    r_re, r_im = seen[slot][r]
                    for c, part in enumerate((r_re * h_re + r_im * h_im, r_im * h_re - r_re * h_im)):
                        hi, lo = split(part)
                        place = (2 * r + c) * L
                        for n, value in enumerate((hi, lo, hi)):
                            g_parts[4 * n * L + place : 4 * n * L + place + L, at(2 * q + w)] = value
        g = dot(grad_left[...], g_parts[:, pair * 4 * S : (pair + 1) * 4 * S])
        outs += [side_by_side(g[:, at(n)]) for n in range(4)]
    out = dot(wide_parts(jnp.concatenate(outs, axis=0)), t["grad_right"][...])
    for q in range(count):
        windows = t["windows"] if q == 0 else t["plain"]
        grad = gain * (out[at(2 * q)] * windows[0, :1] + out[at(2 * q + 1)] * windows[1, :1])
        out_top[:, at(q)] = grad[:H]
        out_bottom[:, at(q)] = grad[H:]
    for copy in sent[1:]:
        copy.start()
    for copy in sent:
        copy.wait()


def f32(*shape):
    return jax.ShapeDtypeStruct(shape, F32)


def call(kernel, named, ready, outs, scratch, limit, flops, loose=()):
    hbm, vmem = pl.BlockSpec(memory_space=pltpu.HBM), pl.BlockSpec(memory_space=pltpu.VMEM)
    held = [x if n in loose else pltpu.with_memory_space_constraint(x, pltpu.HBM) for n, x in named.items()]
    size = sum(math.prod(x.shape) * x.dtype.itemsize for x in named.values())
    return pl.pallas_call(
        kernel,
        out_shape=[place(o.shape, o.dtype) for place, o in outs],
        in_specs=[hbm] * len(named) + [vmem] * len(ready),
        out_specs=[hbm if place is pltpu.HBM else vmem for place, _ in outs],
        scratch_shapes=scratch,
        compiler_params=pltpu.CompilerParams(vmem_limit_bytes=limit * 2**20),
        cost_estimate=pl.CostEstimate(flops=flops, bytes_accessed=size, transcendentals=0),
    )(*held, *ready.values())


def like(arrays):
    shapes = {"right": (S + H, S), "obs_left": (S, S)}
    shapes |= {n: arrays[n].shape[1:] for n in ("windows", "obj_left", "grad_left") if n in arrays}
    return [pltpu.VMEM(shapes.get(n, x.shape), x.dtype) for n, x in arrays.items()]


def ring(value, axes, moves):
    sizes = [lax.axis_size(a) for a in axes]
    pairs = []
    for source in np.ndindex(*sizes):
        target = [(p + m) % n for p, m, n in zip(source, moves, sizes)]
        pairs.append((int(np.ravel_multi_index(source, sizes)), int(np.ravel_multi_index(target, sizes))))
    return lax.ppermute(value, axes, pairs)


def mirrored(value, axis, bits):
    count = lax.axis_size(axis)
    return lax.ppermute(value, axis, [(s, s ^ bits) for s in range(count)])


def runs():
    count = lax.axis_size("sy")
    return 4 if count % 4 == 0 else count


def exchanged(value):
    count_y, count_x, run = lax.axis_size("sy"), lax.axis_size("sx"), runs()
    index = np.arange(count_y * count_x).reshape(count_y // run, run, count_x)
    groups = index.transpose(1, 0, 2).reshape(run, -1).tolist()
    return lax.all_to_all(value, ("sy", "sx"), 0, 0, axis_index_groups=groups)


def down(value):
    return ring(value, ("sy",), (1,))


def up(value):
    return ring(value, ("sy",), (-1,))


def per_device(object_field, frames_data, patch_psfs):
    rows, width = object_field.shape
    count = width // S
    psfs = patch_psfs.reshape(count, S, S)
    observed = frames_data[0]
    t = {name: jnp.asarray(value) for name, value in tables().items()}
    psf_above = down(psfs)
    kept = {k: t[k] for k in ("near_right", "near_left", "windows", "obj_left", "near_inverse", "out_right")}
    named = {"psf": psfs, "object": object_field, "frame": observed} | kept
    pack_down, pack_right, pack_diagonal, obs_last, spec, spec_here, total, *got = call(
        functools.partial(psf_kernel, tuple(named)),
        named,
        {},
        [(pltpu.HBM, f32(H, width)), (pltpu.HBM, f32(2 * S + H, S)), (pltpu.HBM, f32(S + H, S)),
         (pltpu.HBM, f32(S, S)),
         (pltpu.HBM, f32(2 * L, width)), (pltpu.VMEM, f32(2 * L, width)), (pltpu.VMEM, f32(8, S))]
        + [(pltpu.VMEM, x) for x in like(kept)],
        [pltpu.VMEM(psfs.shape, F32), pltpu.VMEM(object_field.shape, F32), pltpu.VMEM(observed.shape, F32),
         pltpu.SemaphoreType.DMA((len(named) + 8,)), pltpu.VMEM((6 * S, width), BF16)],
        16,
        6 * 84 * 10**6,
    )
    obj_above = down(pack_down)
    got_diagonal = ring(pack_diagonal, ("sy", "sx"), (1, 1))
    got_right = ring(pack_right, ("sx",), (1,))
    obs_above = down(observed)
    obs_diagonal = ring(obs_last, ("sy", "sx"), (1, 1))
    ready = dict(zip(kept, got))
    spec_above, spec_above_here = call(
        above_kernel,
        {"psf": psf_above},
        {k: ready[k] for k in ("near_right", "near_left")},
        [(pltpu.HBM, f32(2 * L, width)), (pltpu.VMEM, f32(2 * L, width))],
        [pltpu.VMEM(psfs.shape, F32), pltpu.SemaphoreType.DMA((2,)), pltpu.VMEM((6 * S, width), BF16)],
        16,
        6 * 84 * 10**6,
        ("psf",),
    )
    ready |= {"spec_above": spec_above_here, "spec": spec_here, "total": total, "plain": t["windows"][0]}
    named = {"right": got_right, "diagonal": got_diagonal, "above": obj_above, "own": object_field}
    outs = [f32(2 * L, 2 * S), f32(S, width - S), f32(S, width - S), f32(L, S), f32(L, S)]
    more, mid_top, mid_bottom, first, last, flux = call(
        functools.partial(model_kernel, tuple(named), tuple(ready)),
        named,
        ready,
        [(pltpu.HBM, outs[0])] + [(pltpu.VMEM, o) for o in outs[1:] + [f32(8, S)]],
        like(named) + [pltpu.SemaphoreType.DMA((len(named) + 1,)), pltpu.VMEM(outs[0].shape, F32)]
        + [pltpu.VMEM((2 * width, S), F32), pltpu.VMEM((6 * S, 2 * width + 2 * S), BF16),
           pltpu.VMEM((6 * L, 2 * width + 2 * S), BF16)],
        36,
        6 * 600 * 10**6,
        ("right", "diagonal", "above"),
    )
    mid_top, mid_bottom, first, last, flux, obs_above, obs_diagonal = lax.optimization_barrier(
        (mid_top, mid_bottom, first, last, flux, obs_above, obs_diagonal)
    )
    from_right = ring(first, ("sx",), (-1,))
    from_left = ring(last, ("sx",), (1,))
    fluxes = [flux] + [mirrored(flux, "sy", k) for k in range(1, runs())]
    named = {"from_left": from_left, "from_right": from_right}
    ready = {"mid_top": mid_top, "mid_bottom": mid_bottom, "first": first, "last": last} | dict(enumerate(fluxes))
    outs = [f32(S, width + S)] * 2
    top, bottom, flux = call(
        functools.partial(join_kernel, tuple(named), tuple(ready)),
        named,
        ready,
        [(pltpu.HBM, o) for o in outs]
        + [(pltpu.VMEM, f32(lax.axis_size("sy") // runs() * lax.axis_size("sx"), 8, S))],
        like(named) + [pltpu.SemaphoreType.DMA((len(named) + len(outs),))] + [pltpu.VMEM(o.shape, F32) for o in outs],
        16,
        10**6,
        ("from_left", "from_right"),
    )
    below = up(top)
    above = down(bottom)
    flux = exchanged(flux)

    named = {"top": top, "above": above, "bottom": bottom, "below": below,
             "obs_above": obs_above, "obs": observed,
             "obs_diagonal": obs_diagonal, "obs_left": got_right,
             "res_right": t["res_right"], "near_left": t["near_left"], "spec": spec, "spec_above": spec_above, "more": more,
             "grad_left": t["grad_left"], "grad_right": t["grad_right"],
             "windows": t["windows"], "plain": t["windows"][0]}
    outs = [f32(S, width), f32(H, width), f32(H, width), f32(H, S), f32(H, width - S)]
    residual, g_top, g_bottom, g_first, g_rest = call(
        functools.partial(gradient_kernel, tuple(named)),
        named,
        {"flux": flux},
        [(pltpu.HBM, o) for o in outs],
        like(named) + [pltpu.SemaphoreType.DMA((len(named) + len(outs),))]
        + [pltpu.VMEM(o.shape, F32) for o in outs[:3]]
        + [pltpu.VMEM((L, width + S), F32), pltpu.VMEM((6 * S, 2 * width + 2 * S), BF16),
           pltpu.VMEM((12 * L, 2 * width), BF16)],
        44,
        6 * 500 * 10**6,
        ("above", "below", "obs_above", "obs_diagonal", "obs_left"),
    )
    bottom_other = mirrored(g_bottom, "fr", 1)
    top_same = up(g_top)
    first_other = ring(g_first, ("sy", "fr"), (-1, 1))
    rest_other = ring(g_rest, ("sy", "fr"), (-1, 1))
    side = jnp.concatenate([g_bottom[:, :H] + bottom_other[:, :H], top_same[:, :H] + first_other[:, :H]], axis=0)
    side = ring(side, ("sx",), (-1,))
    upper = g_bottom[:, H:] + bottom_other[:, H:]
    lower_first = top_same[:, H:S] + first_other[:, H:]
    upper, lower_first, top_same, rest_other, side = lax.optimization_barrier(
        (upper, lower_first, top_same, rest_other, side)
    )
    lower = jnp.concatenate([lower_first, top_same[:, S:] + rest_other], axis=1)
    gradient = jnp.concatenate([jnp.concatenate([upper, lower], axis=0), side], axis=1)
    return gradient, residual[None]


def solution(mesh):
    placed = (P("sy", "sx"), P("fr", "sy", "sx"), P("fr", "sy", "sx", None, None))
    return jax.shard_map(
        per_device,
        mesh=mesh,
        in_specs=placed,
        out_specs=(P("sy", "sx"), P("fr", "sy", "sx")),
        check_vma=False,
    )
```

```python
import functools
import math

import jax
import jax.numpy as jnp
import numpy as np
from jax import lax
from jax.experimental import pallas as pl
from jax.experimental.pallas import tpu as pltpu
from jax.sharding import PartitionSpec as P

S = 128
L = 256
H = 64
F32 = jnp.float32
BF16 = jnp.bfloat16


def half_windows():
    n = np.arange(L, dtype=np.float64)
    s = np.sin(np.pi * (n + 0.5) / L) ** 2
    return s[:S], s[S:]


def phases(freqs, positions):
    product = (2 * np.arange(freqs)[:, None] + 1) * positions[None, :] % (2 * L)
    angle = product.astype(np.float64) * (math.pi / L)
    return np.cos(angle), np.sin(angle)


def forward_left(positions):
    c, s = phases(L, positions)
    return np.block([[c, s], [-s, c]])


def inverse_left(positions):
    c, s = phases(L, positions)
    return np.block([[c.T, -s.T], [s.T, c.T]]) / L


def forward_right(positions):
    c, s = phases(S, positions)
    return np.concatenate([c.T, -s.T], axis=1)


def inverse_right(positions):
    c, s = phases(S, positions)
    return np.concatenate([c, -s], axis=0) * (2.0 / L)


def bf16_parts(table):
    hi = table.astype(np.float32).astype(BF16)
    lo = (table - hi.astype(np.float64)).astype(np.float32).astype(BF16)
    return hi, lo


def left_table(table):
    hi, lo = bf16_parts(table)
    return np.concatenate([hi, hi, lo], axis=-1)


def right_table(table):
    hi, lo = bf16_parts(table)
    return np.concatenate([hi, hi, lo], axis=-2)


@functools.lru_cache(maxsize=1)
def tables():
    near = np.arange(S)
    up, down = half_windows()
    pairs = ((up, down), (np.where(near < H, 0.0, up), np.where(near < H, down, 0.0)))
    base, back = forward_left(near), inverse_left(near)
    t = {}
    t["near_right"] = right_table(forward_right(near))
    t["near_left"] = left_table(base)
    t["obj_left"] = np.stack(
        [left_table(np.concatenate([base * np.tile(w, 2)[None, :] for w in pair], axis=0)) for pair in pairs]
    )
    t["near_inverse"] = left_table(back)
    t["out_right"] = right_table(inverse_right(np.arange(L)))
    t["res_right"] = right_table(forward_right(np.arange(L)))
    t["grad_left"] = np.stack(
        [left_table(np.concatenate([np.tile(w, 2)[:, None] * back for w in pair], axis=1)) for pair in pairs]
    )
    t["grad_right"] = right_table(inverse_right(near))
    t["windows"] = np.stack([np.stack([np.tile(w, (8, 1)) for w in pair]) for pair in pairs]).astype(np.float32)
    return t


def split(value):
    hi = value.astype(BF16)
    return hi, (value - hi.astype(F32)).astype(BF16)


def wide_parts(value):
    hi, lo = split(value)
    return jnp.concatenate([hi, lo, hi], axis=1)


def store_parts(ref, lanes, value):
    hi, lo = split(value)
    depth = value.shape[0]
    ref[:depth, lanes] = hi
    ref[depth : 2 * depth, lanes] = lo
    ref[2 * depth :, lanes] = hi


def dot(a, b):
    return jnp.dot(a, b, preferred_element_type=F32)


def stacked(value):
    half = value.shape[1] // 2
    return jnp.concatenate([value[:, :half], value[:, half:]], axis=0)


def side_by_side(value):
    half = value.shape[0] // 2
    return jnp.concatenate([value[:half], value[half:]], axis=1)


def at(n, size=S):
    return slice(n * size, (n + 1) * size)


class Copies:
    def __init__(self, names, sources, refs, semaphores):
        self.buffers = dict(zip(names, refs))
        self.copies = {
            name: pltpu.make_async_copy(source, buffer, semaphores.at[n])
            for n, (name, source, buffer) in enumerate(zip(names, sources, refs))
        }
        self.waited = set()
        for name in names:
            self.copies[name].start()

    def __getitem__(self, name):
        if name not in self.waited:
            self.waited.add(name)
            self.copies[name].wait()
        return self.buffers[name]


def edges():
    return [(lax.axis_index(axis) == 0).astype(jnp.int32) for axis in ("sy", "sx")]


def picked(names, hbm):
    rows, columns = edges()
    edge = {"obj_left": rows, "grad_left": rows, "windows": columns}
    part = {"right": pl.ds(0, S + H), "obs_left": pl.ds(S + H, S)}
    return [h.at[edge[n]] if n in edge else h.at[part[n]] if n in part else h for n, h in zip(names, hbm)]


def psf_kernel(names, *refs):
    total = len(names)
    hbm, refs = refs[:total], refs[total:]
    down_ref, right_ref, diagonal_ref, frame_ref, spec_hbm, spec_ref, total_ref, *buffers = refs[:-5]
    psf, obj, frame, sems, parts = refs[-5:]
    t = Copies(names, picked(names, hbm), (psf, obj, frame) + tuple(buffers), sems)
    count, last = psf.shape[0], pl.ds(obj.shape[1] - S, S)
    psf, obj, frame = t["psf"], t["object"], t["frame"]
    down_ref[...] = obj[H:]
    right_ref[:S] = psf[count - 1]
    right_ref[S : S + H] = obj[:H, last]
    right_ref[S + H :] = frame[:, last]
    diagonal_ref[:S] = psf[count - 1]
    diagonal_ref[S:] = obj[H:, last]
    frame_ref[...] = frame[:, last]
    lanes = dot(wide_parts(jnp.concatenate([psf[j] for j in range(count)], axis=0)), t["near_right"][...])
    for j in range(count):
        store_parts(parts, at(j), stacked(lanes[at(j)]))
    spec_ref[...] = dot(t["near_left"][...], parts[...])
    out = pltpu.make_async_copy(spec_ref, spec_hbm, sems.at[total])
    out.start()
    total_ref[...] = jnp.full(total_ref.shape, jnp.sum(t["frame"][...]), F32)
    for name in names:
        t[name]
    out.wait()


def above_kernel(psf_hbm, right, left, spec_hbm, spec_ref, psf, sems, parts):
    t = Copies(("psf",), (psf_hbm,), (psf,), sems)
    count = psf.shape[0]
    lanes = dot(wide_parts(jnp.concatenate([t["psf"][j] for j in range(count)], axis=0)), right[...])
    for j in range(count):
        store_parts(parts, at(j), stacked(lanes[at(j)]))
    spec_ref[...] = dot(left[...], parts[...])
    out = pltpu.make_async_copy(spec_ref, spec_hbm, sems.at[1])
    out.start()
    out.wait()


def alternating():
    k = lax.broadcasted_iota(jnp.int32, (L, S), 0)
    return jnp.where(k % 2 == 0, 1.0, -1.0).astype(F32)


def model_kernel(names, ready, *refs):
    total = len(names)
    hbm, refs = refs[:total], refs[total:]
    t, refs = dict(zip(ready, refs)), refs[len(ready) :]
    more_hbm, mid_top, mid_bottom, first_ref, last_ref, flux_ref = refs[:6]
    buffers, sems, more_ref, x_ref, x_parts, y_parts = refs[6 : 6 + total], *refs[6 + total :]
    got = Copies(names, picked(names, hbm), buffers, sems)
    out = pltpu.make_async_copy(more_ref, more_hbm, sems.at[total])
    row_edge, column_edge = edges()
    alpha, beta = 1.0 - row_edge.astype(F32), 1.0 - column_edge.astype(F32)
    right_ref, diagonal_ref, above_ref, own_ref = [got[n] for n in ("right", "diagonal", "above", "own")]
    count = own_ref.shape[1] // S
    windows = [t["windows"][w, :1] for w in range(2)]
    plain = [t["plain"][w, :1] for w in range(2)]
    for q in range(count):
        lo = q * S
        if q == 0:
            left = jnp.concatenate([diagonal_ref[S:], right_ref[S:]], axis=0)[:, H:]
        else:
            left = jnp.concatenate([above_ref[:, lo - S : lo], own_ref[:H, lo - S : lo]], axis=0)[:, H:]
        here = jnp.concatenate([above_ref[:, lo : lo + S], own_ref[:H, lo : lo + S]], axis=0)[:, :H]
        x = jnp.concatenate([left, here], axis=1)
        for w in range(2):
            x_ref[at(2 * q + w)] = x * (windows if q == 0 else plain)[w]
    psfs = [diagonal_ref[:S], right_ref[:S]]
    lanes = dot(wide_parts(jnp.concatenate([x_ref[...]] + psfs, axis=0)), t["near_right"][...])
    for n in range(2 * count + 2):
        store_parts(x_parts, at(n), stacked(lanes[at(n)]))
    more_ref[...] = dot(t["near_left"][...], x_parts[:, 2 * count * S :])
    out.start()
    spec_ref, spec_above = t["spec"], t["spec_above"]
    obj_left = t["obj_left"]
    sign = alternating()
    for pair in range(count // 2):
        x_specs = dot(obj_left[...], x_parts[:, pair * 4 * S : (pair + 1) * 4 * S])
        for q in (2 * pair, 2 * pair + 1):
            y = {}
            for r in range(2):
                for w in range(2):
                    lanes = at(2 * (q % 2) + w)
                    x_re = x_specs[at(2 * r, L), lanes]
                    x_im = x_specs[at(2 * r + 1, L), lanes]
                    j = q - w
                    own = (spec_ref, spec_above)[r]
                    source, lanes = (own, at(j)) if j >= 0 else (more_ref, at(1 - r))
                    h_re, h_im = source[:L, lanes], source[L:, lanes]
                    y[r, w] = (x_re * h_re - x_im * h_im, x_re * h_im + x_im * h_re)
            if q == 0:
                variants = [
                    [tuple(y[r, 1][c] + beta * y[r, 0][c] for c in range(2)) for r in range(2)],
                    [tuple(y[r, 0][c] + beta * y[r, 1][c] for c in range(2)) for r in range(2)],
                ]
            else:
                variants = [[tuple(y[r, 0][c] + y[r, 1][c] for c in range(2)) for r in range(2)]]
            for v, (upper, lower) in enumerate(variants):
                slot = v if q == 0 else q + 1
                top = [lower[c] + alpha * upper[c] for c in range(2)]
                bottom = [upper[c] + alpha * lower[c] for c in range(2)]
                store_parts(y_parts, at(slot), jnp.concatenate(top, axis=0))
                turned = jnp.concatenate([-sign * bottom[1], sign * bottom[0]], axis=0)
                store_parts(y_parts, at(count + 1 + slot), turned)
    rows = dot(t["near_inverse"][...], y_parts[...])
    blocks = jnp.concatenate([side_by_side(rows[:, at(n)]) for n in range(2 * count + 2)], axis=0)
    image = dot(wide_parts(blocks), t["out_right"][...])
    flux = 0.0
    for half in range(2):
        base = half * (count + 1)
        lefts = [image[at(base), :S]] + [image[at(base + q + 1), :S] for q in range(1, count)]
        rights = [image[at(base + q + 1), S:] for q in range(count)]
        first_ref[at(half)] = lefts[0]
        last_ref[at(half)] = rights[-1]
        middle = mid_bottom if half else mid_top
        together = lefts[0] + rights[-1]
        for q in range(1, count):
            block = lefts[q] + rights[q - 1]
            middle[:, at(q - 1)] = block
            together = together + block
        flux = flux + jnp.sum(together)
    lane = lax.broadcasted_iota(jnp.int32, flux_ref.shape, 1)
    flux_ref[...] = jnp.where(lane < H, flux, t["total"][...])
    out.wait()


def join_kernel(names, ready, *refs):
    total = len(names)
    hbm, refs = refs[:total], refs[total:]
    here, refs = dict(zip(ready, refs)), refs[len(ready) :]
    fluxes = [here[n] for n in ready if n not in ("mid_top", "mid_bottom", "first", "last")]
    top_hbm, bottom_hbm, totals_ref = refs[:3]
    buffers, sems, top_ref, bottom_ref = refs[3 : 3 + total], refs[3 + total], refs[4 + total], refs[5 + total]
    t = Copies(names, hbm, buffers, sems)
    outs = []
    for half, out, place in ((0, top_ref, top_hbm), (1, bottom_ref, bottom_hbm)):
        mid = here["mid_bottom" if half else "mid_top"]
        width = mid.shape[1]
        out[:, S : S + width] = mid[...]
        out[:, :S] = here["first"][at(half)] + t["from_left"][at(half)]
        out[:, S + width :] = here["last"][at(half)] + t["from_right"][at(half)]
        outs.append(pltpu.make_async_copy(out, place, sems.at[total + half]))
        outs[-1].start()
    flux = sum([f[...] for f in fluxes[1:]], fluxes[0][...])
    totals_ref[...] = jnp.broadcast_to(flux[None], totals_ref.shape)
    for copy in outs:
        copy.wait()


def gradient_kernel(names, *refs):
    total = len(names)
    hbm, flux_ref, refs = refs[:total], refs[total], refs[total + 1 :]
    residual_hbm, out_top, out_bottom, first_ref, rest_ref = refs[:5]
    buffers, sems, residual_ref, r_ref, r_parts, g_parts = refs[5 : 5 + total], *refs[5 + total :]
    t = Copies(names, picked(names, hbm), buffers, sems)
    sent = pltpu.make_async_copy(residual_ref, residual_hbm, sems.at[total])
    row_edge, column_edge = edges()
    alpha, beta = 1.0 - row_edge.astype(F32), 1.0 - column_edge.astype(F32)
    width = residual_ref.shape[1]
    count = width // S
    sums = jnp.sum(flux_ref[...], axis=0)
    gain = sums[0, H] / sums[0, 0]
    r_ref[:S] = gain * (t["top"][...] + t["above"][...])
    r_ref[S:] = gain * (t["bottom"][...] + t["below"][...])
    r_ref[:S, S:] -= t["obs_above"][...]
    r_ref[S:, S:] -= t["obs"][...]
    r_ref[:S, :S] -= t["obs_diagonal"][...]
    r_ref[S:, :S] -= t["obs_left"][...]
    residual_ref[...] = r_ref[S:, S:]
    sent.start()
    near, far = r_ref[:, :S], r_ref[:, S : 2 * S]
    blocks = [
        jnp.concatenate([beta * near, far], axis=1),
        jnp.concatenate([near, beta * far], axis=1),
    ] + [r_ref[:, q * S : (q + 2) * S] for q in range(1, count)]
    lanes = dot(wide_parts(jnp.concatenate(blocks, axis=0)), t["res_right"][...])
    for n in range(count + 1):
        value = lanes[at(n, L)]
        store_parts(r_parts, at(n), stacked(value[:S]))
        store_parts(r_parts, at(count + 1 + n), stacked(value[S:]))
    spectra = dot(t["near_left"][...], r_parts[...])
    sign = alternating()
    spec_ref, spec_above, more_ref = t["spec"], t["spec_above"], t["more"]
    seen = []
    for n in range(count + 1):
        top = [spectra[at(c, L), at(n)] for c in range(2)]
        raw = [spectra[at(c, L), at(count + 1 + n)] for c in range(2)]
        bottom = [sign * raw[1], -sign * raw[0]]
        seen.append(
            [
                [bottom[c] + alpha * top[c] for c in range(2)],
                [top[c] + alpha * bottom[c] for c in range(2)],
            ]
        )
    grad_left = t["grad_left"]
    outs = []
    for pair in range(count // 2):
        for q in (2 * pair, 2 * pair + 1):
            for w in range(2):
                slot = w if q == 0 else q + 1
                j = q - w
                for r in range(2):
                    own = (spec_ref, spec_above)[r]
                    source, lanes = (own, at(j)) if j >= 0 else (more_ref, at(1 - r))
                    h_re, h_im = source[:L, lanes], source[L:, lanes]
                    r_re, r_im = seen[slot][r]
                    for c, part in enumerate((r_re * h_re + r_im * h_im, r_im * h_re - r_re * h_im)):
                        hi, lo = split(part)
                        place = (2 * r + c) * L
                        for n, value in enumerate((hi, lo, hi)):
                            g_parts[4 * n * L + place : 4 * n * L + place + L, at(2 * q + w)] = value
        g = dot(grad_left[...], g_parts[:, pair * 4 * S : (pair + 1) * 4 * S])
        outs += [side_by_side(g[:, at(n)]) for n in range(4)]
    out = dot(wide_parts(jnp.concatenate(outs, axis=0)), t["grad_right"][...])
    for q in range(count):
        windows = t["windows"] if q == 0 else t["plain"]
        grad = gain * (out[at(2 * q)] * windows[0, :1] + out[at(2 * q + 1)] * windows[1, :1])
        out_top[:, at(q)] = grad[:H]
        out_bottom[:, at(q)] = grad[H:]
    first_ref[...] = out_top[:, :S]
    rest_ref[...] = out_top[:, S:]
    sent.wait()


def f32(*shape):
    return jax.ShapeDtypeStruct(shape, F32)


def call(kernel, named, ready, outs, scratch, limit, flops, loose=()):
    hbm, vmem = pl.BlockSpec(memory_space=pltpu.HBM), pl.BlockSpec(memory_space=pltpu.VMEM)
    held = [x if n in loose else pltpu.with_memory_space_constraint(x, pltpu.HBM) for n, x in named.items()]
    size = sum(math.prod(x.shape) * x.dtype.itemsize for x in named.values())
    return pl.pallas_call(
        kernel,
        out_shape=[place(o.shape, o.dtype) for place, o in outs],
        in_specs=[hbm] * len(named) + [vmem] * len(ready),
        out_specs=[hbm if place is pltpu.HBM else vmem for place, _ in outs],
        scratch_shapes=scratch,
        compiler_params=pltpu.CompilerParams(vmem_limit_bytes=limit * 2**20),
        cost_estimate=pl.CostEstimate(flops=flops, bytes_accessed=size, transcendentals=0),
    )(*held, *ready.values())


def like(arrays):
    shapes = {"right": (S + H, S), "obs_left": (S, S)}
    shapes |= {n: arrays[n].shape[1:] for n in ("windows", "obj_left", "grad_left") if n in arrays}
    return [pltpu.VMEM(shapes.get(n, x.shape), x.dtype) for n, x in arrays.items()]


def ring(value, axes, moves):
    sizes = [lax.axis_size(a) for a in axes]
    pairs = []
    for source in np.ndindex(*sizes):
        target = [(p + m) % n for p, m, n in zip(source, moves, sizes)]
        pairs.append((int(np.ravel_multi_index(source, sizes)), int(np.ravel_multi_index(target, sizes))))
    return lax.ppermute(value, axes, pairs)


def mirrored(value, axis, bits):
    count = lax.axis_size(axis)
    return lax.ppermute(value, axis, [(s, s ^ bits) for s in range(count)])


def runs():
    count = lax.axis_size("sy")
    return 4 if count % 4 == 0 else count


def exchanged(value):
    count_y, count_x, run = lax.axis_size("sy"), lax.axis_size("sx"), runs()
    index = np.arange(count_y * count_x).reshape(count_y // run, run, count_x)
    groups = index.transpose(1, 0, 2).reshape(run, -1).tolist()
    return lax.all_to_all(value, ("sy", "sx"), 0, 0, axis_index_groups=groups)


def down(value):
    return ring(value, ("sy",), (1,))


def up(value):
    return ring(value, ("sy",), (-1,))


def per_device(object_field, frames_data, patch_psfs):
    rows, width = object_field.shape
    count = width // S
    psfs = patch_psfs.reshape(count, S, S)
    observed = frames_data[0]
    t = {name: jnp.asarray(value) for name, value in tables().items()}
    psf_above = down(psfs)
    kept = {k: t[k] for k in ("near_right", "near_left", "windows", "obj_left", "near_inverse", "out_right")}
    named = {"psf": psfs, "object": object_field, "frame": observed} | kept
    pack_down, pack_right, pack_diagonal, obs_last, spec, spec_here, total, *got = call(
        functools.partial(psf_kernel, tuple(named)),
        named,
        {},
        [(pltpu.VMEM, f32(H, width)), (pltpu.VMEM, f32(2 * S + H, S)), (pltpu.VMEM, f32(S + H, S)),
         (pltpu.VMEM, f32(S, S)), (pltpu.HBM, f32(2 * L, width)), (pltpu.VMEM, f32(2 * L, width)), (pltpu.VMEM, f32(8, S))]
        + [(pltpu.VMEM, x) for x in like(kept)],
        [pltpu.VMEM(psfs.shape, F32), pltpu.VMEM(object_field.shape, F32), pltpu.VMEM(observed.shape, F32),
         pltpu.SemaphoreType.DMA((len(named) + 1,)), pltpu.VMEM((6 * S, width), BF16)],
        16,
        6 * 84 * 10**6,
    )
    obj_above = down(pack_down)
    got_diagonal = ring(pack_diagonal, ("sy", "sx"), (1, 1))
    got_right = ring(pack_right, ("sx",), (1,))
    obs_above = down(observed)
    obs_diagonal = ring(obs_last, ("sy", "sx"), (1, 1))
    ready = dict(zip(kept, got))
    spec_above, spec_above_here = call(
        above_kernel,
        {"psf": psf_above},
        {k: ready[k] for k in ("near_right", "near_left")},
        [(pltpu.HBM, f32(2 * L, width)), (pltpu.VMEM, f32(2 * L, width))],
        [pltpu.VMEM(psfs.shape, F32), pltpu.SemaphoreType.DMA((2,)), pltpu.VMEM((6 * S, width), BF16)],
        16,
        6 * 84 * 10**6,
        ("psf",),
    )
    ready |= {"spec_above": spec_above_here, "spec": spec_here, "total": total, "plain": t["windows"][0]}
    named = {"right": got_right, "diagonal": got_diagonal, "above": obj_above, "own": object_field}
    outs = [f32(2 * L, 2 * S), f32(S, width - S), f32(S, width - S), f32(L, S), f32(L, S)]
    more, mid_top, mid_bottom, first, last, flux = call(
        functools.partial(model_kernel, tuple(named), tuple(ready)),
        named,
        ready,
        [(pltpu.HBM, outs[0])] + [(pltpu.VMEM, o) for o in outs[1:] + [f32(8, S)]],
        like(named) + [pltpu.SemaphoreType.DMA((len(named) + 1,)), pltpu.VMEM(outs[0].shape, F32)]
        + [pltpu.VMEM((2 * width, S), F32), pltpu.VMEM((6 * S, 2 * width + 2 * S), BF16),
           pltpu.VMEM((6 * L, 2 * width + 2 * S), BF16)],
        36,
        6 * 600 * 10**6,
        ("right", "diagonal", "above"),
    )
    mid_top, mid_bottom, first, last, flux, obs_above, obs_diagonal = lax.optimization_barrier(
        (mid_top, mid_bottom, first, last, flux, obs_above, obs_diagonal)
    )
    from_right = ring(first, ("sx",), (-1,))
    from_left = ring(last, ("sx",), (1,))
    fluxes = [flux] + [mirrored(flux, "sy", k) for k in range(1, runs())]
    named = {"from_left": from_left, "from_right": from_right}
    ready = {"mid_top": mid_top, "mid_bottom": mid_bottom, "first": first, "last": last} | dict(enumerate(fluxes))
    outs = [f32(S, width + S)] * 2
    top, bottom, flux = call(
        functools.partial(join_kernel, tuple(named), tuple(ready)),
        named,
        ready,
        [(pltpu.HBM, o) for o in outs]
        + [(pltpu.VMEM, f32(lax.axis_size("sy") // runs() * lax.axis_size("sx"), 8, S))],
        like(named) + [pltpu.SemaphoreType.DMA((len(named) + len(outs),))] + [pltpu.VMEM(o.shape, F32) for o in outs],
        16,
        10**6,
        ("from_left", "from_right"),
    )
    below = up(top)
    above = down(bottom)
    flux = exchanged(flux)

    named = {"top": top, "above": above, "bottom": bottom, "below": below,
             "obs_above": obs_above, "obs": observed,
             "obs_diagonal": obs_diagonal, "obs_left": got_right,
             "res_right": t["res_right"], "near_left": t["near_left"], "spec": spec, "spec_above": spec_above, "more": more,
             "grad_left": t["grad_left"], "grad_right": t["grad_right"],
             "windows": t["windows"], "plain": t["windows"][0]}
    outs = [f32(S, width), f32(H, width), f32(H, width), f32(H, S), f32(H, width - S)]
    residual, g_top, g_bottom, g_first, g_rest = call(
        functools.partial(gradient_kernel, tuple(named)),
        named,
        {"flux": flux},
        [(pltpu.HBM, outs[0])] + [(pltpu.VMEM, o) for o in outs[1:]],
        like(named) + [pltpu.SemaphoreType.DMA((len(named) + 1,)), pltpu.VMEM(outs[0].shape, F32)]
        + [pltpu.VMEM((L, width + S), F32), pltpu.VMEM((6 * S, 2 * width + 2 * S), BF16),
           pltpu.VMEM((12 * L, 2 * width), BF16)],
        44,
        6 * 500 * 10**6,
        ("above", "below", "obs_above", "obs_diagonal", "obs_left"),
    )
    top_same = up(g_top)
    bottom_other = mirrored(g_bottom, "fr", 1)
    first_other = ring(g_first, ("sy", "fr"), (-1, 1))
    rest_other = ring(g_rest, ("sy", "fr"), (-1, 1))
    side = jnp.concatenate([g_bottom[:, :H] + bottom_other[:, :H], top_same[:, :H] + first_other[:, :H]], axis=0)
    side = ring(side, ("sx",), (-1,))
    upper = g_bottom[:, H:] + bottom_other[:, H:]
    lower_first = top_same[:, H:S] + first_other[:, H:]
    top_same, upper, lower_first, rest_other, side = lax.optimization_barrier(
        (top_same, upper, lower_first, rest_other, side)
    )
    lower = jnp.concatenate([lower_first, top_same[:, S:] + rest_other], axis=1)
    gradient = jnp.concatenate([jnp.concatenate([upper, lower], axis=0), side], axis=1)
    return gradient, residual[None]


def solution(mesh):
    placed = (P("sy", "sx"), P("fr", "sy", "sx"), P("fr", "sy", "sx", None, None))
    return jax.shard_map(
        per_device,
        mesh=mesh,
        in_specs=placed,
        out_specs=(P("sy", "sx"), P("fr", "sy", "sx")),
        check_vma=False,
    )
```

```python
import functools
import math

import jax
import jax.numpy as jnp
import numpy as np
from jax import lax
from jax.experimental import pallas as pl
from jax.experimental.pallas import tpu as pltpu
from jax.sharding import PartitionSpec as P

S = 128
L = 256
H = 64
F32 = jnp.float32
BF16 = jnp.bfloat16


def half_windows():
    n = np.arange(L, dtype=np.float64)
    s = np.sin(np.pi * (n + 0.5) / L) ** 2
    return s[:S], s[S:]


def phases(freqs, positions):
    product = (2 * np.arange(freqs)[:, None] + 1) * positions[None, :] % (2 * L)
    angle = product.astype(np.float64) * (math.pi / L)
    return np.cos(angle), np.sin(angle)


def forward_left(positions):
    c, s = phases(L, positions)
    return np.block([[c, s], [-s, c]])


def inverse_left(positions):
    c, s = phases(L, positions)
    return np.block([[c.T, -s.T], [s.T, c.T]]) / L


def forward_right(positions):
    c, s = phases(S, positions)
    return np.concatenate([c.T, -s.T], axis=1)


def inverse_right(positions):
    c, s = phases(S, positions)
    return np.concatenate([c, -s], axis=0) * (2.0 / L)


def bf16_parts(table):
    hi = table.astype(np.float32).astype(BF16)
    lo = (table - hi.astype(np.float64)).astype(np.float32).astype(BF16)
    return hi, lo


def left_table(table):
    hi, lo = bf16_parts(table)
    return np.concatenate([hi, hi, lo], axis=-1)


def right_table(table):
    hi, lo = bf16_parts(table)
    return np.concatenate([hi, hi, lo], axis=-2)


@functools.lru_cache(maxsize=1)
def tables():
    near = np.arange(S)
    up, down = half_windows()
    pairs = ((up, down), (np.where(near < H, 0.0, up), np.where(near < H, down, 0.0)))
    base, back = forward_left(near), inverse_left(near)
    t = {}
    t["near_right"] = right_table(forward_right(near))
    t["near_left"] = left_table(base)
    t["obj_left"] = np.stack(
        [left_table(np.concatenate([base * np.tile(w, 2)[None, :] for w in pair], axis=0)) for pair in pairs]
    )
    t["near_inverse"] = left_table(back)
    t["out_right"] = right_table(inverse_right(np.arange(L)))
    t["res_right"] = right_table(forward_right(np.arange(L)))
    t["grad_left"] = np.stack(
        [left_table(np.concatenate([np.tile(w, 2)[:, None] * back for w in pair], axis=1)) for pair in pairs]
    )
    t["grad_right"] = right_table(inverse_right(near))
    t["windows"] = np.stack([np.stack([np.tile(w, (8, 1)) for w in pair]) for pair in pairs]).astype(np.float32)
    return t


def split(value):
    hi = value.astype(BF16)
    return hi, (value - hi.astype(F32)).astype(BF16)


def wide_parts(value):
    hi, lo = split(value)
    return jnp.concatenate([hi, lo, hi], axis=1)


def store_parts(ref, lanes, value):
    hi, lo = split(value)
    depth = value.shape[0]
    ref[:depth, lanes] = hi
    ref[depth : 2 * depth, lanes] = lo
    ref[2 * depth :, lanes] = hi


def dot(a, b):
    return jnp.dot(a, b, preferred_element_type=F32)


def stacked(value):
    half = value.shape[1] // 2
    return jnp.concatenate([value[:, :half], value[:, half:]], axis=0)


def side_by_side(value):
    half = value.shape[0] // 2
    return jnp.concatenate([value[:half], value[half:]], axis=1)


def at(n, size=S):
    return slice(n * size, (n + 1) * size)


class Copies:
    def __init__(self, names, sources, refs, semaphores):
        self.buffers = dict(zip(names, refs))
        self.copies = {
            name: pltpu.make_async_copy(source, buffer, semaphores.at[n])
            for n, (name, source, buffer) in enumerate(zip(names, sources, refs))
        }
        self.waited = set()
        for name in names:
            self.copies[name].start()

    def __getitem__(self, name):
        if name not in self.waited:
            self.waited.add(name)
            self.copies[name].wait()
        return self.buffers[name]


def edges():
    return [(lax.axis_index(axis) == 0).astype(jnp.int32) for axis in ("sy", "sx")]


def picked(names, hbm):
    rows, columns = edges()
    edge = {"obj_left": rows, "grad_left": rows, "windows": columns}
    part = {"right": pl.ds(0, S + H), "obs_left": pl.ds(S + H, S)}
    return [h.at[edge[n]] if n in edge else h.at[part[n]] if n in part else h for n, h in zip(names, hbm)]


def psf_kernel(names, *refs):
    total = len(names)
    hbm, refs = refs[:total], refs[total:]
    down_ref, right_ref, diagonal_ref, frame_ref, spec_hbm, spec_ref, total_ref, *buffers = refs[:-5]
    psf, obj, frame, sems, parts = refs[-5:]
    t = Copies(names, picked(names, hbm), (psf, obj, frame) + tuple(buffers), sems)
    count, last = psf.shape[0], pl.ds(obj.shape[1] - S, S)
    psf, obj, frame = t["psf"], t["object"], t["frame"]
    down_ref[...] = obj[H:]
    right_ref[:S] = psf[count - 1]
    right_ref[S : S + H] = obj[:H, last]
    right_ref[S + H :] = frame[:, last]
    diagonal_ref[:S] = psf[count - 1]
    diagonal_ref[S:] = obj[H:, last]
    frame_ref[...] = frame[:, last]
    lanes = dot(wide_parts(jnp.concatenate([psf[j] for j in range(count)], axis=0)), t["near_right"][...])
    for j in range(count):
        store_parts(parts, at(j), stacked(lanes[at(j)]))
    spec_ref[...] = dot(t["near_left"][...], parts[...])
    out = pltpu.make_async_copy(spec_ref, spec_hbm, sems.at[total])
    out.start()
    total_ref[...] = jnp.full(total_ref.shape, jnp.sum(t["frame"][...]), F32)
    for name in names:
        t[name]
    out.wait()


def above_kernel(psf_hbm, right, left, spec_hbm, spec_ref, psf, sems, parts):
    t = Copies(("psf",), (psf_hbm,), (psf,), sems)
    count = psf.shape[0]
    lanes = dot(wide_parts(jnp.concatenate([t["psf"][j] for j in range(count)], axis=0)), right[...])
    for j in range(count):
        store_parts(parts, at(j), stacked(lanes[at(j)]))
    spec_ref[...] = dot(left[...], parts[...])
    out = pltpu.make_async_copy(spec_ref, spec_hbm, sems.at[1])
    out.start()
    out.wait()


def alternating():
    k = lax.broadcasted_iota(jnp.int32, (L, S), 0)
    return jnp.where(k % 2 == 0, 1.0, -1.0).astype(F32)


def model_kernel(names, ready, *refs):
    total = len(names)
    hbm, refs = refs[:total], refs[total:]
    t, refs = dict(zip(ready, refs)), refs[len(ready) :]
    more_hbm, mid_top, mid_bottom, first_ref, last_ref, flux_ref = refs[:6]
    buffers, sems, more_ref, x_ref, x_parts, y_parts = refs[6 : 6 + total], *refs[6 + total :]
    got = Copies(names, picked(names, hbm), buffers, sems)
    out = pltpu.make_async_copy(more_ref, more_hbm, sems.at[total])
    row_edge, column_edge = edges()
    alpha, beta = 1.0 - row_edge.astype(F32), 1.0 - column_edge.astype(F32)
    right_ref, diagonal_ref, above_ref, own_ref = [got[n] for n in ("right", "diagonal", "above", "own")]
    count = own_ref.shape[1] // S
    windows = [t["windows"][w, :1] for w in range(2)]
    plain = [t["plain"][w, :1] for w in range(2)]
    for q in range(count):
        lo = q * S
        if q == 0:
            left = jnp.concatenate([diagonal_ref[S:], right_ref[S:]], axis=0)[:, H:]
        else:
            left = jnp.concatenate([above_ref[:, lo - S : lo], own_ref[:H, lo - S : lo]], axis=0)[:, H:]
        here = jnp.concatenate([above_ref[:, lo : lo + S], own_ref[:H, lo : lo + S]], axis=0)[:, :H]
        x = jnp.concatenate([left, here], axis=1)
        for w in range(2):
            x_ref[at(2 * q + w)] = x * (windows if q == 0 else plain)[w]
    psfs = [diagonal_ref[:S], right_ref[:S]]
    lanes = dot(wide_parts(jnp.concatenate([x_ref[...]] + psfs, axis=0)), t["near_right"][...])
    for n in range(2 * count + 2):
        store_parts(x_parts, at(n), stacked(lanes[at(n)]))
    more_ref[...] = dot(t["near_left"][...], x_parts[:, 2 * count * S :])
    out.start()
    spec_ref, spec_above = t["spec"], t["spec_above"]
    obj_left = t["obj_left"]
    sign = alternating()
    for pair in range(count // 2):
        x_specs = dot(obj_left[...], x_parts[:, pair * 4 * S : (pair + 1) * 4 * S])
        for q in (2 * pair, 2 * pair + 1):
            y = {}
            for r in range(2):
                for w in range(2):
                    lanes = at(2 * (q % 2) + w)
                    x_re = x_specs[at(2 * r, L), lanes]
                    x_im = x_specs[at(2 * r + 1, L), lanes]
                    j = q - w
                    own = (spec_ref, spec_above)[r]
                    source, lanes = (own, at(j)) if j >= 0 else (more_ref, at(1 - r))
                    h_re, h_im = source[:L, lanes], source[L:, lanes]
                    y[r, w] = (x_re * h_re - x_im * h_im, x_re * h_im + x_im * h_re)
            if q == 0:
                variants = [
                    [tuple(y[r, 1][c] + beta * y[r, 0][c] for c in range(2)) for r in range(2)],
                    [tuple(y[r, 0][c] + beta * y[r, 1][c] for c in range(2)) for r in range(2)],
                ]
            else:
                variants = [[tuple(y[r, 0][c] + y[r, 1][c] for c in range(2)) for r in range(2)]]
            for v, (upper, lower) in enumerate(variants):
                slot = v if q == 0 else q + 1
                top = [lower[c] + alpha * upper[c] for c in range(2)]
                bottom = [upper[c] + alpha * lower[c] for c in range(2)]
                store_parts(y_parts, at(slot), jnp.concatenate(top, axis=0))
                turned = jnp.concatenate([-sign * bottom[1], sign * bottom[0]], axis=0)
                store_parts(y_parts, at(count + 1 + slot), turned)
    rows = dot(t["near_inverse"][...], y_parts[...])
    blocks = jnp.concatenate([side_by_side(rows[:, at(n)]) for n in range(2 * count + 2)], axis=0)
    image = dot(wide_parts(blocks), t["out_right"][...])
    flux = 0.0
    for half in range(2):
        base = half * (count + 1)
        lefts = [image[at(base), :S]] + [image[at(base + q + 1), :S] for q in range(1, count)]
        rights = [image[at(base + q + 1), S:] for q in range(count)]
        first_ref[at(half)] = lefts[0]
        last_ref[at(half)] = rights[-1]
        middle = mid_bottom if half else mid_top
        together = lefts[0] + rights[-1]
        for q in range(1, count):
            block = lefts[q] + rights[q - 1]
            middle[:, at(q - 1)] = block
            together = together + block
        flux = flux + jnp.sum(together)
    lane = lax.broadcasted_iota(jnp.int32, flux_ref.shape, 1)
    flux_ref[...] = jnp.where(lane < H, flux, t["total"][...])
    out.wait()


def join_kernel(names, ready, *refs):
    total = len(names)
    hbm, refs = refs[:total], refs[total:]
    here, refs = dict(zip(ready, refs)), refs[len(ready) :]
    fluxes = [here[n] for n in ready if n not in ("mid_top", "mid_bottom", "first", "last")]
    top_hbm, bottom_hbm, totals_ref = refs[:3]
    buffers, sems, top_ref, bottom_ref = refs[3 : 3 + total], refs[3 + total], refs[4 + total], refs[5 + total]
    t = Copies(names, hbm, buffers, sems)
    outs = []
    for half, out, place in ((0, top_ref, top_hbm), (1, bottom_ref, bottom_hbm)):
        mid = here["mid_bottom" if half else "mid_top"]
        width = mid.shape[1]
        out[:, S : S + width] = mid[...]
        out[:, :S] = here["first"][at(half)] + t["from_left"][at(half)]
        out[:, S + width :] = here["last"][at(half)] + t["from_right"][at(half)]
        outs.append(pltpu.make_async_copy(out, place, sems.at[total + half]))
        outs[-1].start()
    flux = sum([f[...] for f in fluxes[1:]], fluxes[0][...])
    totals_ref[...] = jnp.broadcast_to(flux[None, :1], totals_ref.shape)
    for copy in outs:
        copy.wait()


def gradient_kernel(names, *refs):
    total = len(names)
    hbm, flux_ref, refs = refs[:total], refs[total], refs[total + 1 :]
    residual_hbm, out_top, out_bottom, first_ref, rest_ref = refs[:5]
    buffers, sems, residual_ref, r_ref, r_parts, g_parts = refs[5 : 5 + total], *refs[5 + total :]
    t = Copies(names, picked(names, hbm), buffers, sems)
    sent = pltpu.make_async_copy(residual_ref, residual_hbm, sems.at[total])
    row_edge, column_edge = edges()
    alpha, beta = 1.0 - row_edge.astype(F32), 1.0 - column_edge.astype(F32)
    width = residual_ref.shape[1]
    count = width // S
    sums = jnp.sum(flux_ref[...], axis=0)
    gain = sums[0, H] / sums[0, 0]
    r_ref[:S] = gain * (t["top"][...] + t["above"][...])
    r_ref[S:] = gain * (t["bottom"][...] + t["below"][...])
    r_ref[:S, S:] -= t["obs_above"][...]
    r_ref[S:, S:] -= t["obs"][...]
    r_ref[:S, :S] -= t["obs_diagonal"][...]
    r_ref[S:, :S] -= t["obs_left"][...]
    residual_ref[...] = r_ref[S:, S:]
    sent.start()
    near, far = r_ref[:, :S], r_ref[:, S : 2 * S]
    blocks = [
        jnp.concatenate([beta * near, far], axis=1),
        jnp.concatenate([near, beta * far], axis=1),
    ] + [r_ref[:, q * S : (q + 2) * S] for q in range(1, count)]
    lanes = dot(wide_parts(jnp.concatenate(blocks, axis=0)), t["res_right"][...])
    for n in range(count + 1):
        value = lanes[at(n, L)]
        store_parts(r_parts, at(n), stacked(value[:S]))
        store_parts(r_parts, at(count + 1 + n), stacked(value[S:]))
    spectra = dot(t["near_left"][...], r_parts[...])
    sign = alternating()
    spec_ref, spec_above, more_ref = t["spec"], t["spec_above"], t["more"]
    seen = []
    for n in range(count + 1):
        top = [spectra[at(c, L), at(n)] for c in range(2)]
        raw = [spectra[at(c, L), at(count + 1 + n)] for c in range(2)]
        bottom = [sign * raw[1], -sign * raw[0]]
        seen.append(
            [
                [bottom[c] + alpha * top[c] for c in range(2)],
                [top[c] + alpha * bottom[c] for c in range(2)],
            ]
        )
    grad_left = t["grad_left"]
    outs = []
    for pair in range(count // 2):
        for q in (2 * pair, 2 * pair + 1):
            for w in range(2):
                slot = w if q == 0 else q + 1
                j = q - w
                for r in range(2):
                    own = (spec_ref, spec_above)[r]
                    source, lanes = (own, at(j)) if j >= 0 else (more_ref, at(1 - r))
                    h_re, h_im = source[:L, lanes], source[L:, lanes]
                    r_re, r_im = seen[slot][r]
                    for c, part in enumerate((r_re * h_re + r_im * h_im, r_im * h_re - r_re * h_im)):
                        hi, lo = split(part)
                        place = (2 * r + c) * L
                        for n, value in enumerate((hi, lo, hi)):
                            g_parts[4 * n * L + place : 4 * n * L + place + L, at(2 * q + w)] = value
        g = dot(grad_left[...], g_parts[:, pair * 4 * S : (pair + 1) * 4 * S])
        outs += [side_by_side(g[:, at(n)]) for n in range(4)]
    out = dot(wide_parts(jnp.concatenate(outs, axis=0)), t["grad_right"][...])
    for q in range(count):
        windows = t["windows"] if q == 0 else t["plain"]
        grad = gain * (out[at(2 * q)] * windows[0, :1] + out[at(2 * q + 1)] * windows[1, :1])
        out_top[:, at(q)] = grad[:H]
        out_bottom[:, at(q)] = grad[H:]
    first_ref[...] = out_top[:, :S]
    rest_ref[...] = out_top[:, S:]
    sent.wait()


def f32(*shape):
    return jax.ShapeDtypeStruct(shape, F32)


def call(kernel, named, ready, outs, scratch, limit, flops, loose=()):
    hbm, vmem = pl.BlockSpec(memory_space=pltpu.HBM), pl.BlockSpec(memory_space=pltpu.VMEM)
    held = [x if n in loose else pltpu.with_memory_space_constraint(x, pltpu.HBM) for n, x in named.items()]
    size = sum(math.prod(x.shape) * x.dtype.itemsize for x in named.values())
    return pl.pallas_call(
        kernel,
        out_shape=[place(o.shape, o.dtype) for place, o in outs],
        in_specs=[hbm] * len(named) + [vmem] * len(ready),
        out_specs=[hbm if place is pltpu.HBM else vmem for place, _ in outs],
        scratch_shapes=scratch,
        compiler_params=pltpu.CompilerParams(vmem_limit_bytes=limit * 2**20),
        cost_estimate=pl.CostEstimate(flops=flops, bytes_accessed=size, transcendentals=0),
    )(*held, *ready.values())


def like(arrays):
    shapes = {"right": (S + H, S), "obs_left": (S, S)}
    shapes |= {n: arrays[n].shape[1:] for n in ("windows", "obj_left", "grad_left") if n in arrays}
    return [pltpu.VMEM(shapes.get(n, x.shape), x.dtype) for n, x in arrays.items()]


def ring(value, axes, moves):
    sizes = [lax.axis_size(a) for a in axes]
    pairs = []
    for source in np.ndindex(*sizes):
        target = [(p + m) % n for p, m, n in zip(source, moves, sizes)]
        pairs.append((int(np.ravel_multi_index(source, sizes)), int(np.ravel_multi_index(target, sizes))))
    return lax.ppermute(value, axes, pairs)


def mirrored(value, axis, bits):
    count = lax.axis_size(axis)
    return lax.ppermute(value, axis, [(s, s ^ bits) for s in range(count)])


def runs():
    count = lax.axis_size("sy")
    return 4 if count % 4 == 0 else count


def exchanged(value):
    count_y, count_x, run = lax.axis_size("sy"), lax.axis_size("sx"), runs()
    index = np.arange(count_y * count_x).reshape(count_y // run, run, count_x)
    groups = index.transpose(1, 0, 2).reshape(run, -1).tolist()
    return lax.all_to_all(value, ("sy", "sx"), 0, 0, axis_index_groups=groups)


def down(value):
    return ring(value, ("sy",), (1,))


def up(value):
    return ring(value, ("sy",), (-1,))


def per_device(object_field, frames_data, patch_psfs):
    rows, width = object_field.shape
    count = width // S
    psfs = patch_psfs.reshape(count, S, S)
    observed = frames_data[0]
    t = {name: jnp.asarray(value) for name, value in tables().items()}
    psf_above = down(psfs)
    kept = {k: t[k] for k in ("near_right", "near_left", "windows", "obj_left", "near_inverse", "out_right")}
    named = {"psf": psfs, "object": object_field, "frame": observed} | kept
    pack_down, pack_right, pack_diagonal, obs_last, spec, spec_here, total, *got = call(
        functools.partial(psf_kernel, tuple(named)),
        named,
        {},
        [(pltpu.VMEM, f32(H, width)), (pltpu.VMEM, f32(2 * S + H, S)), (pltpu.VMEM, f32(S + H, S)),
         (pltpu.VMEM, f32(S, S)), (pltpu.HBM, f32(2 * L, width)), (pltpu.VMEM, f32(2 * L, width)), (pltpu.VMEM, f32(8, S))]
        + [(pltpu.VMEM, x) for x in like(kept)],
        [pltpu.VMEM(psfs.shape, F32), pltpu.VMEM(object_field.shape, F32), pltpu.VMEM(observed.shape, F32),
         pltpu.SemaphoreType.DMA((len(named) + 1,)), pltpu.VMEM((6 * S, width), BF16)],
        16,
        6 * 84 * 10**6,
    )
    obj_above = down(pack_down)
    got_diagonal = ring(pack_diagonal, ("sy", "sx"), (1, 1))
    got_right = ring(pack_right, ("sx",), (1,))
    obs_above = down(observed)
    obs_diagonal = ring(obs_last, ("sy", "sx"), (1, 1))
    ready = dict(zip(kept, got))
    spec_above, spec_above_here = call(
        above_kernel,
        {"psf": psf_above},
        {k: ready[k] for k in ("near_right", "near_left")},
        [(pltpu.HBM, f32(2 * L, width)), (pltpu.VMEM, f32(2 * L, width))],
        [pltpu.VMEM(psfs.shape, F32), pltpu.SemaphoreType.DMA((2,)), pltpu.VMEM((6 * S, width), BF16)],
        16,
        6 * 84 * 10**6,
        ("psf",),
    )
    ready |= {"spec_above": spec_above_here, "spec": spec_here, "total": total, "plain": t["windows"][0]}
    named = {"right": got_right, "diagonal": got_diagonal, "above": obj_above, "own": object_field}
    outs = [f32(2 * L, 2 * S), f32(S, width - S), f32(S, width - S), f32(L, S), f32(L, S)]
    more, mid_top, mid_bottom, first, last, flux = call(
        functools.partial(model_kernel, tuple(named), tuple(ready)),
        named,
        ready,
        [(pltpu.HBM, outs[0])] + [(pltpu.VMEM, o) for o in outs[1:] + [f32(8, S)]],
        like(named) + [pltpu.SemaphoreType.DMA((len(named) + 1,)), pltpu.VMEM(outs[0].shape, F32)]
        + [pltpu.VMEM((2 * width, S), F32), pltpu.VMEM((6 * S, 2 * width + 2 * S), BF16),
           pltpu.VMEM((6 * L, 2 * width + 2 * S), BF16)],
        36,
        6 * 600 * 10**6,
        ("right", "diagonal", "above"),
    )
    mid_top, mid_bottom, first, last, flux, obs_above, obs_diagonal = lax.optimization_barrier(
        (mid_top, mid_bottom, first, last, flux, obs_above, obs_diagonal)
    )
    from_right = ring(first, ("sx",), (-1,))
    from_left = ring(last, ("sx",), (1,))
    fluxes = [flux] + [mirrored(flux, "sy", k) for k in range(1, runs())]
    named = {"from_left": from_left, "from_right": from_right}
    ready = {"mid_top": mid_top, "mid_bottom": mid_bottom, "first": first, "last": last} | dict(enumerate(fluxes))
    outs = [f32(S, width + S)] * 2
    top, bottom, flux = call(
        functools.partial(join_kernel, tuple(named), tuple(ready)),
        named,
        ready,
        [(pltpu.HBM, o) for o in outs]
        + [(pltpu.VMEM, f32(lax.axis_size("sy") // runs() * lax.axis_size("sx"), 1, S))],
        like(named) + [pltpu.SemaphoreType.DMA((len(named) + len(outs),))] + [pltpu.VMEM(o.shape, F32) for o in outs],
        16,
        10**6,
        ("from_left", "from_right"),
    )
    below = up(top)
    above = down(bottom)
    flux = exchanged(flux)

    named = {"top": top, "above": above, "bottom": bottom, "below": below,
             "obs_above": obs_above, "obs": observed,
             "obs_diagonal": obs_diagonal, "obs_left": got_right,
             "res_right": t["res_right"], "near_left": t["near_left"], "spec": spec, "spec_above": spec_above, "more": more,
             "grad_left": t["grad_left"], "grad_right": t["grad_right"],
             "windows": t["windows"], "plain": t["windows"][0]}
    outs = [f32(S, width), f32(H, width), f32(H, width), f32(H, S), f32(H, width - S)]
    residual, g_top, g_bottom, g_first, g_rest = call(
        functools.partial(gradient_kernel, tuple(named)),
        named,
        {"flux": flux},
        [(pltpu.HBM, outs[0])] + [(pltpu.VMEM, o) for o in outs[1:]],
        like(named) + [pltpu.SemaphoreType.DMA((len(named) + 1,)), pltpu.VMEM(outs[0].shape, F32)]
        + [pltpu.VMEM((L, width + S), F32), pltpu.VMEM((6 * S, 2 * width + 2 * S), BF16),
           pltpu.VMEM((12 * L, 2 * width), BF16)],
        44,
        6 * 500 * 10**6,
        ("above", "below", "obs_above", "obs_diagonal", "obs_left"),
    )
    top_same = up(g_top)
    bottom_other = mirrored(g_bottom, "fr", 1)
    first_other = ring(g_first, ("sy", "fr"), (-1, 1))
    rest_other = ring(g_rest, ("sy", "fr"), (-1, 1))
    side = jnp.concatenate([g_bottom[:, :H] + bottom_other[:, :H], top_same[:, :H] + first_other[:, :H]], axis=0)
    side = ring(side, ("sx",), (-1,))
    upper = g_bottom[:, H:] + bottom_other[:, H:]
    lower_first = top_same[:, H:S] + first_other[:, H:]
    top_same, upper, lower_first, rest_other, side = lax.optimization_barrier(
        (top_same, upper, lower_first, rest_other, side)
    )
    lower = jnp.concatenate([lower_first, top_same[:, S:] + rest_other], axis=1)
    gradient = jnp.concatenate([jnp.concatenate([upper, lower], axis=0), side], axis=1)
    return gradient, residual[None]


def solution(mesh):
    placed = (P("sy", "sx"), P("fr", "sy", "sx"), P("fr", "sy", "sx", None, None))
    return jax.shard_map(
        per_device,
        mesh=mesh,
        in_specs=placed,
        out_specs=(P("sy", "sx"), P("fr", "sy", "sx")),
        check_vma=False,
    )
```

```python
import functools
import math

import jax
import jax.numpy as jnp
import numpy as np
from jax import lax
from jax.experimental import pallas as pl
from jax.experimental.pallas import tpu as pltpu
from jax.sharding import PartitionSpec as P

S = 128
L = 256
H = 64
F32 = jnp.float32
BF16 = jnp.bfloat16


def half_windows():
    n = np.arange(L, dtype=np.float64)
    s = np.sin(np.pi * (n + 0.5) / L) ** 2
    return s[:S], s[S:]


def phases(freqs, positions):
    product = (2 * np.arange(freqs)[:, None] + 1) * positions[None, :] % (2 * L)
    angle = product.astype(np.float64) * (math.pi / L)
    return np.cos(angle), np.sin(angle)


def forward_left(positions):
    c, s = phases(L, positions)
    return np.block([[c, s], [-s, c]])


def inverse_left(positions):
    c, s = phases(L, positions)
    return np.block([[c.T, -s.T], [s.T, c.T]]) / L


def forward_right(positions):
    c, s = phases(S, positions)
    return np.concatenate([c.T, -s.T], axis=1)


def inverse_right(positions):
    c, s = phases(S, positions)
    return np.concatenate([c, -s], axis=0) * (2.0 / L)


def bf16_parts(table):
    hi = table.astype(np.float32).astype(BF16)
    lo = (table - hi.astype(np.float64)).astype(np.float32).astype(BF16)
    return hi, lo


def left_table(table):
    hi, lo = bf16_parts(table)
    return np.concatenate([hi, hi, lo], axis=-1)


def right_table(table):
    hi, lo = bf16_parts(table)
    return np.concatenate([hi, hi, lo], axis=-2)


@functools.lru_cache(maxsize=1)
def tables():
    near = np.arange(S)
    up, down = half_windows()
    pairs = ((up, down), (np.where(near < H, 0.0, up), np.where(near < H, down, 0.0)))
    base, back = forward_left(near), inverse_left(near)
    t = {}
    t["near_right"] = right_table(forward_right(near))
    t["near_left"] = left_table(base)
    t["obj_left"] = np.stack(
        [left_table(np.concatenate([base * np.tile(w, 2)[None, :] for w in pair], axis=0)) for pair in pairs]
    )
    t["near_inverse"] = left_table(back)
    t["out_right"] = right_table(inverse_right(np.arange(L)))
    t["res_right"] = right_table(forward_right(np.arange(L)))
    t["grad_left"] = np.stack(
        [left_table(np.concatenate([np.tile(w, 2)[:, None] * back for w in pair], axis=1)) for pair in pairs]
    )
    t["grad_right"] = right_table(inverse_right(near))
    t["windows"] = np.stack([np.stack([np.tile(w, (8, 1)) for w in pair]) for pair in pairs]).astype(np.float32)
    return t


def split(value):
    hi = value.astype(BF16)
    return hi, (value - hi.astype(F32)).astype(BF16)


def wide_parts(value):
    hi, lo = split(value)
    return jnp.concatenate([hi, lo, hi], axis=1)


def store_parts(ref, lanes, value):
    hi, lo = split(value)
    depth = value.shape[0]
    ref[:depth, lanes] = hi
    ref[depth : 2 * depth, lanes] = lo
    ref[2 * depth :, lanes] = hi


def dot(a, b):
    return jnp.dot(a, b, preferred_element_type=F32)


def stacked(value):
    half = value.shape[1] // 2
    return jnp.concatenate([value[:, :half], value[:, half:]], axis=0)


def side_by_side(value):
    half = value.shape[0] // 2
    return jnp.concatenate([value[:half], value[half:]], axis=1)


def at(n, size=S):
    return slice(n * size, (n + 1) * size)


class Copies:
    def __init__(self, names, sources, refs, semaphores):
        self.buffers = dict(zip(names, refs))
        self.copies = {
            name: pltpu.make_async_copy(source, buffer, semaphores.at[n])
            for n, (name, source, buffer) in enumerate(zip(names, sources, refs))
        }
        self.waited = set()
        for name in names:
            self.copies[name].start()

    def __getitem__(self, name):
        if name not in self.waited:
            self.waited.add(name)
            self.copies[name].wait()
        return self.buffers[name]


def edges():
    return [(lax.axis_index(axis) == 0).astype(jnp.int32) for axis in ("sy", "sx")]


def picked(names, hbm):
    rows, columns = edges()
    edge = {"obj_left": rows, "grad_left": rows, "windows": columns}
    part = {"right": pl.ds(0, S + H), "obs_left": pl.ds(S + H, S)}
    return [h.at[edge[n]] if n in edge else h.at[part[n]] if n in part else h for n, h in zip(names, hbm)]


def psf_kernel(names, *refs):
    total = len(names)
    hbm, refs = refs[:total], refs[total:]
    down_ref, right_ref, diagonal_ref, frame_ref, spec_hbm, spec_ref, total_ref, *buffers = refs[:-5]
    psf, obj, frame, sems, parts = refs[-5:]
    t = Copies(names, picked(names, hbm), (psf, obj, frame) + tuple(buffers), sems)
    count, last = psf.shape[0], pl.ds(obj.shape[1] - S, S)
    psf, obj, frame = t["psf"], t["object"], t["frame"]
    down_ref[...] = obj[H:]
    right_ref[:S] = psf[count - 1]
    right_ref[S : S + H] = obj[:H, last]
    right_ref[S + H :] = frame[:, last]
    diagonal_ref[:S] = psf[count - 1]
    diagonal_ref[S:] = obj[H:, last]
    frame_ref[...] = frame[:, last]
    lanes = dot(wide_parts(jnp.concatenate([psf[j] for j in range(count)], axis=0)), t["near_right"][...])
    for j in range(count):
        store_parts(parts, at(j), stacked(lanes[at(j)]))
    spec_ref[...] = dot(t["near_left"][...], parts[...])
    out = pltpu.make_async_copy(spec_ref, spec_hbm, sems.at[total])
    out.start()
    total_ref[...] = jnp.full(total_ref.shape, jnp.sum(t["frame"][...]), F32)
    for name in names:
        t[name]
    out.wait()


def above_kernel(psf_hbm, right, left, spec_hbm, spec_ref, psf, sems, parts):
    t = Copies(("psf",), (psf_hbm,), (psf,), sems)
    count = psf.shape[0]
    lanes = dot(wide_parts(jnp.concatenate([t["psf"][j] for j in range(count)], axis=0)), right[...])
    for j in range(count):
        store_parts(parts, at(j), stacked(lanes[at(j)]))
    spec_ref[...] = dot(left[...], parts[...])
    out = pltpu.make_async_copy(spec_ref, spec_hbm, sems.at[1])
    out.start()
    out.wait()


def alternating():
    k = lax.broadcasted_iota(jnp.int32, (L, S), 0)
    return jnp.where(k % 2 == 0, 1.0, -1.0).astype(F32)


def model_kernel(names, ready, *refs):
    total = len(names)
    hbm, refs = refs[:total], refs[total:]
    t, refs = dict(zip(ready, refs)), refs[len(ready) :]
    more_hbm, mid_top, mid_bottom, first_ref, last_ref, flux_ref = refs[:6]
    buffers, sems, more_ref, x_ref, x_parts, y_parts = refs[6 : 6 + total], *refs[6 + total :]
    got = Copies(names, picked(names, hbm), buffers, sems)
    out = pltpu.make_async_copy(more_ref, more_hbm, sems.at[total])
    row_edge, column_edge = edges()
    alpha, beta = 1.0 - row_edge.astype(F32), 1.0 - column_edge.astype(F32)
    right_ref, diagonal_ref, above_ref, own_ref = [got[n] for n in ("right", "diagonal", "above", "own")]
    count = own_ref.shape[1] // S
    windows = [t["windows"][w, :1] for w in range(2)]
    plain = [t["plain"][w, :1] for w in range(2)]
    for q in range(count):
        lo = q * S
        if q == 0:
            left = jnp.concatenate([diagonal_ref[S:], right_ref[S:]], axis=0)[:, H:]
        else:
            left = jnp.concatenate([above_ref[:, lo - S : lo], own_ref[:H, lo - S : lo]], axis=0)[:, H:]
        here = jnp.concatenate([above_ref[:, lo : lo + S], own_ref[:H, lo : lo + S]], axis=0)[:, :H]
        x = jnp.concatenate([left, here], axis=1)
        for w in range(2):
            x_ref[at(2 * q + w)] = x * (windows if q == 0 else plain)[w]
    psfs = [diagonal_ref[:S], right_ref[:S]]
    lanes = dot(wide_parts(jnp.concatenate([x_ref[...]] + psfs, axis=0)), t["near_right"][...])
    for n in range(2 * count + 2):
        store_parts(x_parts, at(n), stacked(lanes[at(n)]))
    more_ref[...] = dot(t["near_left"][...], x_parts[:, 2 * count * S :])
    out.start()
    spec_ref, spec_above = t["spec"], t["spec_above"]
    obj_left = t["obj_left"]
    sign = alternating()
    for pair in range(count // 2):
        x_specs = dot(obj_left[...], x_parts[:, pair * 4 * S : (pair + 1) * 4 * S])
        for q in (2 * pair, 2 * pair + 1):
            y = {}
            for r in range(2):
                for w in range(2):
                    lanes = at(2 * (q % 2) + w)
                    x_re = x_specs[at(2 * r, L), lanes]
                    x_im = x_specs[at(2 * r + 1, L), lanes]
                    j = q - w
                    own = (spec_ref, spec_above)[r]
                    source, lanes = (own, at(j)) if j >= 0 else (more_ref, at(1 - r))
                    h_re, h_im = source[:L, lanes], source[L:, lanes]
                    y[r, w] = (x_re * h_re - x_im * h_im, x_re * h_im + x_im * h_re)
            if q == 0:
                variants = [
                    [tuple(y[r, 1][c] + beta * y[r, 0][c] for c in range(2)) for r in range(2)],
                    [tuple(y[r, 0][c] + beta * y[r, 1][c] for c in range(2)) for r in range(2)],
                ]
            else:
                variants = [[tuple(y[r, 0][c] + y[r, 1][c] for c in range(2)) for r in range(2)]]
            for v, (upper, lower) in enumerate(variants):
                slot = v if q == 0 else q + 1
                top = [lower[c] + alpha * upper[c] for c in range(2)]
                bottom = [upper[c] + alpha * lower[c] for c in range(2)]
                store_parts(y_parts, at(slot), jnp.concatenate(top, axis=0))
                turned = jnp.concatenate([-sign * bottom[1], sign * bottom[0]], axis=0)
                store_parts(y_parts, at(count + 1 + slot), turned)
    rows = dot(t["near_inverse"][...], y_parts[...])
    blocks = jnp.concatenate([side_by_side(rows[:, at(n)]) for n in range(2 * count + 2)], axis=0)
    image = dot(wide_parts(blocks), t["out_right"][...])
    flux = 0.0
    for half in range(2):
        base = half * (count + 1)
        lefts = [image[at(base), :S]] + [image[at(base + q + 1), :S] for q in range(1, count)]
        rights = [image[at(base + q + 1), S:] for q in range(count)]
        first_ref[at(half)] = lefts[0]
        last_ref[at(half)] = rights[-1]
        middle = mid_bottom if half else mid_top
        together = lefts[0] + rights[-1]
        for q in range(1, count):
            block = lefts[q] + rights[q - 1]
            middle[:, at(q - 1)] = block
            together = together + block
        flux = flux + jnp.sum(together)
    lane = lax.broadcasted_iota(jnp.int32, flux_ref.shape, 1)
    flux_ref[...] = jnp.where(lane < H, flux, t["total"][:1])
    out.wait()


def join_kernel(names, ready, *refs):
    total = len(names)
    hbm, refs = refs[:total], refs[total:]
    here, refs = dict(zip(ready, refs)), refs[len(ready) :]
    fluxes = [here[n] for n in ready if n not in ("mid_top", "mid_bottom", "first", "last")]
    top_hbm, bottom_hbm, totals_ref = refs[:3]
    buffers, sems, top_ref, bottom_ref = refs[3 : 3 + total], refs[3 + total], refs[4 + total], refs[5 + total]
    t = Copies(names, hbm, buffers, sems)
    outs = []
    for half, out, place in ((0, top_ref, top_hbm), (1, bottom_ref, bottom_hbm)):
        mid = here["mid_bottom" if half else "mid_top"]
        width = mid.shape[1]
        out[:, S : S + width] = mid[...]
        out[:, :S] = here["first"][at(half)] + t["from_left"][at(half)]
        out[:, S + width :] = here["last"][at(half)] + t["from_right"][at(half)]
        outs.append(pltpu.make_async_copy(out, place, sems.at[total + half]))
        outs[-1].start()
    flux = sum([f[...] for f in fluxes[1:]], fluxes[0][...])
    totals_ref[...] = jnp.broadcast_to(flux[None, :1], totals_ref.shape)
    for copy in outs:
        copy.wait()


def gradient_kernel(names, *refs):
    total = len(names)
    hbm, flux_ref, refs = refs[:total], refs[total], refs[total + 1 :]
    residual_hbm, out_top, out_bottom, first_ref, rest_ref = refs[:5]
    buffers, sems, residual_ref, r_ref, r_parts, g_parts = refs[5 : 5 + total], *refs[5 + total :]
    t = Copies(names, picked(names, hbm), buffers, sems)
    sent = pltpu.make_async_copy(residual_ref, residual_hbm, sems.at[total])
    row_edge, column_edge = edges()
    alpha, beta = 1.0 - row_edge.astype(F32), 1.0 - column_edge.astype(F32)
    width = residual_ref.shape[1]
    count = width // S
    sums = jnp.sum(flux_ref[...], axis=0)
    gain = sums[0, H] / sums[0, 0]
    r_ref[:S] = gain * (t["top"][...] + t["above"][...])
    r_ref[S:] = gain * (t["bottom"][...] + t["below"][...])
    r_ref[:S, S:] -= t["obs_above"][...]
    r_ref[S:, S:] -= t["obs"][...]
    r_ref[:S, :S] -= t["obs_diagonal"][...]
    r_ref[S:, :S] -= t["obs_left"][...]
    residual_ref[...] = r_ref[S:, S:]
    sent.start()
    near, far = r_ref[:, :S], r_ref[:, S : 2 * S]
    blocks = [
        jnp.concatenate([beta * near, far], axis=1),
        jnp.concatenate([near, beta * far], axis=1),
    ] + [r_ref[:, q * S : (q + 2) * S] for q in range(1, count)]
    lanes = dot(wide_parts(jnp.concatenate(blocks, axis=0)), t["res_right"][...])
    for n in range(count + 1):
        value = lanes[at(n, L)]
        store_parts(r_parts, at(n), stacked(value[:S]))
        store_parts(r_parts, at(count + 1 + n), stacked(value[S:]))
    spectra = dot(t["near_left"][...], r_parts[...])
    sign = alternating()
    spec_ref, spec_above, more_ref = t["spec"], t["spec_above"], t["more"]
    seen = []
    for n in range(count + 1):
        top = [spectra[at(c, L), at(n)] for c in range(2)]
        raw = [spectra[at(c, L), at(count + 1 + n)] for c in range(2)]
        bottom = [sign * raw[1], -sign * raw[0]]
        seen.append(
            [
                [bottom[c] + alpha * top[c] for c in range(2)],
                [top[c] + alpha * bottom[c] for c in range(2)],
            ]
        )
    grad_left = t["grad_left"]
    outs = []
    for pair in range(count // 2):
        for q in (2 * pair, 2 * pair + 1):
            for w in range(2):
                slot = w if q == 0 else q + 1
                j = q - w
                for r in range(2):
                    own = (spec_ref, spec_above)[r]
                    source, lanes = (own, at(j)) if j >= 0 else (more_ref, at(1 - r))
                    h_re, h_im = source[:L, lanes], source[L:, lanes]
                    r_re, r_im = seen[slot][r]
                    for c, part in enumerate((r_re * h_re + r_im * h_im, r_im * h_re - r_re * h_im)):
                        hi, lo = split(part)
                        place = (2 * r + c) * L
                        for n, value in enumerate((hi, lo, hi)):
                            g_parts[4 * n * L + place : 4 * n * L + place + L, at(2 * q + w)] = value
        g = dot(grad_left[...], g_parts[:, pair * 4 * S : (pair + 1) * 4 * S])
        outs += [side_by_side(g[:, at(n)]) for n in range(4)]
    out = dot(wide_parts(jnp.concatenate(outs, axis=0)), t["grad_right"][...])
    for q in range(count):
        windows = t["windows"] if q == 0 else t["plain"]
        grad = gain * (out[at(2 * q)] * windows[0, :1] + out[at(2 * q + 1)] * windows[1, :1])
        out_top[:, at(q)] = grad[:H]
        out_bottom[:, at(q)] = grad[H:]
    first_ref[...] = out_top[:, :S]
    rest_ref[...] = out_top[:, S:]
    sent.wait()


def f32(*shape):
    return jax.ShapeDtypeStruct(shape, F32)


def call(kernel, named, ready, outs, scratch, limit, flops, loose=()):
    hbm, vmem = pl.BlockSpec(memory_space=pltpu.HBM), pl.BlockSpec(memory_space=pltpu.VMEM)
    held = [x if n in loose else pltpu.with_memory_space_constraint(x, pltpu.HBM) for n, x in named.items()]
    size = sum(math.prod(x.shape) * x.dtype.itemsize for x in named.values())
    return pl.pallas_call(
        kernel,
        out_shape=[place(o.shape, o.dtype) for place, o in outs],
        in_specs=[hbm] * len(named) + [vmem] * len(ready),
        out_specs=[hbm if place is pltpu.HBM else vmem for place, _ in outs],
        scratch_shapes=scratch,
        compiler_params=pltpu.CompilerParams(vmem_limit_bytes=limit * 2**20),
        cost_estimate=pl.CostEstimate(flops=flops, bytes_accessed=size, transcendentals=0),
    )(*held, *ready.values())


def like(arrays):
    shapes = {"right": (S + H, S), "obs_left": (S, S)}
    shapes |= {n: arrays[n].shape[1:] for n in ("windows", "obj_left", "grad_left") if n in arrays}
    return [pltpu.VMEM(shapes.get(n, x.shape), x.dtype) for n, x in arrays.items()]


def ring(value, axes, moves):
    sizes = [lax.axis_size(a) for a in axes]
    pairs = []
    for source in np.ndindex(*sizes):
        target = [(p + m) % n for p, m, n in zip(source, moves, sizes)]
        pairs.append((int(np.ravel_multi_index(source, sizes)), int(np.ravel_multi_index(target, sizes))))
    return lax.ppermute(value, axes, pairs)


def mirrored(value, axis, bits):
    count = lax.axis_size(axis)
    return lax.ppermute(value, axis, [(s, s ^ bits) for s in range(count)])


def runs():
    count = lax.axis_size("sy")
    return 4 if count % 4 == 0 else count


def exchanged(value):
    count_y, count_x, run = lax.axis_size("sy"), lax.axis_size("sx"), runs()
    index = np.arange(count_y * count_x).reshape(count_y // run, run, count_x)
    groups = index.transpose(1, 0, 2).reshape(run, -1).tolist()
    return lax.all_to_all(value, ("sy", "sx"), 0, 0, axis_index_groups=groups)


def down(value):
    return ring(value, ("sy",), (1,))


def up(value):
    return ring(value, ("sy",), (-1,))


def per_device(object_field, frames_data, patch_psfs):
    rows, width = object_field.shape
    count = width // S
    psfs = patch_psfs.reshape(count, S, S)
    observed = frames_data[0]
    t = {name: jnp.asarray(value) for name, value in tables().items()}
    psf_above = down(psfs)
    kept = {k: t[k] for k in ("near_right", "near_left", "windows", "obj_left", "near_inverse", "out_right")}
    named = {"psf": psfs, "object": object_field, "frame": observed} | kept
    pack_down, pack_right, pack_diagonal, obs_last, spec, spec_here, total, *got = call(
        functools.partial(psf_kernel, tuple(named)),
        named,
        {},
        [(pltpu.VMEM, f32(H, width)), (pltpu.VMEM, f32(2 * S + H, S)), (pltpu.VMEM, f32(S + H, S)),
         (pltpu.VMEM, f32(S, S)), (pltpu.HBM, f32(2 * L, width)), (pltpu.VMEM, f32(2 * L, width)), (pltpu.VMEM, f32(8, S))]
        + [(pltpu.VMEM, x) for x in like(kept)],
        [pltpu.VMEM(psfs.shape, F32), pltpu.VMEM(object_field.shape, F32), pltpu.VMEM(observed.shape, F32),
         pltpu.SemaphoreType.DMA((len(named) + 1,)), pltpu.VMEM((6 * S, width), BF16)],
        16,
        6 * 84 * 10**6,
    )
    obj_above = down(pack_down)
    got_diagonal = ring(pack_diagonal, ("sy", "sx"), (1, 1))
    got_right = ring(pack_right, ("sx",), (1,))
    obs_above = down(observed)
    obs_diagonal = ring(obs_last, ("sy", "sx"), (1, 1))
    ready = dict(zip(kept, got))
    spec_above, spec_above_here = call(
        above_kernel,
        {"psf": psf_above},
        {k: ready[k] for k in ("near_right", "near_left")},
        [(pltpu.HBM, f32(2 * L, width)), (pltpu.VMEM, f32(2 * L, width))],
        [pltpu.VMEM(psfs.shape, F32), pltpu.SemaphoreType.DMA((2,)), pltpu.VMEM((6 * S, width), BF16)],
        16,
        6 * 84 * 10**6,
        ("psf",),
    )
    ready |= {"spec_above": spec_above_here, "spec": spec_here, "total": total, "plain": t["windows"][0]}
    named = {"right": got_right, "diagonal": got_diagonal, "above": obj_above, "own": object_field}
    outs = [f32(2 * L, 2 * S), f32(S, width - S), f32(S, width - S), f32(L, S), f32(L, S)]
    more, mid_top, mid_bottom, first, last, flux = call(
        functools.partial(model_kernel, tuple(named), tuple(ready)),
        named,
        ready,
        [(pltpu.HBM, outs[0])] + [(pltpu.VMEM, o) for o in outs[1:] + [f32(1, S)]],
        like(named) + [pltpu.SemaphoreType.DMA((len(named) + 1,)), pltpu.VMEM(outs[0].shape, F32)]
        + [pltpu.VMEM((2 * width, S), F32), pltpu.VMEM((6 * S, 2 * width + 2 * S), BF16),
           pltpu.VMEM((6 * L, 2 * width + 2 * S), BF16)],
        36,
        6 * 600 * 10**6,
        ("right", "diagonal", "above"),
    )
    mid_top, mid_bottom, first, last, flux, obs_above, obs_diagonal = lax.optimization_barrier(
        (mid_top, mid_bottom, first, last, flux, obs_above, obs_diagonal)
    )
    from_right = ring(first, ("sx",), (-1,))
    from_left = ring(last, ("sx",), (1,))
    fluxes = [flux] + [mirrored(flux, "sy", k) for k in range(1, runs())]
    named = {"from_left": from_left, "from_right": from_right}
    ready = {"mid_top": mid_top, "mid_bottom": mid_bottom, "first": first, "last": last} | dict(enumerate(fluxes))
    outs = [f32(S, width + S)] * 2
    top, bottom, flux = call(
        functools.partial(join_kernel, tuple(named), tuple(ready)),
        named,
        ready,
        [(pltpu.HBM, o) for o in outs]
        + [(pltpu.VMEM, f32(lax.axis_size("sy") // runs() * lax.axis_size("sx"), 1, S))],
        like(named) + [pltpu.SemaphoreType.DMA((len(named) + len(outs),))] + [pltpu.VMEM(o.shape, F32) for o in outs],
        16,
        10**6,
        ("from_left", "from_right"),
    )
    below = up(top)
    above = down(bottom)
    flux = exchanged(flux)

    named = {"top": top, "above": above, "bottom": bottom, "below": below,
             "obs_above": obs_above, "obs": observed,
             "obs_diagonal": obs_diagonal, "obs_left": got_right,
             "res_right": t["res_right"], "near_left": t["near_left"], "spec": spec, "spec_above": spec_above, "more": more,
             "grad_left": t["grad_left"], "grad_right": t["grad_right"],
             "windows": t["windows"], "plain": t["windows"][0]}
    outs = [f32(S, width), f32(H, width), f32(H, width), f32(H, S), f32(H, width - S)]
    residual, g_top, g_bottom, g_first, g_rest = call(
        functools.partial(gradient_kernel, tuple(named)),
        named,
        {"flux": flux},
        [(pltpu.HBM, outs[0])] + [(pltpu.VMEM, o) for o in outs[1:]],
        like(named) + [pltpu.SemaphoreType.DMA((len(named) + 1,)), pltpu.VMEM(outs[0].shape, F32)]
        + [pltpu.VMEM((L, width + S), F32), pltpu.VMEM((6 * S, 2 * width + 2 * S), BF16),
           pltpu.VMEM((12 * L, 2 * width), BF16)],
        44,
        6 * 500 * 10**6,
        ("above", "below", "obs_above", "obs_diagonal", "obs_left"),
    )
    top_same = up(g_top)
    bottom_other = mirrored(g_bottom, "fr", 1)
    first_other = ring(g_first, ("sy", "fr"), (-1, 1))
    rest_other = ring(g_rest, ("sy", "fr"), (-1, 1))
    side = jnp.concatenate([g_bottom[:, :H] + bottom_other[:, :H], top_same[:, :H] + first_other[:, :H]], axis=0)
    side = ring(side, ("sx",), (-1,))
    upper = g_bottom[:, H:] + bottom_other[:, H:]
    lower_first = top_same[:, H:S] + first_other[:, H:]
    top_same, upper, lower_first, rest_other, side = lax.optimization_barrier(
        (top_same, upper, lower_first, rest_other, side)
    )
    lower = jnp.concatenate([lower_first, top_same[:, S:] + rest_other], axis=1)
    gradient = jnp.concatenate([jnp.concatenate([upper, lower], axis=0), side], axis=1)
    return gradient, residual[None]


def solution(mesh):
    placed = (P("sy", "sx"), P("fr", "sy", "sx"), P("fr", "sy", "sx", None, None))
    return jax.shard_map(
        per_device,
        mesh=mesh,
        in_specs=placed,
        out_specs=(P("sy", "sx"), P("fr", "sy", "sx")),
        check_vma=False,
    )
```
